256 devices in a mesh: sky: 64 (over x, z, core), tm: 4 (over y).
Axes of the slice: x: 4, y: 4, z: 8, core: 2. Of those that a mesh axis runs over, the one named last changes fastest.
Arguments:
- observed: float32 [32768, 128], P(('sky', 'tm')), may hold values from -12 to 12
- att_partials: bfloat16 [3, 32768, 128], P(None, ('sky', 'tm')), may hold values from -6 to 6
- src_partials: bfloat16 [5, 32768, 128], P(None, ('sky', 'tm')), may hold values from -6 to 6
- src_slot: int32 [32768], P(('sky', 'tm')), may hold values from 0 to 1023
- knot_block: int32 [32768], P(('sky', 'tm')), may hold values from 0 to 2047, as said below
- live_count: int32 [256], P(('sky', 'tm')), may hold values from 32 to 128, as said below
- sources: float32 [5, 65536], P(None, 'sky'), may hold values from -6 to 6
- inverses: float32 [5, 5, 65536], P(None, None, 'sky')
- attitude: float32 [3, 4, 32768], P(None, 'tm', 'sky'), may hold values from -6 to 6
- band_coef: float32 [3, 3, 4, 32768], P(None, None, 'tm', 'sky'), may hold values from 0.5 to 4
- extra_diag: float32 [3, 4, 32768], P(None, 'tm', 'sky'), may hold values from 0.05 to 0.5
- band_offsets: int32 [3], replicated, may hold values from 1 to 16, as said below
Outputs:
- sources_out: float32 [5, 65536], P(None, 'sky')
- attitude_out: float32 [3, 4, 32768], P(None, 'tm', 'sky')
The draws below stay inside these ranges and needn't reach their ends.
Inputs may be any that keep to these rules, and one draw needn't show every extreme that they name: On every device, the crossings name blocks of one holder (knot_block // 32) at most 4 times, and some holder exactly 4 times; dead crossings carry blocks too. `live_count`: some device uses all its crossings. `band_offsets`: Distinct; one of them is 16.
All inputs are finite; a program needn't handle non-finite values.
Results may differ from the reference program's by a relative error of at most 0.0003.
Values sent between devices are 32-bit elements; how exact they have to be, the bound alone decides.
No kernel may reach another device: no remote copies, remote signals or barrier semaphores. Data moves between devices by JAX's collectives and lax.ppermute only.
A program may use at most 64 MiB of HBM per device.

```python
import math
import jax
import jax.numpy as jnp
from jax import lax

CROSS_DEV = 128
ROWS = 128
BLOCK_KNOTS = 16
SRC_DEV = 1024
NB = 3
HW = 16
SWEEPS = 3
ITERS = 2
BLK_DEV = 32
NBLK = 2048
SUBK = 32768
CAP = 4
SOURCES = 65536
CROSSINGS = 32768
N_TM = 4


def draw_knot_block(key, part):
    devices_all = CROSSINGS // CROSS_DEV
    holders = NBLK // BLK_DEV
    slot_total = holders * CAP

    def one_device(device_key):
        key_full, key_score, key_order, key_local = jax.random.split(device_key, 4)
        full_holder = jax.random.randint(key_full, (), 0, holders)
        slot_ids = jnp.arange(slot_total, dtype=jnp.int32)
        scores = jax.random.randint(key_score, (slot_total,), 0, 65536)
        scores = jnp.where(slot_ids // CAP == full_holder, -1, scores)
        ranked = jnp.argsort(scores * slot_total + slot_ids)
        chosen = ranked[:CROSS_DEV] // CAP
        chosen = chosen[jax.random.permutation(key_order, CROSS_DEV)]
        local_blocks = jax.random.randint(key_local, (CROSS_DEV,), 0, BLK_DEV)
        return (chosen * BLK_DEV + local_blocks).astype(jnp.int32)
    keys_all = jax.random.split(jax.random.fold_in(key, 11), devices_all)
    return jax.vmap(one_device)(keys_all).reshape(-1)


def draw_live_count(key, part):
    devices_all = CROSSINGS // CROSS_DEV
    key_div, key_full = jax.random.split(jax.random.fold_in(key, 23))
    divisor = jax.random.randint(key_div, (devices_all,), 1, 5)
    counts = CROSS_DEV // divisor
    full_device = jax.random.randint(key_full, (), 0, devices_all)
    return counts.at[full_device].set(CROSS_DEV).astype(jnp.int32)


def draw_band_offsets(key, part):
    key_pick, key_place = jax.random.split(jax.random.fold_in(key, 37))
    order = jax.random.permutation(key_pick, HW - 1) + 1
    picked = jnp.concatenate([jnp.full((1,), HW, jnp.int32), order[:NB - 1].astype(jnp.int32)])
    placed = jax.random.permutation(key_place, NB)
    return picked[placed].astype(jnp.int32)


def draw_inverses(key, part):
    key_scale, key_noise = jax.random.split(jax.random.fold_in(key, 51))
    scales = jnp.exp(jax.random.uniform(key_scale, (5, SOURCES), jnp.float32, jnp.log(0.001), jnp.log(0.012)))
    noise = 0.2 * jax.random.normal(key_noise, (5, 5, SOURCES), jnp.float32)
    symmetric = 0.5 * (noise + jnp.transpose(noise, (1, 0, 2)))
    identity = jnp.eye(5, dtype=jnp.float32)
    shape_part = identity[:, :, None] + symmetric * (1.0 - identity)[:, :, None]
    return (shape_part * jnp.sqrt(scales[:, None, :] * scales[None, :, :])).astype(jnp.float32)


def place_ends(array, stream_key, low, top_value):
    spot = [jax.random.randint(jax.random.fold_in(stream_key, axis), (), 0, length) for axis, length in enumerate(array.shape)]
    main_axis = array.shape.index(max(array.shape))
    next_to = spot[:main_axis] + [(spot[main_axis] + 1) % array.shape[main_axis]] + spot[main_axis + 1:]
    return array.at[tuple(spot)].set(low).at[tuple(next_to)].set(top_value)


def block_scale(rng, extent, cuts, low, top_value):
    def one(axis_at, blocks):
        heights = jax.random.uniform(jax.random.fold_in(jax.random.fold_in(rng, 6), axis_at), (blocks,), jnp.float32, low / len(cuts), top_value / len(cuts))
        return jnp.repeat(jnp.exp(heights), extent[axis_at] // blocks).reshape((-1,) + (1,) * (len(extent) - axis_at - 1))

    gain = one(*cuts[0])
    for cut in cuts[1:]:
        gain = gain * one(*cut)
    return gain


def bell_draw(rng, shape, deviation, limit, cuts=(), kind=jnp.bfloat16):
    array = deviation * jax.random.normal(rng, shape, jnp.float32)
    if cuts:
        array = array * block_scale(rng, shape, cuts, -0.22, 0.18)
    return jnp.clip(array, -limit, limit).astype(kind)


def setup_inputs(seed: int = 0) -> dict:
    keys = jax.random.split(jax.random.key(seed), 13)
    observed = bell_draw(keys[0], (CROSSINGS, ROWS), 2.0, 12.0, ((0, 256),), jnp.float32)
    att_partials = bell_draw(keys[1], (3, CROSSINGS, ROWS), 1.0, 6.0, ((1, 256),))
    src_partials = bell_draw(keys[2], (5, CROSSINGS, ROWS), 1.0, 6.0, ((1, 256),))
    src_slot = place_ends(jax.random.randint(keys[3], (CROSSINGS,), 0, SRC_DEV), jax.random.fold_in(keys[3], 1), 0, SRC_DEV - 1).astype(jnp.int32)
    knot_block = draw_knot_block(jax.random.fold_in(keys[12], 71), 0)
    live_count = draw_live_count(jax.random.fold_in(keys[12], 71), 0)
    sources = bell_draw(keys[6], (5, SOURCES), 1.0, 6.0, ((1, 64),), jnp.float32)
    inverses = draw_inverses(jax.random.fold_in(keys[12], 71), 0)
    attitude = bell_draw(keys[8], (3, N_TM, SUBK), 1.0, 6.0, ((1, 4), (2, 64)), jnp.float32)
    band_coef = jnp.clip(jnp.exp(math.log(4.0) - 2.0794415 * jax.random.uniform(keys[9], (NB, 3, N_TM, SUBK), jnp.float32) ** block_scale(keys[9], (NB, 3, N_TM, SUBK), ((2, 4), (3, 64)), -0.2, 0.2)), 0.5, 4.0)
    extra_diag = jnp.clip(jnp.exp(math.log(0.5) - 2.3025851 * jax.random.uniform(keys[10], (3, N_TM, SUBK), jnp.float32) ** block_scale(keys[10], (3, N_TM, SUBK), ((1, 4), (2, 64)), -0.2, 0.2)), 0.05, 0.5)
    band_offsets = draw_band_offsets(jax.random.fold_in(keys[12], 71), 0)
    return dict(observed=observed, att_partials=att_partials, src_partials=src_partials, src_slot=src_slot, knot_block=knot_block, live_count=live_count, sources=sources, inverses=inverses, attitude=attitude, band_coef=band_coef, extra_diag=extra_diag, band_offsets=band_offsets)


def spline_table():
    rows_pos = jnp.arange(ROWS, dtype=jnp.float32)
    moments = 1.5 + (BLOCK_KNOTS - 3) * (rows_pos + 0.5) / ROWS
    knot_pos = jnp.arange(BLOCK_KNOTS, dtype=jnp.float32)
    dist = jnp.abs(moments[:, None] - knot_pos[None, :])
    inner = 2.0 / 3.0 - dist * dist + 0.5 * dist * dist * dist
    rest = 2.0 - dist
    outer = rest * rest * rest / 6.0
    return jnp.where(dist < 1.0, inner, jnp.where(dist < 2.0, outer, 0.0))


def source_term(src_partials, values):
    total = jnp.zeros(src_partials.shape[1:], jnp.float32)
    for component in range(5):
        total = total + src_partials[component].astype(jnp.float32) * values[component][:, None]
    return total


def neighbour_sum(field, band_terms, band_offsets, base, length):
    total = jnp.zeros(band_terms.shape[1:], jnp.float32)
    for band_index in range(band_terms.shape[0]):
        offset = band_offsets[band_index].astype(jnp.int32)
        upper = lax.dynamic_slice_in_dim(field, base + offset, length, 1)
        lower = lax.dynamic_slice_in_dim(field, base - offset, length, 1)
        total = total + band_terms[band_index] * (upper + lower)
    return total


def reference(observed, att_partials, src_partials, src_slot, knot_block, live_count, sources, inverses, attitude, band_coef, extra_diag, band_offsets):
    spline = spline_table()
    crossing_count = observed.shape[0]
    position = jnp.arange(crossing_count, dtype=jnp.int32)
    device = position // CROSS_DEV
    sky_block = device // N_TM
    interval = device % N_TM
    live_rows = ((position % CROSS_DEV) < live_count[device]).astype(jnp.float32)[:, None]
    source_index = sky_block * SRC_DEV + src_slot
    block_index = interval * NBLK + knot_block
    knot_total = N_TM * SUBK
    band_terms = band_coef.reshape(NB, 3, knot_total)
    diagonal = extra_diag.reshape(3, knot_total) + 2.0 * jnp.sum(band_terms, axis=0)
    sources_now = sources
    knots_now = attitude.reshape(3, knot_total)
    for outer_step in range(ITERS):
        fetched = jnp.take(knots_now.reshape(3, N_TM * NBLK, BLOCK_KNOTS), block_index, axis=1)
        att_term = jnp.zeros(observed.shape, jnp.float32)
        for axis_index in range(3):
            att_term = att_term + att_partials[axis_index].astype(jnp.float32) * jnp.dot(fetched[axis_index], spline.T, precision=lax.Precision.HIGHEST)
        src_values = jnp.take(sources_now, source_index, axis=1)
        resid = (observed - source_term(src_partials, src_values) - att_term) * live_rows
        rhs = jnp.stack([jnp.sum(src_partials[component].astype(jnp.float32) * resid, axis=1) for component in range(5)])
        normal = jax.ops.segment_sum(rhs.T, source_index, num_segments=SOURCES).T
        step = jnp.einsum("klm,lm->km", inverses, normal, precision=lax.Precision.HIGHEST)
        sources_now = sources_now + step
        resid = resid - live_rows * source_term(src_partials, jnp.take(step, source_index, axis=1))
        grads = jnp.stack([jnp.dot(att_partials[axis_index].astype(jnp.float32) * resid, spline, precision=lax.Precision.HIGHEST) for axis_index in range(3)])
        knot_grad = jnp.stack([jax.ops.segment_sum(grads[axis_index], block_index, num_segments=N_TM * NBLK) for axis_index in range(3)]).reshape(3, knot_total)
        delta = knot_grad / diagonal
        for sweep_index in range(SWEEPS - 1):
            padded = jnp.pad(delta, ((0, 0), (HW, HW)))
            delta = (knot_grad + neighbour_sum(padded, band_terms, band_offsets, HW, knot_total)) / diagonal
        knots_now = knots_now + delta
    return sources_now, knots_now.reshape(3, N_TM, SUBK)
```

```python
import jax
import jax.numpy as jnp
from jax import lax
from jax.experimental import pallas as pl
from jax.experimental.pallas import tpu as pltpu
from jax.sharding import Mesh
from jax.sharding import PartitionSpec as P

F32 = jnp.float32
BF16 = jnp.bfloat16
I32 = jnp.int32
ROWS = 128
KNOTS = 16
CROSS = 128
SKY_N = 64
CHIPS = 32
TM_N = 4
SRC_N = 1024
RUN = 512
WIDE = RUN + 128
HEAD = 64
SKY = ("x", "z", "c")
SKY_TM = ("x", "z", "c", "tm")


def iota(shape, dim):
    return lax.broadcasted_iota(I32, shape, dim)


def dot(a, b):
    return jnp.dot(a.astype(BF16), b.astype(BF16), preferred_element_type=F32)


def dot_nt(a, b):
    return lax.dot_general(
        a.astype(BF16), b.astype(BF16), (((1,), (1,)), ((), ())), preferred_element_type=F32
    )


def halves(x):
    high = x.astype(BF16)
    return high, (x - high.astype(F32)).astype(BF16)


def thirds(x):
    high = x.astype(BF16).astype(F32)
    rest = x - high
    middle = rest.astype(BF16).astype(F32)
    return high, middle, rest - middle


def dot_split(values, table):
    vh, vl = halves(values)
    th, tl = halves(table)
    return dot(jnp.concatenate([vh, vl, vh], 1), jnp.concatenate([th, th, tl], 0))


def b_spline(moment_row, knot):
    tau = 1.5 + (KNOTS - 3) * (moment_row.astype(F32) + 0.5) / ROWS
    dist = jnp.abs(tau - knot.astype(F32))
    inner = 2.0 / 3.0 - dist * dist + 0.5 * dist * dist * dist
    rest = 2.0 - dist
    outer = rest * rest * rest / 6.0
    return jnp.where(dist < 1.0, inner, jnp.where(dist < 2.0, outer, 0.0))


def spline_by_lane():
    return b_spline(iota((128, 128), 1), iota((128, 128), 0) & 15)


def spline_by_row():
    return b_spline(iota((128, 128), 0), iota((128, 128), 1) & 15)


def fold_table():
    return jnp.where((iota((128, 128), 0) & 15) == (iota((128, 128), 1) & 15), 1.0, 0.0)


def as_columns(rows):
    sub = iota((128, 128), 0)
    square = jnp.zeros((128, 128), F32)
    for i, row in enumerate(rows):
        square = jnp.where(sub == i, row.astype(F32), square)
    turned = square.T
    return [turned[:, i : i + 1].astype(I32) for i in range(len(rows))]


class Meta:
    def __init__(self, kb_ref, slot_ref):
        kb, slot = kb_ref[...], slot_ref[...]
        self.h, self.lb, self.slot = kb >> 5, kb & 31, slot
        self.hc, self.lbc, self.slotc = as_columns([self.h, self.lb, slot])
        sub, lane = iota((128, 128), 0), iota((128, 128), 1)
        same = self.hc == self.h
        self.c = jnp.sum(
            jnp.where(same & (sub < lane), 1.0, 0.0), axis=0, keepdims=True
        ).astype(I32)
        self.cc = jnp.sum(
            jnp.where(same & (lane < sub), 1.0, 0.0), axis=1, keepdims=True
        ).astype(I32)
        self.group = lane >> 4

    def ghost_rows(self, live):
        sub = iota((8, 128), 0)
        place = self.c == (sub & 3)
        after = (self.h == SKY_N - 1) & (self.lb >= 30) & (sub < 4)
        before = (self.h == 0) & (self.lb <= 1) & (sub >= 4)
        used = iota((8, 128), 1) < live
        return jnp.where(place & (after | before) & used, 1.0, 0.0)

    def source_onehot(self):
        return jnp.where(iota((128, SRC_N), 1) == self.slotc, 1.0, 0.0).astype(BF16)


def attitude_term(att_ref, masked):
    spread = dot_split(jnp.concatenate(masked, 0), spline_by_lane())
    total = jnp.zeros((CROSS, ROWS), F32)
    for a in range(3):
        total = total + att_ref[a].astype(F32) * spread[a * 128 : a * 128 + 128]
    return total


def local_normal(src_ref, resid, onehot):
    lane = iota((128, 128), 1)
    square = jnp.zeros((128, 128), F32)
    for p in range(5):
        rhs = jnp.sum(src_ref[p].astype(F32) * resid, axis=1, keepdims=True)
        square = jnp.where(lane == p, rhs, square)
    rows = square.T[0:8]
    parts = dot(jnp.concatenate(thirds(rows), 0), onehot)
    return parts[0:8] + parts[8:16] + parts[16:24]


def gather_source(values8, onehot):
    parts = dot_nt(onehot, jnp.concatenate(thirds(values8), 0))
    return [
        parts[:, p : p + 1] + parts[:, 8 + p : 9 + p] + parts[:, 16 + p : 17 + p] for p in range(5)
    ]


def padded_rows(x):
    return jnp.concatenate([x, jnp.zeros((8 - x.shape[0], x.shape[1]), F32)], 0)


def first_kernel(
    live_ref, core_ref, near_ref, far_ref, obs_ref, att_ref, src_ref, slot_ref, kb_ref, sources_ref,
    resid_ref, plain_ref, up_ref, down_ref,
):
    meta = Meta(kb_ref, slot_ref)
    live, core = live_ref[0], core_ref[0]
    place = (meta.lbc >> 3) * CHIPS + (meta.hc >> 1)
    place = place + jnp.where((meta.hc & 1) == core, 0, 128)
    onehot = jnp.where(iota((128, 256), 1) == place, 1.0, 0.0)
    tables = []
    for a in range(3):
        rows = [ref[:, a, r, :] for ref in (near_ref, far_ref) for r in range(4)]
        tables += halves(jnp.concatenate(rows, 0))
    found = dot(onehot, jnp.concatenate(tables, 1))
    mine = meta.group == (meta.lbc & 7)
    masked = []
    for a in range(3):
        whole = found[:, 256 * a : 256 * a + 128] + found[:, 256 * a + 128 : 256 * a + 256]
        masked.append(jnp.where(mine, whole, 0.0))
    att_term = attitude_term(att_ref, masked)
    by_source = meta.source_onehot()
    values = gather_source(padded_rows(sources_ref[...]), by_source)
    src_term = jnp.zeros((CROSS, ROWS), F32)
    for p in range(5):
        src_term = src_term + src_ref[p].astype(F32) * values[p]
    used = jnp.where(iota((CROSS, 1), 0) < live, 1.0, 0.0)
    resid = (obs_ref[...] - src_term - att_term) * used
    resid_ref[...] = resid
    normal = local_normal(src_ref, resid, by_source)
    for ref in (plain_ref, up_ref, down_ref):
        for j in range(8):
            ref[8 * j : 8 * j + 8, :] = normal[:, 128 * j : 128 * j + 128]
    choose = meta.ghost_rows(live)
    high, low = halves(resid)
    pieces = [att_ref[a] for a in range(3)] + [src_ref[p] for p in range(5)] + [high, low]
    ghosts = dot(choose, jnp.concatenate(pieces, 1))
    items = [ghosts[:, 128 * i : 128 * i + 128] for i in range(10)]
    slot = jnp.sum(choose * meta.slot.astype(F32), axis=1, keepdims=True)
    block = jnp.sum(choose * meta.lb.astype(F32), axis=1, keepdims=True)
    items[8] = items[8] + items[9]
    items[9] = jnp.where(iota((8, 128), 1) < 64, slot, block)
    for q in range(5):
        even, odd = items[2 * q], items[2 * q + 1]
        low_row = HEAD + 8 * q
        up_ref[low_row : low_row + 8, :] = jnp.concatenate([even[0:4], odd[0:4]], 0)
        down_ref[low_row : low_row + 8, :] = jnp.concatenate([even[4:8], odd[4:8]], 0)


def middle_kernel(
    live_ref, got_ref, resid_in_ref, att_ref, src_ref, slot_ref, kb_ref, resid_ref, send_ref
):
    meta = Meta(kb_ref, slot_ref)
    peers = jnp.where(iota((128, SKY_N), 1) == meta.hc, 1.0, 0.0)
    table = jnp.concatenate([*halves(got_ref[:, 0, :]), *halves(got_ref[:, 1, :])], 1)
    found = dot(peers, table)
    front = found[:, 0:128] + found[:, 128:256]
    back = found[:, 256:384] + found[:, 384:512]
    masked = [
        jnp.where(meta.group == meta.cc, front, 0.0),
        jnp.where(meta.group == meta.cc + 4, front, 0.0),
        jnp.where(meta.group == meta.cc, back, 0.0),
    ]
    used = jnp.where(iota((CROSS, 1), 0) < live_ref[0], 1.0, 0.0)
    resid = resid_in_ref[...] - attitude_term(att_ref, masked) * used
    resid_ref[...] = resid
    normal = local_normal(src_ref, resid, meta.source_onehot())
    for j in range(8):
        send_ref[8 * j : 8 * j + 8, :] = normal[:, 128 * j : 128 * j + 128]
    ghosts = dot(meta.ghost_rows(live_ref[0]), jnp.concatenate(halves(resid), 1))
    send_ref[HEAD : HEAD + 8, :] = ghosts[:, 0:128] + ghosts[:, 128:256]


def return_kernel(
    live_ref, tm_ref, own_ref, below_ref, above_ref, across_ref, up_ref, down_ref, inverses_ref,
    sources_in_ref, resid_in_ref, att_ref, src_ref, slot_ref, kb_ref,
    out_ref, resid_ref, sources_ref, *, second,
):
    meta = Meta(kb_ref, slot_ref)
    tm = tm_ref[0]
    total = (
        own_ref[0:HEAD, :] + across_ref[0:HEAD, :] + below_ref[0:HEAD, :] + above_ref[0:HEAD, :]
    )
    normal = jnp.concatenate([total[8 * j : 8 * j + 8] for j in range(8)], 1)
    sub8 = iota((8, SRC_N), 0)
    step = jnp.zeros((8, SRC_N), F32)
    for p in range(5):
        row = jnp.sum(inverses_ref[p] * normal[0:5], axis=0, keepdims=True)
        step = jnp.where(sub8 == p, row, step)
    sources_ref[...] = sources_in_ref[...] + step[0:5]
    ghost8 = iota((8, 128), 0)
    there = jnp.where(ghost8 < 4, jnp.where(tm > 0, 1.0, 0.0), jnp.where(tm < TM_N - 1, 1.0, 0.0))

    def item(i):
        row = HEAD + 4 * i
        return jnp.concatenate([up_ref[row : row + 4, :], down_ref[row : row + 4, :]], 0)

    facts = item(9)
    ghost_slot = facts[:, 0:1].astype(I32)
    ghost_block = facts[:, 64:65].astype(I32)
    ghost_onehot = jnp.where(iota((8, SRC_N), 1) == ghost_slot, 1.0, 0.0)
    values = gather_source(step, meta.source_onehot())
    ghost_values = gather_source(step, ghost_onehot)
    change = jnp.zeros((CROSS, ROWS), F32)
    ghost_change = jnp.zeros((8, ROWS), F32)
    for p in range(5):
        change = change + src_ref[p].astype(F32) * values[p]
        ghost_change = ghost_change + item(3 + p) * ghost_values[p]
    used = jnp.where(iota((CROSS, 1), 0) < live_ref[0], 1.0, 0.0)
    resid = resid_in_ref[...] - used * change
    resid_ref[...] = resid
    if second:
        ghost_resid = jnp.concatenate(
            [below_ref[HEAD : HEAD + 4, :], above_ref[HEAD + 4 : HEAD + 8, :]], 0
        )
    else:
        ghost_resid = item(8)
    ghost_resid = (ghost_resid - ghost_change) * there
    rows = [att_ref[a].astype(F32) * resid for a in range(3)]
    rows += [item(a) * ghost_resid for a in range(3)]
    grads = dot_split(jnp.concatenate(rows, 0), spline_by_row())
    to_row = jnp.where(
        meta.lb <= 1, meta.h - 1, jnp.where(meta.lb >= 30, meta.h + 1, jnp.full_like(meta.h, -1))
    )
    edge_group = jnp.where(meta.lbc <= 1, meta.lbc, meta.lbc - 24)
    own = meta.group == meta.cc + 2
    edge = meta.group == edge_group
    peer = iota((SKY_N, 128), 0)
    onehot = jnp.concatenate(
        [jnp.where(peer == meta.h, 1.0, 0.0), jnp.where(peer == to_row, 1.0, 0.0)], 1
    )
    top, bottom = [], []
    for a in range(3):
        g = grads[128 * a : 128 * a + 128]
        top += halves(jnp.where(own, g, 0.0))
        bottom += halves(jnp.where(edge, g, 0.0))
    if not second:
        top.append(jnp.where(own, (meta.lbc + 1).astype(F32), 0.0).astype(BF16))
        bottom.append(jnp.zeros((128, 128), BF16))
    table = jnp.concatenate([jnp.concatenate(top, 1), jnp.concatenate(bottom, 1)], 0)
    packed = dot(onehot, table)
    ghost_group = iota((8, 128), 1) >> 4
    ghost_own = ghost_group == jnp.where(ghost8[:, 0:1] < 4, ghost_block - 24, ghost_block)
    for a in range(3):
        ghost = jnp.where(ghost_own, grads[384 + 8 * a : 392 + 8 * a], 0.0)
        from_below = jnp.sum(jnp.where(ghost8 < 4, ghost, 0.0), axis=0, keepdims=True)
        from_above = jnp.sum(jnp.where(ghost8 >= 4, ghost, 0.0), axis=0, keepdims=True)
        block = packed[:, 256 * a : 256 * a + 128] + packed[:, 256 * a + 128 : 256 * a + 256]
        block = block + jnp.where(peer == 0, from_below, 0.0)
        block = block + jnp.where(peer == SKY_N - 1, from_above, 0.0)
        out_ref[:, a, :] = block
    if second:
        out_ref[:, 3, :] = jnp.zeros((SKY_N, 128), F32)
    else:
        out_ref[:, 3, :] = packed[:, 768:896]


def smooth_kernel(
    offsets_ref, got_ref, index_ref, knots_in_ref, bands_ref, before_ref, after_ref, *outs, last
):
    knots_ref = outs[0]
    lane = iota((SKY_N, 128), 1)
    index = index_ref[:, 3, :]
    square = jnp.concatenate([index, jnp.zeros((128 - SKY_N, 128), F32)], 0).T
    block32 = (iota((32, SKY_N), 0) + 1).astype(F32)
    pick = jnp.concatenate(
        [
            jnp.where(square[16 * (2 + c) : 16 * (2 + c) + 1, 0:SKY_N] == block32, 1.0, 0.0)
            for c in range(4)
        ],
        0,
    )
    got = [got_ref[:, a, :] for a in range(3)]
    table = jnp.concatenate([part for g in got for part in halves(g)], 1)
    summed = dot(pick, table)
    row128 = iota((128, 128), 0)
    group128 = iota((128, 128), 1) >> 4
    keep = group128 == (row128 >> 5) + 2
    fold = fold_table()
    stack = []
    for a in range(3):
        one = summed[:, 256 * a : 256 * a + 128] + summed[:, 256 * a + 128 : 256 * a + 256]
        one = jnp.where(keep, one, 0.0)
        stack.append(one[0:32] + one[32:64] + one[64:96] + one[96:128])
    high, low = halves(jnp.concatenate(stack, 0))
    spread = dot(jnp.concatenate([high, low], 1), jnp.concatenate([fold, fold], 0))
    in_row = (iota((8, 128), 1) >> 4) == iota((8, 128), 0)
    sub_w = iota((8, WIDE), 0)
    grad = jnp.zeros((8, WIDE), F32)
    for a in range(3):
        tiles = []
        for r in range(4):
            piece = spread[32 * a + 8 * r : 32 * a + 8 * r + 8]
            tiles.append(jnp.sum(jnp.where(in_row, piece, 0.0), axis=0, keepdims=True))
        rim = jnp.where((lane < 32) | (lane >= 96), got[a], 0.0)
        tiles.append(jnp.sum(rim, axis=0, keepdims=True))
        grad = jnp.where(sub_w == a, jnp.concatenate(tiles, 1), grad)
    lane3 = iota((3, 128), 1)

    def wide(i):
        rim = jnp.where(
            lane3 < 32,
            after_ref[3 * i : 3 * i + 3, :],
            jnp.where(lane3 >= 96, before_ref[3 * i : 3 * i + 3, :], 0.0),
        )
        return padded_rows(jnp.concatenate([bands_ref[3 * i : 3 * i + 3, :], rim], 1))

    bands = [wide(b) for b in range(3)]
    diag = wide(3) + 2.0 * (bands[0] + bands[1] + bands[2])
    diag = jnp.where(diag > 0.0, diag, 1.0)
    delta = grad / diag
    for _ in range(2):
        total = jnp.zeros((8, WIDE), F32)
        for b in range(3):
            offset = offsets_ref[b]
            upper = pltpu.roll(delta, WIDE - offset, 1)
            lower = pltpu.roll(delta, offset, 1)
            total = total + bands[b] * (upper + lower)
        delta = (grad + total) / diag
    knots_ref[...] = knots_in_ref[...] + delta[0:3, 0:RUN]
    if last:
        return
    send_ref = outs[1]
    sub8 = iota((8, 128), 0)
    tables = []
    for a in range(3):
        rows = jnp.zeros((8, 128), F32)
        for r in range(4):
            rows = jnp.where(sub8 == r, delta[a : a + 1, 128 * r : 128 * r + 128], rows)
        tables += halves(rows)
    slots = [index[:, 16 * (2 + c) : 16 * (2 + c) + 1].astype(I32) - 1 for c in range(4)]
    slot = jnp.concatenate(slots, 0)
    by_row = jnp.where(iota((4 * SKY_N, 8), 1) == (slot >> 3), 1.0, 0.0)
    found = dot(by_row, jnp.concatenate(tables, 1))
    mine = (iota((4 * SKY_N, 128), 1) >> 4) == (slot & 7)
    masked = []
    for a in range(3):
        one = found[:, 256 * a : 256 * a + 128] + found[:, 256 * a + 128 : 256 * a + 256]
        masked.append(jnp.where(mine, one, 0.0))
    high, low = halves(jnp.concatenate(masked, 0))
    spread = dot(jnp.concatenate([high, low], 1), jnp.concatenate([fold, fold], 0))
    group = lane >> 4
    front = jnp.zeros((SKY_N, 128), F32)
    back = jnp.zeros((SKY_N, 128), F32)
    for c in range(4):
        part = [
            spread[4 * SKY_N * a + SKY_N * c : 4 * SKY_N * a + SKY_N * (c + 1)] for a in range(3)
        ]
        front = jnp.where(group == c, part[0], jnp.where(group == c + 4, part[1], front))
        back = jnp.where(group == c, part[2], back)
    send_ref[:, 0, :] = front
    send_ref[:, 1, :] = back


def run_kernel(body, scalars, outs, *args, **static):
    specs = [
        pl.BlockSpec(memory_space=pltpu.SMEM if i < scalars else pltpu.VMEM)
        for i in range(len(args))
    ]

    def kernel(*refs):
        body(*refs, **static)

    return pl.pallas_call(
        kernel,
        out_shape=[jax.ShapeDtypeStruct(shape, F32) for shape in outs],
        in_specs=specs,
        out_specs=[pl.BlockSpec(memory_space=pltpu.VMEM) for _ in outs],
        compiler_params=pltpu.CompilerParams(vmem_limit_bytes=32 * 1024 * 1024),
    )(*args)


def shifts(k):
    return [(i, (i + k) % TM_N) for i in range(TM_N)]


def per_device(
    observed,
    att_partials,
    src_partials,
    src_slot,
    knot_block,
    live_count,
    sources,
    inverses,
    attitude,
    band_coef,
    extra_diag,
    band_offsets,
):
    core = lax.axis_index("c").astype(I32).reshape(1)
    tm = lax.axis_index("tm").astype(I32).reshape(1)
    slot = src_slot.reshape(1, CROSS)
    kb = knot_block.reshape(1, CROSS)
    knots = attitude[:, 0, :]
    static = jnp.concatenate([band_coef.reshape(9, RUN), extra_diag.reshape(3, RUN)], 0)
    chain = [s * TM_N + t for t in range(TM_N) for s in range(SKY_N)]
    pairs = list(zip(chain[:-1], chain[1:], strict=True))
    before = lax.ppermute(static[:, RUN - 128 :], SKY_TM, pairs)
    after = lax.ppermute(static[:, :128], SKY_TM, [(b, a) for a, b in pairs])

    dense = jnp.broadcast_to(attitude.reshape(1, 3, 4, 128), (CHIPS, 3, 4, 128))
    near = lax.all_to_all(dense, ("x", "z"), 0, 0, tiled=True)
    far = lax.ppermute(near, "c", [(0, 1), (1, 0)])
    resid, plain, up, down = run_kernel(
        first_kernel, 2, [(CROSS, ROWS), (HEAD, 128), (HEAD + 40, 128), (HEAD + 40, 128)],
        live_count, core, near, far, observed, att_partials, src_partials, slot, kb, sources,
    )
    up = lax.ppermute(up, "tm", shifts(1))
    down = lax.ppermute(down, "tm", shifts(-1))
    across = lax.ppermute(plain, "tm", shifts(2))
    back_shapes = [(SKY_N, 4, 128), (CROSS, ROWS), (5, SRC_N)]
    outgoing, resid, sources = run_kernel(
        return_kernel, 2, back_shapes,
        live_count, tm, plain, up, down, across, up, down, inverses, sources, resid,
        att_partials, src_partials, slot, kb, second=False,
    )
    first = lax.all_to_all(outgoing, SKY, 0, 0, tiled=True)
    knots, served = run_kernel(
        smooth_kernel, 1, [(3, RUN), (SKY_N, 2, 128)],
        band_offsets, first, first, knots, static, before, after, last=False,
    )
    arrived = lax.all_to_all(served, SKY, 0, 0, tiled=True)
    resid, mine = run_kernel(
        middle_kernel, 1, [(CROSS, ROWS), (HEAD + 8, 128)],
        live_count, arrived, resid, att_partials, src_partials, slot, kb,
    )
    below = lax.ppermute(mine, "tm", shifts(1))
    above = lax.ppermute(mine, "tm", shifts(-1))
    across = lax.ppermute(mine, "tm", shifts(2))
    outgoing, resid, sources = run_kernel(
        return_kernel, 2, back_shapes,
        live_count, tm, mine, below, above, across, up, down, inverses, sources, resid,
        att_partials, src_partials, slot, kb, second=True,
    )
    second = lax.all_to_all(outgoing, SKY, 0, 0, tiled=True)
    (knots,) = run_kernel(
        smooth_kernel, 1, [(3, RUN)],
        band_offsets, second, first, knots, static, before, after, last=True,
    )
    return (sources, knots[:, None, :])


def solution(mesh):
    torus = Mesh(mesh.devices.reshape(4, 8, 2, mesh.shape["tm"]), SKY_TM)
    return jax.shard_map(
        per_device,
        mesh=torus,
        in_specs=(
            P(SKY_TM, None),
            P(None, SKY_TM, None),
            P(None, SKY_TM, None),
            P(SKY_TM),
            P(SKY_TM),
            P(SKY_TM),
            P(None, SKY),
            P(None, None, SKY),
            P(None, "tm", SKY),
            P(None, None, "tm", SKY),
            P(None, "tm", SKY),
            P(),
        ),
        out_specs=(P(None, SKY), P(None, "tm", SKY)),
        check_vma=False,
    )
```

```python
import jax
import jax.numpy as jnp
from jax import lax
from jax.experimental import pallas as pl
from jax.experimental.pallas import tpu as pltpu
from jax.sharding import Mesh
from jax.sharding import PartitionSpec as P

F32 = jnp.float32
BF16 = jnp.bfloat16
I32 = jnp.int32
ROWS = 128
KNOTS = 16
CROSS = 128
SKY_N = 64
CHIPS = 32
TM_N = 4
SRC_N = 1024
RUN = 512
WIDE = RUN + 128
HEAD = 40
SKY = ("x", "z", "c")
SKY_TM = ("x", "z", "c", "tm")


def iota(shape, dim):
    return lax.broadcasted_iota(I32, shape, dim)


def dot(a, b):
    return jnp.dot(a.astype(BF16), b.astype(BF16), preferred_element_type=F32)


def dot_nt(a, b):
    return lax.dot_general(
        a.astype(BF16), b.astype(BF16), (((1,), (1,)), ((), ())), preferred_element_type=F32
    )


def halves(x):
    high = x.astype(BF16)
    return high, (x - high.astype(F32)).astype(BF16)


def thirds(x):
    high = x.astype(BF16).astype(F32)
    rest = x - high
    middle = rest.astype(BF16).astype(F32)
    return high, middle, rest - middle


def b_spline(moment_row, knot):
    tau = 1.5 + (KNOTS - 3) * (moment_row.astype(F32) + 0.5) / ROWS
    dist = jnp.abs(tau - knot.astype(F32))
    inner = 2.0 / 3.0 - dist * dist + 0.5 * dist * dist * dist
    rest = 2.0 - dist
    outer = rest * rest * rest / 6.0
    return jnp.where(dist < 1.0, inner, jnp.where(dist < 2.0, outer, 0.0))


def spline_by_lane():
    return b_spline(iota((128, 128), 1), iota((128, 128), 0) & 15)


def spline_by_row():
    return b_spline(iota((128, 128), 0), iota((128, 128), 1) & 15)


def fold_table():
    return jnp.where((iota((128, 128), 0) & 15) == (iota((128, 128), 1) & 15), 1.0, 0.0)


def attitude_term(att_ref, masked, table_ref):
    high, low = halves(jnp.concatenate(masked, 0))
    spread = dot(jnp.concatenate([high, low, high], 1), table_ref[...])
    total = jnp.zeros((CROSS, ROWS), F32)
    for a in range(3):
        total = total + att_ref[a].astype(F32) * spread[a * 128 : a * 128 + 128]
    return total


def send_normal(src_ref, resid, onehot, refs):
    lane = iota((128, 128), 1)
    square = jnp.zeros((128, 128), F32)
    for p in range(5):
        rhs = jnp.sum(src_ref[p].astype(F32) * resid, axis=1, keepdims=True)
        square = jnp.where(lane == p, rhs, square)
    rows = square.T[0:8]
    parts = dot(jnp.concatenate(thirds(rows), 0), onehot)
    normal = parts[0:8] + parts[8:16] + parts[16:24]
    for ref in refs:
        for j in range(8):
            ref[pl.ds(j, 5, stride=8), :] = normal[0:5, 128 * j : 128 * j + 128]


def gather_source(values8, onehot):
    parts = dot_nt(onehot, jnp.concatenate(thirds(values8), 0))
    return [
        parts[:, p : p + 1] + parts[:, 8 + p : 9 + p] + parts[:, 16 + p : 17 + p] for p in range(5)
    ]


def padded_rows(x):
    return jnp.concatenate([x, jnp.zeros((8 - x.shape[0], x.shape[1]), F32)], 0)


def column(cols_ref, i):
    return cols_ref[:, i : i + 1].astype(I32)


def stacked_spline(table):
    high, low = halves(table)
    return jnp.concatenate([high, high, low], 0)


def prepare_kernel(
    live_ref, core_ref, obs_ref, att_ref, src_ref, slot_ref, kb_ref, sources_ref,
    cols_ref, places_ref, by_source_ref, base_ref, by_lane_ref, by_row_ref, pack_ref, index_ref,
    peers_ref, choose_ref, up_ref, down_ref,
):
    live, core = live_ref[0], core_ref[0]
    kb, slot = kb_ref[...], slot_ref[...]
    h, lb = kb >> 5, kb & 31
    sub, lane = iota((128, 128), 0), iota((128, 128), 1)
    square = jnp.zeros((128, 128), F32)
    for i, row in enumerate((h, lb, slot)):
        square = jnp.where(sub == i, row.astype(F32), square)
    turned = square.T
    hc, lbc, slotc = (turned[:, i : i + 1].astype(I32) for i in range(3))
    same = hc == h
    c = jnp.sum(jnp.where(same & (sub < lane), 1.0, 0.0), axis=0, keepdims=True).astype(I32)
    cc = jnp.sum(jnp.where(same & (lane < sub), 1.0, 0.0), axis=1, keepdims=True)
    cols_ref[...] = jnp.where(lane == 3, cc, turned)
    cc = cc.astype(I32)
    group = lane >> 4

    place = (lbc >> 3) * CHIPS + (hc >> 1) + jnp.where((hc & 1) == core, 0, 128)
    places_ref[...] = jnp.where(iota((128, 256), 1) == place, 1.0, 0.0).astype(BF16)
    by_source = jnp.where(iota((128, SRC_N), 1) == slotc, 1.0, 0.0).astype(BF16)
    by_source_ref[...] = by_source
    values = gather_source(padded_rows(sources_ref[...]), by_source)
    src_term = jnp.zeros((CROSS, ROWS), F32)
    for p in range(5):
        src_term = src_term + src_ref[p].astype(F32) * values[p]
    base_ref[...] = obs_ref[...] - src_term
    by_lane_ref[...] = stacked_spline(spline_by_lane())
    by_row_ref[...] = stacked_spline(spline_by_row())

    peer = iota((SKY_N, 128), 0)
    to_row = jnp.where(lb <= 1, h - 1, jnp.where(lb >= 30, h + 1, jnp.full_like(h, -1)))
    own = jnp.where(peer == h, 1.0, 0.0)
    pack_ref[...] = jnp.concatenate([own, jnp.where(peer == to_row, 1.0, 0.0)], 1).astype(BF16)
    index_ref[...] = dot(own, jnp.where(group == cc + 2, (lbc + 1).astype(F32), 0.0))
    peers_ref[...] = jnp.where(iota((128, SKY_N), 1) == hc, 1.0, 0.0).astype(BF16)

    sub8 = iota((8, 128), 0)
    after = (h == SKY_N - 1) & (lb >= 30) & (sub8 < 4)
    before = (h == 0) & (lb <= 1) & (sub8 >= 4)
    chosen = (c == (sub8 & 3)) & (after | before) & (iota((8, 128), 1) < live)
    choose = jnp.where(chosen, 1.0, 0.0)
    choose_ref[...] = choose
    pieces = [att_ref[a] for a in range(3)] + [src_ref[p] for p in range(5)]
    ghosts = dot(choose, jnp.concatenate(pieces, 1))
    items = [ghosts[:, 128 * i : 128 * i + 128] for i in range(8)]
    ghost_slot = jnp.sum(choose * slot.astype(F32), axis=1, keepdims=True)
    ghost_block = jnp.sum(choose * lb.astype(F32), axis=1, keepdims=True)
    items.append(jnp.zeros((8, 128), F32))
    items.append(jnp.where(iota((8, 128), 1) < 64, ghost_slot, ghost_block))
    for q in range(5):
        even, odd = items[2 * q], items[2 * q + 1]
        up_ref[8 * q : 8 * q + 8, :] = jnp.concatenate([even[0:4], odd[0:4]], 0)
        down_ref[8 * q : 8 * q + 8, :] = jnp.concatenate([even[4:8], odd[4:8]], 0)


def widen_kernel(bands_ref, extra_ref, before_ref, after_ref, wide_ref):
    sub, lane = iota((8, RUN), 0), iota((8, 128), 1)

    def wide(i):
        core = jnp.zeros((8, RUN), F32)
        for a in range(3):
            rows = bands_ref[i, a] if i < 3 else extra_ref[a]
            core = jnp.where(sub == a, jnp.concatenate([rows[r : r + 1] for r in range(4)], 1), core)
        after = padded_rows(after_ref[3 * i : 3 * i + 3, :])
        before = padded_rows(before_ref[3 * i : 3 * i + 3, :])
        rim = jnp.where(lane < 32, after, jnp.where(lane >= 96, before, 0.0))
        return jnp.concatenate([core, rim], 1)

    bands = [wide(b) for b in range(3)]
    diag = wide(3) + 2.0 * (bands[0] + bands[1] + bands[2])
    for b in range(3):
        wide_ref[8 * b : 8 * b + 8, :] = bands[b]
    wide_ref[24:32, :] = 1.0 / jnp.where(diag > 0.0, diag, 1.0)


def first_kernel(
    live_ref, near_ref, far_ref, att_ref, src_ref, cols_ref, places_ref, by_source_ref, base_ref,
    by_lane_ref, choose_ref, up_in_ref, down_in_ref,
    resid_ref, plain_ref, up_ref, down_ref,
):
    tables = []
    for a in range(3):
        rows = [ref[:, a, r, :] for ref in (near_ref, far_ref) for r in range(4)]
        tables += halves(jnp.concatenate(rows, 0))
    found = dot(places_ref[...], jnp.concatenate(tables, 1))
    mine = (iota((128, 128), 1) >> 4) == (column(cols_ref, 1) & 7)
    masked = []
    for a in range(3):
        whole = found[:, 256 * a : 256 * a + 128] + found[:, 256 * a + 128 : 256 * a + 256]
        masked.append(jnp.where(mine, whole, 0.0))
    used = jnp.where(iota((CROSS, 1), 0) < live_ref[0], 1.0, 0.0)
    resid = (base_ref[...] - attitude_term(att_ref, masked, by_lane_ref)) * used
    resid_ref[...] = resid
    send_normal(src_ref, resid, by_source_ref[...], (plain_ref, up_ref, down_ref))
    ghosts = dot(choose_ref[...], jnp.concatenate(halves(resid), 1))
    ghosts = ghosts[:, 0:128] + ghosts[:, 128:256]
    up_ref[HEAD : HEAD + 40, :] = up_in_ref[...]
    down_ref[HEAD : HEAD + 40, :] = down_in_ref[...]
    up_ref[HEAD + 32 : HEAD + 36, :] = ghosts[0:4]
    down_ref[HEAD + 32 : HEAD + 36, :] = ghosts[4:8]


def middle_kernel(
    live_ref, got_ref, resid_in_ref, att_ref, src_ref, cols_ref, peers_ref, by_source_ref,
    by_lane_ref, choose_ref, resid_ref, send_ref,
):
    table = jnp.concatenate([*halves(got_ref[:, 0, :]), *halves(got_ref[:, 1, :])], 1)
    found = dot(peers_ref[...], table)
    front = found[:, 0:128] + found[:, 128:256]
    back = found[:, 256:384] + found[:, 384:512]
    group, cc = iota((128, 128), 1) >> 4, column(cols_ref, 3)
    masked = [
        jnp.where(group == cc, front, 0.0),
        jnp.where(group == cc + 4, front, 0.0),
        jnp.where(group == cc, back, 0.0),
    ]
    used = jnp.where(iota((CROSS, 1), 0) < live_ref[0], 1.0, 0.0)
    resid = resid_in_ref[...] - attitude_term(att_ref, masked, by_lane_ref) * used
    resid_ref[...] = resid
    send_normal(src_ref, resid, by_source_ref[...], (send_ref,))
    ghosts = dot(choose_ref[...], jnp.concatenate(halves(resid), 1))
    send_ref[HEAD : HEAD + 8, :] = ghosts[:, 0:128] + ghosts[:, 128:256]


def return_kernel(
    live_ref, tm_ref, own_ref, below_ref, above_ref, across_ref, up_ref, down_ref, inverses_ref,
    sources_in_ref, resid_in_ref, att_ref, src_ref, cols_ref, by_source_ref, by_row_ref, pack_ref,
    index_ref, out_ref, resid_ref, sources_ref, total_ref, *, second,
):
    tm = tm_ref[0]
    total_ref[...] = (
        own_ref[0:HEAD, :] + across_ref[0:HEAD, :] + below_ref[0:HEAD, :] + above_ref[0:HEAD, :]
    )
    normal = jnp.concatenate([total_ref[pl.ds(j, 5, stride=8), :] for j in range(8)], 1)
    sub8 = iota((8, SRC_N), 0)
    step = jnp.zeros((8, SRC_N), F32)
    for p in range(5):
        row = jnp.sum(inverses_ref[p] * normal, axis=0, keepdims=True)
        step = jnp.where(sub8 == p, row, step)
    sources_ref[...] = step[0:5] if second else sources_in_ref[...] + step[0:5]
    ghost8 = iota((8, 128), 0)
    there = jnp.where(ghost8 < 4, jnp.where(tm > 0, 1.0, 0.0), jnp.where(tm < TM_N - 1, 1.0, 0.0))

    def item(i):
        row = HEAD + 4 * i
        return jnp.concatenate([up_ref[row : row + 4, :], down_ref[row : row + 4, :]], 0)

    facts = item(9)
    ghost_slot = facts[:, 0:1].astype(I32)
    ghost_block = facts[:, 64:65].astype(I32)
    ghost_onehot = jnp.where(iota((8, SRC_N), 1) == ghost_slot, 1.0, 0.0)
    values = gather_source(step, by_source_ref[...])
    ghost_values = gather_source(step, ghost_onehot)
    change = jnp.zeros((CROSS, ROWS), F32)
    ghost_change = jnp.zeros((8, ROWS), F32)
    for p in range(5):
        change = change + src_ref[p].astype(F32) * values[p]
        ghost_change = ghost_change + item(3 + p) * ghost_values[p]
    used = jnp.where(iota((CROSS, 1), 0) < live_ref[0], 1.0, 0.0)
    resid = resid_in_ref[...] - used * change
    resid_ref[...] = resid
    if second:
        ghost_resid = jnp.concatenate(
            [below_ref[HEAD : HEAD + 4, :], above_ref[HEAD + 4 : HEAD + 8, :]], 0
        )
    else:
        ghost_resid = item(8)
    ghost_resid = (ghost_resid - ghost_change) * there
    rows = [att_ref[a].astype(F32) * resid for a in range(3)]
    rows += [item(a) * ghost_resid for a in range(3)]
    high, low = halves(jnp.concatenate(rows, 0))
    grads = dot(jnp.concatenate([high, low, high], 1), by_row_ref[...])
    lbc, cc = column(cols_ref, 1), column(cols_ref, 3)
    group = iota((128, 128), 1) >> 4
    edge_group = jnp.where(lbc <= 1, lbc, lbc - 24)
    own = group == cc + 2
    edge = group == edge_group
    top, bottom = [], []
    for a in range(3):
        g = grads[128 * a : 128 * a + 128]
        top += halves(jnp.where(own, g, 0.0))
        bottom += halves(jnp.where(edge, g, 0.0))
    table = jnp.concatenate([jnp.concatenate(top, 1), jnp.concatenate(bottom, 1)], 0)
    packed = dot(pack_ref[...], table)
    peer = iota((SKY_N, 128), 0)
    ghost_group = iota((8, 128), 1) >> 4
    ghost_own = ghost_group == jnp.where(ghost8[:, 0:1] < 4, ghost_block - 24, ghost_block)
    for a in range(3):
        ghost = jnp.where(ghost_own, grads[384 + 8 * a : 392 + 8 * a], 0.0)
        from_below = jnp.sum(jnp.where(ghost8 < 4, ghost, 0.0), axis=0, keepdims=True)
        from_above = jnp.sum(jnp.where(ghost8 >= 4, ghost, 0.0), axis=0, keepdims=True)
        block = packed[:, 256 * a : 256 * a + 128] + packed[:, 256 * a + 128 : 256 * a + 256]
        block = block + jnp.where(peer == 0, from_below, 0.0)
        block = block + jnp.where(peer == SKY_N - 1, from_above, 0.0)
        out_ref[:, a, :] = block
    out_ref[:, 3, :] = index_ref[...]


def smooth_kernel(
    offsets_ref, got_ref, pick_in_ref, knots_in_ref, wide_ref, sources_in_ref, step_ref, *outs, last
):
    knots_ref = outs[0]
    lane = iota((SKY_N, 128), 1)
    if last:
        pick = pick_in_ref[...]
    else:
        index = got_ref[:, 3, :]
        square = jnp.concatenate([index, jnp.zeros((128 - SKY_N, 128), F32)], 0).T
        block32 = (iota((32, SKY_N), 0) + 1).astype(F32)
        pick = jnp.concatenate(
            [
                jnp.where(square[16 * (2 + c) : 16 * (2 + c) + 1, 0:SKY_N] == block32, 1.0, 0.0)
                for c in range(4)
            ],
            0,
        ).astype(BF16)
        outs[2][...] = pick
    got = [got_ref[:, a, :] for a in range(3)]
    table = jnp.concatenate([part for g in got for part in halves(g)], 1)
    summed = dot(pick, table)
    row128 = iota((128, 128), 0)
    group128 = iota((128, 128), 1) >> 4
    keep = group128 == (row128 >> 5) + 2
    fold = fold_table()
    stack = []
    for a in range(3):
        one = summed[:, 256 * a : 256 * a + 128] + summed[:, 256 * a + 128 : 256 * a + 256]
        one = jnp.where(keep, one, 0.0)
        stack.append(one[0:32] + one[32:64] + one[64:96] + one[96:128])
    high, low = halves(jnp.concatenate(stack, 0))
    spread = dot(jnp.concatenate([high, low], 1), jnp.concatenate([fold, fold], 0))
    in_row = (iota((8, 128), 1) >> 4) == iota((8, 128), 0)
    sub_w = iota((8, WIDE), 0)
    grad = jnp.zeros((8, WIDE), F32)
    for a in range(3):
        tiles = []
        for r in range(4):
            piece = spread[32 * a + 8 * r : 32 * a + 8 * r + 8]
            tiles.append(jnp.sum(jnp.where(in_row, piece, 0.0), axis=0, keepdims=True))
        rim = jnp.where((lane < 32) | (lane >= 96), got[a], 0.0)
        tiles.append(jnp.sum(rim, axis=0, keepdims=True))
        grad = jnp.where(sub_w == a, jnp.concatenate(tiles, 1), grad)
    bands = [wide_ref[8 * b : 8 * b + 8, :] for b in range(3)]
    scale = wide_ref[24:32, :]
    delta = grad * scale
    for _ in range(2):
        total = jnp.zeros((8, WIDE), F32)
        for b in range(3):
            offset = offsets_ref[b]
            upper = pltpu.roll(delta, WIDE - offset, 1)
            lower = pltpu.roll(delta, offset, 1)
            total = total + bands[b] * (upper + lower)
        delta = (grad + total) * scale
    for a in range(3):
        for r in range(4):
            tile = delta[a : a + 1, 128 * r : 128 * r + 128]
            knots_ref[a, r : r + 1, :] = knots_in_ref[a, r : r + 1, :] + tile
    if last:
        outs[1][...] = sources_in_ref[...] + step_ref[...]
        return
    send_ref = outs[1]
    spreads = []
    for a in range(3):
        for r in range(4):
            tile = delta[a : a + 1, 128 * r : 128 * r + 128]
            spreads.append(jnp.where(in_row, tile, 0.0))
    high, low = halves(jnp.concatenate(spreads, 0))
    blocks = dot(jnp.concatenate([high, low], 1), jnp.concatenate([fold, fold], 0))
    tables = [part for a in range(3) for part in halves(blocks[32 * a : 32 * a + 32])]
    slots = [index[:, 16 * (2 + c) : 16 * (2 + c) + 1].astype(I32) - 1 for c in range(4)]
    slot = jnp.concatenate(slots, 0)
    by_block = jnp.where(iota((4 * SKY_N, 32), 1) == slot, 1.0, 0.0)
    found = dot(by_block, jnp.concatenate(tables, 1))
    group = lane >> 4
    front = jnp.zeros((SKY_N, 128), F32)
    back = jnp.zeros((SKY_N, 128), F32)
    for c in range(4):
        rows = found[SKY_N * c : SKY_N * (c + 1)]
        part = [
            rows[:, 256 * a : 256 * a + 128] + rows[:, 256 * a + 128 : 256 * a + 256]
            for a in range(3)
        ]
        front = jnp.where(group == c, part[0], jnp.where(group == c + 4, part[1], front))
        back = jnp.where(group == c, part[2], back)
    send_ref[:, 0, :] = front
    send_ref[:, 1, :] = back


def run_kernel(body, scalars, outs, *args, scratch=(), flops=10_000_000, **static):
    specs = [
        pl.BlockSpec(memory_space=pltpu.SMEM if i < scalars else pltpu.VMEM)
        for i in range(len(args))
    ]
    shapes = [o if isinstance(o, jax.ShapeDtypeStruct) else jax.ShapeDtypeStruct(o, F32) for o in outs]

    def kernel(*refs):
        body(*refs, **static)

    return pl.pallas_call(
        kernel,
        out_shape=shapes,
        in_specs=specs,
        out_specs=[pl.BlockSpec(memory_space=pltpu.VMEM) for _ in outs],
        scratch_shapes=[pltpu.VMEM(shape, F32) for shape in scratch],
        cost_estimate=pl.CostEstimate(flops=flops, bytes_accessed=2_000_000, transcendentals=0),
        compiler_params=pltpu.CompilerParams(vmem_limit_bytes=32 * 1024 * 1024),
    )(*args)


def half(*shape):
    return jax.ShapeDtypeStruct(shape, BF16)


def shifts(k):
    return [(i, (i + k) % TM_N) for i in range(TM_N)]


def per_device(
    observed,
    att_partials,
    src_partials,
    src_slot,
    knot_block,
    live_count,
    sources,
    inverses,
    attitude,
    band_coef,
    extra_diag,
    band_offsets,
):
    core = lax.axis_index("c").astype(I32).reshape(1)
    tm = lax.axis_index("tm").astype(I32).reshape(1)
    slot = src_slot.reshape(1, CROSS)
    kb = knot_block.reshape(1, CROSS)
    static = jnp.concatenate([band_coef.reshape(9, RUN), extra_diag.reshape(3, RUN)], 0)

    dense = jnp.broadcast_to(attitude.reshape(1, 3, 4, 128), (CHIPS, 3, 4, 128))
    near = lax.all_to_all(dense, ("x", "z"), 0, 0, tiled=True)
    chain = [s * TM_N + t for t in range(TM_N) for s in range(SKY_N)]
    pairs = list(zip(chain[:-1], chain[1:], strict=True))
    after = lax.ppermute(static[:, :128], SKY_TM, [(b, a) for a, b in pairs])
    (
        cols, places, by_source, base, by_lane, by_row, pack, index, peers, choose, up, down,
    ) = run_kernel(
        prepare_kernel, 2,
        [
            (128, 128), half(128, 256), half(128, SRC_N), (CROSS, ROWS), half(384, 128),
            half(384, 128), half(SKY_N, 256), (SKY_N, 128), half(128, SKY_N), (8, 128), (40, 128),
            (40, 128),
        ],
        live_count, core, observed, att_partials, src_partials, slot, kb, sources,
    )
    near, after, cols = lax.optimization_barrier((near, after, cols))
    far = lax.ppermute(near, "c", [(0, 1), (1, 0)])
    resid, plain, up, down = run_kernel(
        first_kernel, 1, [(CROSS, ROWS), (HEAD, 128), (HEAD + 40, 128), (HEAD + 40, 128)],
        live_count, near, far, att_partials, src_partials, cols, places, by_source, base, by_lane,
        choose, up, down,
    )
    across = lax.ppermute(plain, "tm", shifts(2))
    up = lax.ppermute(up, "tm", shifts(1))
    down = lax.ppermute(down, "tm", shifts(-1))
    back_shapes = [(SKY_N, 4, 128), (CROSS, ROWS), (5, SRC_N)]
    last_run, cols = lax.optimization_barrier((static[:, RUN - 128 :], cols))
    before = lax.ppermute(last_run, SKY_TM, pairs)
    (wide,) = run_kernel(
        widen_kernel, 0, [(32, WIDE)],
        band_coef.reshape(3, 3, 4, 128), extra_diag.reshape(3, 4, 128), before, after,
    )
    outgoing, resid, sources = run_kernel(
        return_kernel, 2, back_shapes,
        live_count, tm, plain, up, down, across, up, down, inverses, sources, resid,
        att_partials, src_partials, cols, by_source, by_row, pack, index,
        scratch=[(HEAD, 128)], second=False,
    )
    got = lax.all_to_all(outgoing, SKY, 0, 0, tiled=True)
    knots, served, pick = run_kernel(
        smooth_kernel, 1, [(3, 4, 128), (SKY_N, 2, 128), half(128, SKY_N)],
        band_offsets, got, pack, attitude.reshape(3, 4, 128), wide, choose, choose, last=False,
    )
    arrived = lax.all_to_all(served, SKY, 0, 0, tiled=True)
    resid, mine = run_kernel(
        middle_kernel, 1, [(CROSS, ROWS), (HEAD + 8, 128)],
        live_count, arrived, resid, att_partials, src_partials, cols, peers, by_source, by_lane,
        choose,
    )
    across = lax.ppermute(mine, "tm", shifts(2))
    below = lax.ppermute(mine, "tm", shifts(1))
    above = lax.ppermute(mine, "tm", shifts(-1))
    outgoing, resid, step = run_kernel(
        return_kernel, 2, back_shapes,
        live_count, tm, mine, below, above, across, up, down, inverses, sources, resid,
        att_partials, src_partials, cols, by_source, by_row, pack, index,
        scratch=[(HEAD, 128)], second=True,
    )
    got = lax.all_to_all(outgoing, SKY, 0, 0, tiled=True)
    knots, sources = run_kernel(
        smooth_kernel, 1, [(3, 4, 128), (5, SRC_N)],
        band_offsets, got, pick, knots, wide, sources, step, last=True,
    )
    return (sources, knots.reshape(3, 1, RUN))


def solution(mesh):
    torus = Mesh(mesh.devices.reshape(4, 8, 2, mesh.shape["tm"]), SKY_TM)
    return jax.shard_map(
        per_device,
        mesh=torus,
        in_specs=(
            P(SKY_TM, None),
            P(None, SKY_TM, None),
            P(None, SKY_TM, None),
            P(SKY_TM),
            P(SKY_TM),
            P(SKY_TM),
            P(None, SKY),
            P(None, None, SKY),
            P(None, "tm", SKY),
            P(None, None, "tm", SKY),
            P(None, "tm", SKY),
            P(),
        ),
        out_specs=(P(None, SKY), P(None, "tm", SKY)),
        check_vma=False,
    )
```

```python
import jax
import jax.numpy as jnp
from jax import lax
from jax.experimental import pallas as pl
from jax.experimental.pallas import tpu as pltpu
from jax.sharding import Mesh
from jax.sharding import PartitionSpec as P

F32 = jnp.float32
BF16 = jnp.bfloat16
I32 = jnp.int32
ROWS = 128
KNOTS = 16
CROSS = 128
SKY_N = 64
CHIPS = 32
TM_N = 4
SRC_N = 1024
RUN = 512
WIDE = RUN + 128
HEAD = 40
SKY = ("x", "z", "c")
SKY_TM = ("x", "z", "c", "tm")


def iota(shape, dim):
    return lax.broadcasted_iota(I32, shape, dim)


def dot(a, b):
    return jnp.dot(a.astype(BF16), b.astype(BF16), preferred_element_type=F32)


def dot_nt(a, b):
    return lax.dot_general(
        a.astype(BF16), b.astype(BF16), (((1,), (1,)), ((), ())), preferred_element_type=F32
    )


def halves(x):
    high = x.astype(BF16)
    return high, (x - high.astype(F32)).astype(BF16)


def thirds(x):
    high = x.astype(BF16).astype(F32)
    rest = x - high
    middle = rest.astype(BF16).astype(F32)
    return high, middle, rest - middle


def b_spline(moment_row, knot):
    tau = 1.5 + (KNOTS - 3) * (moment_row.astype(F32) + 0.5) / ROWS
    dist = jnp.abs(tau - knot.astype(F32))
    inner = 2.0 / 3.0 - dist * dist + 0.5 * dist * dist * dist
    rest = 2.0 - dist
    outer = rest * rest * rest / 6.0
    return jnp.where(dist < 1.0, inner, jnp.where(dist < 2.0, outer, 0.0))


def spline_by_lane():
    return b_spline(iota((128, 128), 1), iota((128, 128), 0) & 15)


def spline_by_row():
    return b_spline(iota((128, 128), 0), iota((128, 128), 1) & 15)


def fold_table():
    return jnp.where((iota((128, 128), 0) & 15) == (iota((128, 128), 1) & 15), 1.0, 0.0)


def attitude_term(att_ref, masked, table_ref):
    high, low = halves(jnp.concatenate(masked, 0))
    spread = dot(jnp.concatenate([high, low, high], 1), table_ref[...])
    total = jnp.zeros((CROSS, ROWS), F32)
    for a in range(3):
        total = total + att_ref[a].astype(F32) * spread[a * 128 : a * 128 + 128]
    return total


def send_normal(src_ref, resid, onehot, refs):
    lane = iota((128, 128), 1)
    square = jnp.zeros((128, 128), F32)
    for p in range(5):
        rhs = jnp.sum(src_ref[p].astype(F32) * resid, axis=1, keepdims=True)
        square = jnp.where(lane == p, rhs, square)
    rows = square.T[0:8]
    parts = dot(jnp.concatenate(thirds(rows), 0), onehot)
    normal = parts[0:8] + parts[8:16] + parts[16:24]
    for ref in refs:
        for j in range(8):
            ref[pl.ds(j, 5, stride=8), :] = normal[0:5, 128 * j : 128 * j + 128]


def gather_source(values8, onehot):
    parts = dot_nt(onehot, jnp.concatenate(thirds(values8), 0))
    return [
        parts[:, p : p + 1] + parts[:, 8 + p : 9 + p] + parts[:, 16 + p : 17 + p] for p in range(5)
    ]


def padded_rows(x):
    return jnp.concatenate([x, jnp.zeros((8 - x.shape[0], x.shape[1]), F32)], 0)


def column(cols_ref, i):
    return cols_ref[:, i : i + 1].astype(I32)


def stacked_spline(table):
    high, low = halves(table)
    return jnp.concatenate([high, high, low], 0)


def prepare_kernel(
    live_ref, core_ref, offsets_in_ref, obs_ref, att_ref, src_ref, slot_ref, kb_ref, sources_ref,
    bands_ref, extra_ref,
    cols_ref, places_ref, by_source_ref, base_ref, by_lane_ref, by_row_ref, pack_ref, index_ref,
    peers_ref, choose_ref, up_ref, down_ref, wide_ref, offsets_ref,
):
    live, core = live_ref[0], core_ref[0]
    for b in range(3):
        offsets_ref[b] = offsets_in_ref[b]
    kb, slot = kb_ref[...], slot_ref[...]
    h, lb = kb >> 5, kb & 31
    sub, lane = iota((128, 128), 0), iota((128, 128), 1)
    square = jnp.zeros((128, 128), F32)
    for i, row in enumerate((h, lb, slot)):
        square = jnp.where(sub == i, row.astype(F32), square)
    turned = square.T
    hc, lbc, slotc = (turned[:, i : i + 1].astype(I32) for i in range(3))
    same = hc == h
    c = jnp.sum(jnp.where(same & (sub < lane), 1.0, 0.0), axis=0, keepdims=True).astype(I32)
    cc = jnp.sum(jnp.where(same & (lane < sub), 1.0, 0.0), axis=1, keepdims=True)
    cols_ref[...] = jnp.where(lane == 3, cc, turned)
    cc = cc.astype(I32)
    group = lane >> 4

    place = (lbc >> 3) * CHIPS + (hc >> 1) + jnp.where((hc & 1) == core, 0, 128)
    places_ref[...] = jnp.where(iota((128, 256), 1) == place, 1.0, 0.0).astype(BF16)
    by_source = jnp.where(iota((128, SRC_N), 1) == slotc, 1.0, 0.0).astype(BF16)
    by_source_ref[...] = by_source
    values = gather_source(padded_rows(sources_ref[...]), by_source)
    src_term = jnp.zeros((CROSS, ROWS), F32)
    for p in range(5):
        src_term = src_term + src_ref[p].astype(F32) * values[p]
    base_ref[...] = obs_ref[...] - src_term
    by_lane_ref[...] = stacked_spline(spline_by_lane())
    by_row_ref[...] = stacked_spline(spline_by_row())

    peer = iota((SKY_N, 128), 0)
    to_row = jnp.where(lb <= 1, h - 1, jnp.where(lb >= 30, h + 1, jnp.full_like(h, -1)))
    own = jnp.where(peer == h, 1.0, 0.0)
    pack_ref[...] = jnp.concatenate([own, jnp.where(peer == to_row, 1.0, 0.0)], 1).astype(BF16)
    index_ref[...] = dot(own, jnp.where(group == cc + 2, (lbc + 1).astype(F32), 0.0))
    peers_ref[...] = jnp.where(iota((128, SKY_N), 1) == hc, 1.0, 0.0).astype(BF16)

    sub8 = iota((8, 128), 0)
    after = (h == SKY_N - 1) & (lb >= 30) & (sub8 < 4)
    before = (h == 0) & (lb <= 1) & (sub8 >= 4)
    chosen = (c == (sub8 & 3)) & (after | before) & (iota((8, 128), 1) < live)
    choose = jnp.where(chosen, 1.0, 0.0)
    choose_ref[...] = choose
    pieces = [att_ref[a] for a in range(3)] + [src_ref[p] for p in range(5)]
    ghosts = dot(choose, jnp.concatenate(pieces, 1))
    items = [ghosts[:, 128 * i : 128 * i + 128] for i in range(8)]
    ghost_slot = jnp.sum(choose * slot.astype(F32), axis=1, keepdims=True)
    ghost_block = jnp.sum(choose * lb.astype(F32), axis=1, keepdims=True)
    items.append(jnp.zeros((8, 128), F32))
    items.append(jnp.where(iota((8, 128), 1) < 64, ghost_slot, ghost_block))
    for q in range(5):
        even, odd = items[2 * q], items[2 * q + 1]
        up_ref[8 * q : 8 * q + 8, :] = jnp.concatenate([even[0:4], odd[0:4]], 0)
        down_ref[8 * q : 8 * q + 8, :] = jnp.concatenate([even[4:8], odd[4:8]], 0)

    bands = [axis_rows(bands_ref[b]) for b in range(3)]
    diag = axis_rows(extra_ref) + 2.0 * (bands[0] + bands[1] + bands[2])
    for b in range(3):
        wide_ref[8 * b : 8 * b + 8, :] = bands[b]
    wide_ref[24:32, :] = 1.0 / jnp.where(diag > 0.0, diag, 1.0)


def axis_rows(tiles):
    sub = iota((8, RUN), 0)
    out = jnp.zeros((8, RUN), F32)
    for a in range(3):
        out = jnp.where(sub == a, jnp.concatenate([tiles[a][r : r + 1] for r in range(4)], 1), out)
    return out


def payload_kernel(knots_hbm, bands_hbm, extra_hbm, out_ref, knots_ref, bands_ref, extra_ref, sems):
    copies = [
        pltpu.make_async_copy(source, target, sems.at[i])
        for i, (source, target) in enumerate(
            ((bands_hbm, bands_ref), (extra_hbm, extra_ref), (knots_hbm, knots_ref))
        )
    ]
    for copy in copies:
        copy.start()
    for copy in copies:
        copy.wait()
    lane = iota((1, 128), 1)

    def ends(tiles, width):
        low, high = tiles[0:1], tiles[3:4]
        return jnp.where(lane < width, low, jnp.where(lane >= 128 - width, high, 0.0))

    rows = []
    for a in range(3):
        bands = [bands_ref[b, a] for b in range(3)]
        diag = extra_ref[a] + 2.0 * (bands[0] + bands[1] + bands[2])
        row = ends(diag, 32) + pltpu.roll(ends(bands[0], 16), 48, 1)
        rows.append(row + pltpu.roll(ends(bands[1], 16), 80, 1))
    third = [ends(bands_ref[2, a], 16) for a in range(3)]
    rows.append(third[0] + pltpu.roll(third[1], 48, 1) + pltpu.roll(third[2], 80, 1))
    sub = iota((4, 128), 0)
    edge = jnp.zeros((4, 128), F32)
    for i, row in enumerate(rows):
        edge = jnp.where(sub == i, row, edge)
    for chip in range(CHIPS):
        out_ref[chip, 0:3] = knots_ref[...]
        out_ref[chip, 3] = edge


def rim_tiles(before, after):
    sub, lane = iota((8, 128), 0), iota((8, 128), 1)

    def tile(sources, width):
        out = jnp.zeros((8, 128), F32)
        for a, (row, turn) in enumerate(sources):
            both = [e[row : row + 1] for e in (after, before)]
            if turn:
                both = [pltpu.roll(e, 128 - turn, 1) for e in both]
            one = jnp.where(lane < width, both[0], jnp.where(lane >= 128 - width, both[1], 0.0))
            out = jnp.where(sub == a, one, out)
        return out

    bands = [
        tile([(a, 48) for a in range(3)], 16),
        tile([(a, 80) for a in range(3)], 16),
        tile([(3, 0), (3, 48), (3, 80)], 16),
    ]
    diag = tile([(a, 0) for a in range(3)], 32)
    return bands + [1.0 / jnp.where(diag > 0.0, diag, 1.0)]


def first_kernel(
    live_ref, core_ref, chip_ref, near_ref, far_ref, att_ref, src_ref, cols_ref, places_ref,
    by_source_ref, base_ref, by_lane_ref, choose_ref, up_in_ref, down_in_ref,
    resid_ref, plain_ref, up_ref, down_ref, sides_ref,
):
    tables = []
    for a in range(3):
        rows = [ref[:, a, r, :] for ref in (near_ref, far_ref) for r in range(4)]
        tables += halves(jnp.concatenate(rows, 0))
    found = dot(places_ref[...], jnp.concatenate(tables, 1))
    mine = (iota((128, 128), 1) >> 4) == (column(cols_ref, 1) & 7)
    masked = []
    for a in range(3):
        whole = found[:, 256 * a : 256 * a + 128] + found[:, 256 * a + 128 : 256 * a + 256]
        masked.append(jnp.where(mine, whole, 0.0))
    used = jnp.where(iota((CROSS, 1), 0) < live_ref[0], 1.0, 0.0)
    resid = (base_ref[...] - attitude_term(att_ref, masked, by_lane_ref)) * used
    resid_ref[...] = resid
    send_normal(src_ref, resid, by_source_ref[...], (plain_ref, up_ref, down_ref))
    ghosts = dot(choose_ref[...], jnp.concatenate(halves(resid), 1))
    ghosts = ghosts[:, 0:128] + ghosts[:, 128:256]
    up_ref[HEAD : HEAD + 40, :] = up_in_ref[...]
    down_ref[HEAD : HEAD + 40, :] = down_in_ref[...]
    up_ref[HEAD + 32 : HEAD + 36, :] = ghosts[0:4]
    down_ref[HEAD + 32 : HEAD + 36, :] = ghosts[4:8]
    core, chip = core_ref[0], chip_ref[0]
    before = jnp.where(core == 0, jnp.maximum(chip - 1, 0), chip)
    after = jnp.where(core == 0, chip, jnp.minimum(chip + 1, CHIPS - 1))
    sides_ref[0:4, :] = far_ref[before, 3]
    sides_ref[4:8, :] = far_ref[after, 3]
    empty = jnp.zeros((4, 128), F32)
    final = jnp.where(core == 1, near_ref[CHIPS - 1, 3], far_ref[CHIPS - 1, 3])
    initial = jnp.where(core == 0, near_ref[0, 3], far_ref[0, 3])
    up_ref[HEAD + 40 : HEAD + 48, :] = jnp.concatenate([final, empty], 0)
    down_ref[HEAD + 40 : HEAD + 48, :] = jnp.concatenate([initial, empty], 0)


def middle_kernel(
    live_ref, got_ref, resid_in_ref, att_ref, src_ref, cols_ref, peers_ref, by_source_ref,
    by_lane_ref, choose_ref, resid_ref, send_ref,
):
    table = jnp.concatenate([*halves(got_ref[:, 0, :]), *halves(got_ref[:, 1, :])], 1)
    found = dot(peers_ref[...], table)
    front = found[:, 0:128] + found[:, 128:256]
    back = found[:, 256:384] + found[:, 384:512]
    group, cc = iota((128, 128), 1) >> 4, column(cols_ref, 3)
    masked = [
        jnp.where(group == cc, front, 0.0),
        jnp.where(group == cc + 4, front, 0.0),
        jnp.where(group == cc, back, 0.0),
    ]
    used = jnp.where(iota((CROSS, 1), 0) < live_ref[0], 1.0, 0.0)
    resid = resid_in_ref[...] - attitude_term(att_ref, masked, by_lane_ref) * used
    resid_ref[...] = resid
    send_normal(src_ref, resid, by_source_ref[...], (send_ref,))
    ghosts = dot(choose_ref[...], jnp.concatenate(halves(resid), 1))
    send_ref[HEAD : HEAD + 8, :] = ghosts[:, 0:128] + ghosts[:, 128:256]


def return_kernel(
    live_ref, tm_ref, across_ref, own_ref, below_ref, above_ref, up_ref, down_ref, inverses_ref,
    sources_in_ref, resid_in_ref, att_ref, src_ref, cols_ref, by_source_ref, by_row_ref, pack_ref,
    index_ref, out_ref, resid_ref, sources_ref, total_ref, *, second,
):
    tm = tm_ref[0]
    total_ref[...] = (
        own_ref[0:HEAD, :] + across_ref[0:HEAD, :] + below_ref[0:HEAD, :] + above_ref[0:HEAD, :]
    )
    normal = jnp.concatenate([total_ref[pl.ds(j, 5, stride=8), :] for j in range(8)], 1)
    sub8 = iota((8, SRC_N), 0)
    step = jnp.zeros((8, SRC_N), F32)
    for p in range(5):
        row = jnp.sum(inverses_ref[p] * normal, axis=0, keepdims=True)
        step = jnp.where(sub8 == p, row, step)
    sources_ref[...] = step[0:5] if second else sources_in_ref[...] + step[0:5]
    ghost8 = iota((8, 128), 0)
    there = jnp.where(ghost8 < 4, jnp.where(tm > 0, 1.0, 0.0), jnp.where(tm < TM_N - 1, 1.0, 0.0))

    def item(i):
        row = HEAD + 4 * i
        return jnp.concatenate([up_ref[row : row + 4, :], down_ref[row : row + 4, :]], 0)

    facts = item(9)
    ghost_slot = facts[:, 0:1].astype(I32)
    ghost_block = facts[:, 64:65].astype(I32)
    ghost_onehot = jnp.where(iota((8, SRC_N), 1) == ghost_slot, 1.0, 0.0)
    values = gather_source(step, by_source_ref[...])
    ghost_values = gather_source(step, ghost_onehot)
    change = jnp.zeros((CROSS, ROWS), F32)
    ghost_change = jnp.zeros((8, ROWS), F32)
    for p in range(5):
        change = change + src_ref[p].astype(F32) * values[p]
        ghost_change = ghost_change + item(3 + p) * ghost_values[p]
    used = jnp.where(iota((CROSS, 1), 0) < live_ref[0], 1.0, 0.0)
    resid = resid_in_ref[...] - used * change
    resid_ref[...] = resid
    if second:
        ghost_resid = jnp.concatenate(
            [below_ref[HEAD : HEAD + 4, :], above_ref[HEAD + 4 : HEAD + 8, :]], 0
        )
    else:
        ghost_resid = item(8)
    ghost_resid = (ghost_resid - ghost_change) * there
    rows = [att_ref[a].astype(F32) * resid for a in range(3)]
    rows += [item(a) * ghost_resid for a in range(3)]
    high, low = halves(jnp.concatenate(rows, 0))
    grads = dot(jnp.concatenate([high, low, high], 1), by_row_ref[...])
    lbc, cc = column(cols_ref, 1), column(cols_ref, 3)
    group = iota((128, 128), 1) >> 4
    edge_group = jnp.where(lbc <= 1, lbc, lbc - 24)
    own = group == cc + 2
    edge = group == edge_group
    top, bottom = [], []
    for a in range(3):
        g = grads[128 * a : 128 * a + 128]
        top += halves(jnp.where(own, g, 0.0))
        bottom += halves(jnp.where(edge, g, 0.0))
    table = jnp.concatenate([jnp.concatenate(top, 1), jnp.concatenate(bottom, 1)], 0)
    packed = dot(pack_ref[...], table)
    peer = iota((SKY_N, 128), 0)
    ghost_group = iota((8, 128), 1) >> 4
    ghost_own = ghost_group == jnp.where(ghost8[:, 0:1] < 4, ghost_block - 24, ghost_block)
    for a in range(3):
        ghost = jnp.where(ghost_own, grads[384 + 8 * a : 392 + 8 * a], 0.0)
        from_below = jnp.sum(jnp.where(ghost8 < 4, ghost, 0.0), axis=0, keepdims=True)
        from_above = jnp.sum(jnp.where(ghost8 >= 4, ghost, 0.0), axis=0, keepdims=True)
        block = packed[:, 256 * a : 256 * a + 128] + packed[:, 256 * a + 128 : 256 * a + 256]
        block = block + jnp.where(peer == 0, from_below, 0.0)
        block = block + jnp.where(peer == SKY_N - 1, from_above, 0.0)
        out_ref[:, a, :] = block
    out_ref[:, 3, :] = index_ref[...]


def smooth_kernel(
    offsets_ref, chip_ref, core_ref, tm_ref, got_ref, knots_in_ref, wide_ref, one_ref, two_ref,
    three_ref, four_ref, *outs, last,
):
    knots_ref = outs[0]
    lane = iota((SKY_N, 128), 1)
    if last:
        sources_in_ref, step_ref, pick_ref, rims_ref = one_ref, two_ref, three_ref, four_ref
        pick = pick_ref[...]
        rims = [rims_ref[8 * i : 8 * i + 8, :] for i in range(4)]
    else:
        sides_ref, up_ref, down_ref = one_ref, two_ref, three_ref
        place, tm = chip_ref[0] * 2 + core_ref[0], tm_ref[0]
        below = jnp.where(tm > 0, up_ref[HEAD + 40 : HEAD + 44, :], 0.0)
        above = jnp.where(tm < TM_N - 1, down_ref[HEAD + 40 : HEAD + 44, :], 0.0)
        before = jnp.where(place == 0, below, sides_ref[0:4, :])
        after = jnp.where(place == SKY_N - 1, above, sides_ref[4:8, :])
        rims = rim_tiles(before, after)
        for i in range(4):
            outs[3][8 * i : 8 * i + 8, :] = rims[i]
        index = got_ref[:, 3, :]
        square = jnp.concatenate([index, jnp.zeros((128 - SKY_N, 128), F32)], 0).T
        block32 = (iota((32, SKY_N), 0) + 1).astype(F32)
        pick = jnp.concatenate(
            [
                jnp.where(square[16 * (2 + c) : 16 * (2 + c) + 1, 0:SKY_N] == block32, 1.0, 0.0)
                for c in range(4)
            ],
            0,
        ).astype(BF16)
        outs[2][...] = pick
    got = [got_ref[:, a, :] for a in range(3)]
    table = jnp.concatenate([part for g in got for part in halves(g)], 1)
    summed = dot(pick, table)
    row128 = iota((128, 128), 0)
    group128 = iota((128, 128), 1) >> 4
    keep = group128 == (row128 >> 5) + 2
    fold = fold_table()
    stack = []
    for a in range(3):
        one = summed[:, 256 * a : 256 * a + 128] + summed[:, 256 * a + 128 : 256 * a + 256]
        one = jnp.where(keep, one, 0.0)
        stack.append(one[0:32] + one[32:64] + one[64:96] + one[96:128])
    high, low = halves(jnp.concatenate(stack, 0))
    spread = dot(jnp.concatenate([high, low], 1), jnp.concatenate([fold, fold], 0))
    in_row = (iota((8, 128), 1) >> 4) == iota((8, 128), 0)
    sub_w = iota((8, WIDE), 0)
    grad = jnp.zeros((8, WIDE), F32)
    for a in range(3):
        tiles = []
        for r in range(4):
            piece = spread[32 * a + 8 * r : 32 * a + 8 * r + 8]
            tiles.append(jnp.sum(jnp.where(in_row, piece, 0.0), axis=0, keepdims=True))
        rim = jnp.where((lane < 32) | (lane >= 96), got[a], 0.0)
        tiles.append(jnp.sum(rim, axis=0, keepdims=True))
        grad = jnp.where(sub_w == a, jnp.concatenate(tiles, 1), grad)
    *bands, scale = (
        jnp.concatenate([wide_ref[8 * i : 8 * i + 8, :], rims[i]], 1) for i in range(4)
    )
    delta = grad * scale
    for _ in range(2):
        total = jnp.zeros((8, WIDE), F32)
        for b in range(3):
            offset = offsets_ref[b]
            upper = pltpu.roll(delta, WIDE - offset, 1)
            lower = pltpu.roll(delta, offset, 1)
            total = total + bands[b] * (upper + lower)
        delta = (grad + total) * scale
    for a in range(3):
        for r in range(4):
            tile = delta[a : a + 1, 128 * r : 128 * r + 128]
            knots_ref[a, r : r + 1, :] = knots_in_ref[a, r : r + 1, :] + tile
    if last:
        outs[1][...] = sources_in_ref[...] + step_ref[...]
        return
    send_ref = outs[1]
    spreads = []
    for a in range(3):
        for r in range(4):
            tile = delta[a : a + 1, 128 * r : 128 * r + 128]
            spreads.append(jnp.where(in_row, tile, 0.0))
    high, low = halves(jnp.concatenate(spreads, 0))
    blocks = dot(jnp.concatenate([high, low], 1), jnp.concatenate([fold, fold], 0))
    tables = [part for a in range(3) for part in halves(blocks[32 * a : 32 * a + 32])]
    slots = [index[:, 16 * (2 + c) : 16 * (2 + c) + 1].astype(I32) - 1 for c in range(4)]
    slot = jnp.concatenate(slots, 0)
    by_block = jnp.where(iota((4 * SKY_N, 32), 1) == slot, 1.0, 0.0)
    found = dot(by_block, jnp.concatenate(tables, 1))
    group = lane >> 4
    front = jnp.zeros((SKY_N, 128), F32)
    back = jnp.zeros((SKY_N, 128), F32)
    for c in range(4):
        rows = found[SKY_N * c : SKY_N * (c + 1)]
        part = [
            rows[:, 256 * a : 256 * a + 128] + rows[:, 256 * a + 128 : 256 * a + 256]
            for a in range(3)
        ]
        front = jnp.where(group == c, part[0], jnp.where(group == c + 4, part[1], front))
        back = jnp.where(group == c, part[2], back)
    send_ref[:, 0, :] = front
    send_ref[:, 1, :] = back


def run_kernel(body, scalars, outs, *args, scratch=(), flops=10_000_000, **static):
    specs = [
        pl.BlockSpec(memory_space=pltpu.SMEM if i < scalars else pltpu.VMEM)
        for i in range(len(args))
    ]
    shapes = [o if isinstance(o, jax.ShapeDtypeStruct) else jax.ShapeDtypeStruct(o, F32) for o in outs]

    def kernel(*refs):
        body(*refs, **static)

    return pl.pallas_call(
        kernel,
        out_shape=shapes,
        in_specs=specs,
        out_specs=[
            pl.BlockSpec(memory_space=pltpu.SMEM if s.dtype == I32 else pltpu.VMEM) for s in shapes
        ],
        scratch_shapes=[pltpu.VMEM(shape, F32) for shape in scratch],
        cost_estimate=pl.CostEstimate(flops=flops, bytes_accessed=2_000_000, transcendentals=0),
        compiler_params=pltpu.CompilerParams(vmem_limit_bytes=32 * 1024 * 1024),
    )(*args)


def half(*shape):
    return jax.ShapeDtypeStruct(shape, BF16)


def shifts(k):
    return [(i, (i + k) % TM_N) for i in range(TM_N)]


def per_device(
    observed,
    att_partials,
    src_partials,
    src_slot,
    knot_block,
    live_count,
    sources,
    inverses,
    attitude,
    band_coef,
    extra_diag,
    band_offsets,
):
    core = lax.axis_index("c").astype(I32).reshape(1)
    tm = lax.axis_index("tm").astype(I32).reshape(1)
    slot = src_slot.reshape(1, CROSS)
    kb = knot_block.reshape(1, CROSS)
    chip = lax.axis_index(("x", "z")).astype(I32).reshape(1)
    knots = attitude.reshape(3, 4, 128)
    bands = band_coef.reshape(3, 3, 4, 128)
    extra = extra_diag.reshape(3, 4, 128)

    dense = pl.pallas_call(
        payload_kernel,
        out_shape=jax.ShapeDtypeStruct((CHIPS, 4, 4, 128), F32),
        in_specs=[pl.BlockSpec(memory_space=pl.ANY)] * 3,
        out_specs=pl.BlockSpec(memory_space=pltpu.VMEM),
        scratch_shapes=[
            pltpu.VMEM((3, 4, 128), F32),
            pltpu.VMEM((3, 3, 4, 128), F32),
            pltpu.VMEM((3, 4, 128), F32),
            pltpu.SemaphoreType.DMA((3,)),
        ],
        compiler_params=pltpu.CompilerParams(vmem_limit_bytes=56 * 1024 * 1024),
    )(knots, bands, extra)
    near = lax.all_to_all(dense, ("x", "z"), 0, 0, tiled=True)
    (
        cols, places, by_source, base, by_lane, by_row, pack, index, peers, choose, up, down, wide,
        offsets,
    ) = run_kernel(
        prepare_kernel, 3,
        [
            (128, 128), half(128, 256), half(128, SRC_N), (CROSS, ROWS), half(384, 128),
            half(384, 128), half(SKY_N, 256), (SKY_N, 128), half(128, SKY_N), (8, 128), (40, 128),
            (40, 128), (32, RUN), jax.ShapeDtypeStruct((3,), I32),
        ],
        live_count, core, band_offsets, observed, att_partials, src_partials, slot, kb, sources, bands, extra,
    )
    near, cols = lax.optimization_barrier((near, cols))
    far = lax.ppermute(near, "c", [(0, 1), (1, 0)])
    resid, plain, up, down, sides = run_kernel(
        first_kernel, 3,
        [(CROSS, ROWS), (HEAD, 128), (HEAD + 48, 128), (HEAD + 48, 128), (8, 128)],
        live_count, core, chip, near, far, att_partials, src_partials, cols, places, by_source,
        base, by_lane, choose, up, down,
    )
    across = lax.ppermute(plain, "tm", shifts(2))
    up = lax.ppermute(up, "tm", shifts(1))
    down = lax.ppermute(down, "tm", shifts(-1))
    back_shapes = [(SKY_N, 4, 128), (CROSS, ROWS), (5, SRC_N)]
    outgoing, resid, sources = run_kernel(
        return_kernel, 2, back_shapes,
        live_count, tm, across, plain, up, down, up, down, inverses, sources, resid,
        att_partials, src_partials, cols, by_source, by_row, pack, index,
        scratch=[(HEAD, 128)], second=False,
    )
    got = lax.all_to_all(outgoing, SKY, 0, 0, tiled=True)
    knots, served, pick, rims = run_kernel(
        smooth_kernel, 4, [(3, 4, 128), (SKY_N, 2, 128), half(128, SKY_N), (32, 128)],
        offsets, chip, core, tm, got, knots, wide, sides, up, down, choose, last=False,
    )
    arrived = lax.all_to_all(served, SKY, 0, 0, tiled=True)
    resid, mine = run_kernel(
        middle_kernel, 1, [(CROSS, ROWS), (HEAD + 8, 128)],
        live_count, arrived, resid, att_partials, src_partials, cols, peers, by_source, by_lane,
        choose,
    )
    across = lax.ppermute(mine, "tm", shifts(2))
    below = lax.ppermute(mine, "tm", shifts(1))
    above = lax.ppermute(mine, "tm", shifts(-1))
    outgoing, resid, step = run_kernel(
        return_kernel, 2, back_shapes,
        live_count, tm, across, mine, below, above, up, down, inverses, sources, resid,
        att_partials, src_partials, cols, by_source, by_row, pack, index,
        scratch=[(HEAD, 128)], second=True,
    )
    got = lax.all_to_all(outgoing, SKY, 0, 0, tiled=True)
    knots, sources = run_kernel(
        smooth_kernel, 4, [(3, 4, 128), (5, SRC_N)],
        offsets, chip, core, tm, got, knots, wide, sources, step, pick, rims, last=True,
    )
    return (sources, knots.reshape(3, 1, RUN))


def solution(mesh):
    torus = Mesh(mesh.devices.reshape(4, 8, 2, mesh.shape["tm"]), SKY_TM)
    return jax.shard_map(
        per_device,
        mesh=torus,
        in_specs=(
            P(SKY_TM, None),
            P(None, SKY_TM, None),
            P(None, SKY_TM, None),
            P(SKY_TM),
            P(SKY_TM),
            P(SKY_TM),
            P(None, SKY),
            P(None, None, SKY),
            P(None, "tm", SKY),
            P(None, None, "tm", SKY),
            P(None, "tm", SKY),
            P(),
        ),
        out_specs=(P(None, SKY), P(None, "tm", SKY)),
        check_vma=False,
    )
```

```python
import jax
import jax.numpy as jnp
from jax import lax
from jax.experimental import pallas as pl
from jax.experimental.pallas import tpu as pltpu
from jax.sharding import Mesh
from jax.sharding import PartitionSpec as P

F32 = jnp.float32
BF16 = jnp.bfloat16
I32 = jnp.int32
ROWS = 128
KNOTS = 16
CROSS = 128
SKY_N = 64
CHIPS = 32
TM_N = 4
SRC_N = 1024
RUN = 512
HEAD = 40
SKY = ("x", "z", "c")
SKY_TM = ("x", "z", "c", "tm")


def iota(shape, dim):
    return lax.broadcasted_iota(I32, shape, dim)


def dot(a, b):
    return jnp.dot(a.astype(BF16), b.astype(BF16), preferred_element_type=F32)


def dot_nt(a, b):
    return lax.dot_general(
        a.astype(BF16), b.astype(BF16), (((1,), (1,)), ((), ())), preferred_element_type=F32
    )


def halves(x):
    high = x.astype(BF16)
    return high, (x - high.astype(F32)).astype(BF16)


def split_dot(twice, values):
    return dot(twice, jnp.concatenate(halves(values), 0))


def thirds(x):
    high = x.astype(BF16).astype(F32)
    rest = x - high
    middle = rest.astype(BF16).astype(F32)
    return high, middle, rest - middle


def b_spline(moment_row, knot):
    tau = 1.5 + (KNOTS - 3) * (moment_row.astype(F32) + 0.5) / ROWS
    dist = jnp.abs(tau - knot.astype(F32))
    inner = 2.0 / 3.0 - dist * dist + 0.5 * dist * dist * dist
    rest = 2.0 - dist
    outer = rest * rest * rest / 6.0
    return jnp.where(dist < 1.0, inner, jnp.where(dist < 2.0, outer, 0.0))


def spline_by_lane():
    return b_spline(iota((128, 128), 1), iota((128, 128), 0) & 15)


def spline_by_row():
    return b_spline(iota((128, 128), 0), iota((128, 128), 1) & 15)


def fold_table():
    return jnp.where((iota((128, 128), 0) & 15) == (iota((128, 128), 1) & 15), 1.0, 0.0)


def attitude_term(att_ref, masked, table_ref):
    high, low = halves(jnp.concatenate(masked, 0))
    spread = dot(jnp.concatenate([high, low, high], 1), table_ref[...])
    total = jnp.zeros((CROSS, ROWS), F32)
    for a in range(3):
        total = total + att_ref[a].astype(F32) * spread[a * 128 : a * 128 + 128]
    return total


def send_normal(src_ref, resid, onehot, refs):
    lane = iota((128, 128), 1)
    square = jnp.zeros((128, 128), F32)
    for p in range(5):
        rhs = jnp.sum(src_ref[p].astype(F32) * resid, axis=1, keepdims=True)
        square = jnp.where(lane == p, rhs, square)
    rows = square.T[0:8]
    parts = dot(jnp.concatenate(thirds(rows), 0), onehot)
    normal = parts[0:8] + parts[8:16] + parts[16:24]
    for ref in refs:
        for j in range(8):
            ref[pl.ds(j, 5, stride=8), :] = normal[0:5, 128 * j : 128 * j + 128]


def gather_source(values8, onehot):
    parts = dot_nt(onehot, jnp.concatenate(thirds(values8), 0))
    return [
        parts[:, p : p + 1] + parts[:, 8 + p : 9 + p] + parts[:, 16 + p : 17 + p] for p in range(5)
    ]


def padded_rows(x):
    return jnp.concatenate([x, jnp.zeros((8 - x.shape[0], x.shape[1]), F32)], 0)


def column(cols_ref, i):
    return cols_ref[:, i : i + 1].astype(I32)


def stacked_spline(table):
    high, low = halves(table)
    return jnp.concatenate([high, high, low], 0)


def prepare_kernel(
    live_ref, core_ref, offsets_in_ref, obs_ref, att_ref, src_ref, slot_ref, kb_ref, sources_ref,
    bands_ref, extra_ref,
    cols_ref, places_ref, by_source_ref, base_ref, by_lane_ref, by_row_ref, pack_ref, index_ref,
    peers_ref, choose_ref, up_ref, down_ref, wide_ref, offsets_ref,
):
    live, core = live_ref[0], core_ref[0]
    for b in range(3):
        offsets_ref[b] = offsets_in_ref[b]
    kb, slot = kb_ref[...], slot_ref[...]
    h, lb = kb >> 5, kb & 31
    sub, lane = iota((128, 128), 0), iota((128, 128), 1)
    square = jnp.zeros((128, 128), F32)
    for i, row in enumerate((h, lb, slot)):
        square = jnp.where(sub == i, row.astype(F32), square)
    turned = square.T
    hc, lbc, slotc = (turned[:, i : i + 1].astype(I32) for i in range(3))
    same = hc == h
    c = jnp.sum(jnp.where(same & (sub < lane), 1.0, 0.0), axis=0, keepdims=True).astype(I32)
    cc = jnp.sum(jnp.where(same & (lane < sub), 1.0, 0.0), axis=1, keepdims=True)
    cols_ref[...] = jnp.where(lane == 3, cc, turned)
    cc = cc.astype(I32)
    group = lane >> 4

    place = (lbc >> 3) * CHIPS + (hc >> 1) + jnp.where((hc & 1) == core, 0, 128)
    places_ref[...] = jnp.where(iota((128, 256), 1) == place, 1.0, 0.0).astype(BF16)
    by_source = jnp.where(iota((128, SRC_N), 1) == slotc, 1.0, 0.0).astype(BF16)
    by_source_ref[...] = by_source
    values = gather_source(padded_rows(sources_ref[...]), by_source)
    src_term = jnp.zeros((CROSS, ROWS), F32)
    for p in range(5):
        src_term = src_term + src_ref[p].astype(F32) * values[p]
    base_ref[...] = obs_ref[...] - src_term
    by_lane_ref[...] = stacked_spline(spline_by_lane())
    by_row_ref[...] = stacked_spline(spline_by_row())

    peer = iota((SKY_N, 128), 0)
    to_row = jnp.where(lb <= 1, h - 1, jnp.where(lb >= 30, h + 1, jnp.full_like(h, -1)))
    own = jnp.where(peer == h, 1.0, 0.0)
    edge = jnp.where(peer == to_row, 1.0, 0.0)
    pack_ref[...] = jnp.concatenate([own, edge, own, edge], 1).astype(BF16)
    index_ref[...] = dot(own, jnp.where(group == cc + 2, (lbc + 1).astype(F32), 0.0))
    peers_ref[...] = jnp.where((iota((128, 128), 1) & 63) == hc, 1.0, 0.0).astype(BF16)

    sub8 = iota((8, 128), 0)
    after = (h == SKY_N - 1) & (lb >= 30) & (sub8 < 4)
    before = (h == 0) & (lb <= 1) & (sub8 >= 4)
    chosen = (c == (sub8 & 3)) & (after | before) & (iota((8, 128), 1) < live)
    choose = jnp.where(chosen, 1.0, 0.0)
    choose_ref[...] = choose
    pieces = [att_ref[a] for a in range(3)] + [src_ref[p] for p in range(5)]
    ghosts = dot(choose, jnp.concatenate(pieces, 1))
    items = [ghosts[:, 128 * i : 128 * i + 128] for i in range(8)]
    ghost_slot = jnp.sum(choose * slot.astype(F32), axis=1, keepdims=True)
    ghost_block = jnp.sum(choose * lb.astype(F32), axis=1, keepdims=True)
    items.append(jnp.zeros((8, 128), F32))
    items.append(jnp.where(iota((8, 128), 1) < 64, ghost_slot, ghost_block))
    for q in range(5):
        even, odd = items[2 * q], items[2 * q + 1]
        up_ref[8 * q : 8 * q + 8, :] = jnp.concatenate([even[0:4], odd[0:4]], 0)
        down_ref[8 * q : 8 * q + 8, :] = jnp.concatenate([even[4:8], odd[4:8]], 0)

    bands = [axis_rows(bands_ref[b]) for b in range(3)]
    diag = axis_rows(extra_ref) + 2.0 * (bands[0] + bands[1] + bands[2])
    for b in range(3):
        wide_ref[8 * b : 8 * b + 8, :] = bands[b]
    wide_ref[24:32, :] = 1.0 / jnp.where(diag > 0.0, diag, 1.0)


def axis_rows(tiles):
    sub = iota((8, RUN), 0)
    out = jnp.zeros((8, RUN), F32)
    for a in range(3):
        out = jnp.where(sub == a, jnp.concatenate([tiles[a][r : r + 1] for r in range(4)], 1), out)
    return out


def payload_kernel(knots_hbm, bands_hbm, extra_hbm, out_ref, knots_ref, bands_ref, extra_ref, sems):
    copies = [
        pltpu.make_async_copy(source, target, sems.at[i])
        for i, (source, target) in enumerate(
            ((bands_hbm, bands_ref), (extra_hbm, extra_ref), (knots_hbm, knots_ref))
        )
    ]
    for copy in copies:
        copy.start()
    for copy in copies:
        copy.wait()
    lane = iota((1, 128), 1)

    def ends(tiles, width):
        low, high = tiles[0:1], tiles[3:4]
        return jnp.where(lane < width, low, jnp.where(lane >= 128 - width, high, 0.0))

    rows = []
    for a in range(3):
        bands = [bands_ref[b, a] for b in range(3)]
        diag = extra_ref[a] + 2.0 * (bands[0] + bands[1] + bands[2])
        row = ends(diag, 32) + pltpu.roll(ends(bands[0], 16), 48, 1)
        rows.append(row + pltpu.roll(ends(bands[1], 16), 80, 1))
    third = [ends(bands_ref[2, a], 16) for a in range(3)]
    rows.append(third[0] + pltpu.roll(third[1], 48, 1) + pltpu.roll(third[2], 80, 1))
    sub = iota((4, 128), 0)
    edge = jnp.zeros((4, 128), F32)
    for i, row in enumerate(rows):
        edge = jnp.where(sub == i, row, edge)
    for chip in range(CHIPS):
        out_ref[chip, 0:3] = knots_ref[...]
        out_ref[chip, 3] = edge


def rim_tiles(before, after):
    sub, lane = iota((8, 128), 0), iota((8, 128), 1)

    def tile(sources, width):
        out = jnp.zeros((8, 128), F32)
        for a, (row, turn) in enumerate(sources):
            both = [e[row : row + 1] for e in (after, before)]
            if turn:
                both = [pltpu.roll(e, 128 - turn, 1) for e in both]
            one = jnp.where(lane < width, both[0], jnp.where(lane >= 128 - width, both[1], 0.0))
            out = jnp.where(sub == a, one, out)
        return out

    bands = [
        tile([(a, 48) for a in range(3)], 16),
        tile([(a, 80) for a in range(3)], 16),
        tile([(3, 0), (3, 48), (3, 80)], 16),
    ]
    diag = tile([(a, 0) for a in range(3)], 32)
    return bands + [1.0 / jnp.where(diag > 0.0, diag, 1.0)]


def first_kernel(
    live_ref, core_ref, chip_ref, near_ref, far_ref, att_ref, src_ref, cols_ref, places_ref,
    by_source_ref, base_ref, by_lane_ref, choose_ref, up_in_ref, down_in_ref,
    resid_ref, plain_ref, up_ref, down_ref, sides_ref,
):
    tables = []
    for a in range(3):
        rows = [ref[:, a, r, :] for ref in (near_ref, far_ref) for r in range(4)]
        tables += halves(jnp.concatenate(rows, 0))
    found = dot(places_ref[...], jnp.concatenate(tables, 1))
    mine = (iota((128, 128), 1) >> 4) == (column(cols_ref, 1) & 7)
    masked = []
    for a in range(3):
        whole = found[:, 256 * a : 256 * a + 128] + found[:, 256 * a + 128 : 256 * a + 256]
        masked.append(jnp.where(mine, whole, 0.0))
    used = jnp.where(iota((CROSS, 1), 0) < live_ref[0], 1.0, 0.0)
    resid = (base_ref[...] - attitude_term(att_ref, masked, by_lane_ref)) * used
    resid_ref[...] = resid
    send_normal(src_ref, resid, by_source_ref[...], (plain_ref, up_ref, down_ref))
    ghosts = dot(choose_ref[...], jnp.concatenate(halves(resid), 1))
    ghosts = ghosts[:, 0:128] + ghosts[:, 128:256]
    up_ref[HEAD : HEAD + 40, :] = up_in_ref[...]
    down_ref[HEAD : HEAD + 40, :] = down_in_ref[...]
    up_ref[HEAD + 32 : HEAD + 36, :] = ghosts[0:4]
    down_ref[HEAD + 32 : HEAD + 36, :] = ghosts[4:8]
    core, chip = core_ref[0], chip_ref[0]
    before = jnp.where(core == 0, jnp.maximum(chip - 1, 0), chip)
    after = jnp.where(core == 0, chip, jnp.minimum(chip + 1, CHIPS - 1))
    sides_ref[0:4, :] = far_ref[before, 3]
    sides_ref[4:8, :] = far_ref[after, 3]
    empty = jnp.zeros((4, 128), F32)
    final = jnp.where(core == 1, near_ref[CHIPS - 1, 3], far_ref[CHIPS - 1, 3])
    initial = jnp.where(core == 0, near_ref[0, 3], far_ref[0, 3])
    up_ref[HEAD + 40 : HEAD + 48, :] = jnp.concatenate([final, empty], 0)
    down_ref[HEAD + 40 : HEAD + 48, :] = jnp.concatenate([initial, empty], 0)


def middle_kernel(
    live_ref, got_ref, resid_in_ref, att_ref, src_ref, cols_ref, peers_ref, by_source_ref,
    by_lane_ref, choose_ref, resid_ref, send_ref,
):
    found = split_dot(peers_ref[...], jnp.concatenate([got_ref[:, 0, :], got_ref[:, 1, :]], 1))
    front, back = found[:, 0:128], found[:, 128:256]
    group, cc = iota((128, 128), 1) >> 4, column(cols_ref, 3)
    masked = [
        jnp.where(group == cc, front, 0.0),
        jnp.where(group == cc + 4, front, 0.0),
        jnp.where(group == cc, back, 0.0),
    ]
    used = jnp.where(iota((CROSS, 1), 0) < live_ref[0], 1.0, 0.0)
    resid = resid_in_ref[...] - attitude_term(att_ref, masked, by_lane_ref) * used
    resid_ref[...] = resid
    send_normal(src_ref, resid, by_source_ref[...], (send_ref,))
    ghosts = dot(choose_ref[...], jnp.concatenate(halves(resid), 1))
    send_ref[HEAD : HEAD + 8, :] = ghosts[:, 0:128] + ghosts[:, 128:256]


def return_kernel(
    live_ref, tm_ref, across_ref, own_ref, below_ref, above_ref, up_ref, down_ref, inverses_ref,
    sources_in_ref, resid_in_ref, att_ref, src_ref, cols_ref, by_source_ref, by_row_ref, pack_ref,
    index_ref, out_ref, sources_ref, *rest, second,
):
    tm, total_ref = tm_ref[0], rest[-1]
    total_ref[...] = (
        own_ref[0:HEAD, :] + across_ref[0:HEAD, :] + below_ref[0:HEAD, :] + above_ref[0:HEAD, :]
    )
    normal = jnp.concatenate([total_ref[pl.ds(j, 5, stride=8), :] for j in range(8)], 1)
    sub8 = iota((8, SRC_N), 0)
    step = jnp.zeros((8, SRC_N), F32)
    for p in range(5):
        row = jnp.sum(inverses_ref[p] * normal, axis=0, keepdims=True)
        step = jnp.where(sub8 == p, row, step)
    sources_ref[...] = step[0:5] if second else sources_in_ref[...] + step[0:5]
    ghost8 = iota((8, 128), 0)
    there = jnp.where(ghost8 < 4, jnp.where(tm > 0, 1.0, 0.0), jnp.where(tm < TM_N - 1, 1.0, 0.0))

    def item(i):
        row = HEAD + 4 * i
        return jnp.concatenate([up_ref[row : row + 4, :], down_ref[row : row + 4, :]], 0)

    facts = item(9)
    ghost_slot = facts[:, 0:1].astype(I32)
    ghost_block = facts[:, 64:65].astype(I32)
    ghost_onehot = jnp.where(iota((8, SRC_N), 1) == ghost_slot, 1.0, 0.0)
    values = gather_source(step, by_source_ref[...])
    ghost_values = gather_source(step, ghost_onehot)
    change = jnp.zeros((CROSS, ROWS), F32)
    ghost_change = jnp.zeros((8, ROWS), F32)
    for p in range(5):
        change = change + src_ref[p].astype(F32) * values[p]
        ghost_change = ghost_change + item(3 + p) * ghost_values[p]
    used = jnp.where(iota((CROSS, 1), 0) < live_ref[0], 1.0, 0.0)
    resid = resid_in_ref[...] - used * change
    if not second:
        rest[0][...] = resid
    if second:
        ghost_resid = jnp.concatenate(
            [below_ref[HEAD : HEAD + 4, :], above_ref[HEAD + 4 : HEAD + 8, :]], 0
        )
    else:
        ghost_resid = item(8)
    ghost_resid = (ghost_resid - ghost_change) * there
    rows = [att_ref[a].astype(F32) * resid for a in range(3)]
    rows += [item(a) * ghost_resid for a in range(3)]
    high, low = halves(jnp.concatenate(rows, 0))
    grads = dot(jnp.concatenate([high, low, high], 1), by_row_ref[...])
    lbc, cc = column(cols_ref, 1), column(cols_ref, 3)
    group = iota((128, 128), 1) >> 4
    edge_group = jnp.where(lbc <= 1, lbc, lbc - 24)
    own = group == cc + 2
    edge = group == edge_group
    whole = jnp.concatenate([grads[128 * a : 128 * a + 128] for a in range(3)], 1)
    high, low = halves(whole)
    own3, edge3 = jnp.concatenate([own] * 3, 1), jnp.concatenate([edge] * 3, 1)
    none = jnp.zeros_like(high)
    table = [jnp.where(mask, part, none) for part in (high, low) for mask in (own3, edge3)]
    packed = dot(pack_ref[...], jnp.concatenate(table, 0))
    peer = iota((SKY_N, 128), 0)
    ghost_group = iota((8, 128), 1) >> 4
    ghost_own = ghost_group == jnp.where(ghost8[:, 0:1] < 4, ghost_block - 24, ghost_block)
    for a in range(3):
        ghost = jnp.where(ghost_own, grads[384 + 8 * a : 392 + 8 * a], 0.0)
        from_below = jnp.sum(jnp.where(ghost8 < 4, ghost, 0.0), axis=0, keepdims=True)
        from_above = jnp.sum(jnp.where(ghost8 >= 4, ghost, 0.0), axis=0, keepdims=True)
        block = packed[:, 128 * a : 128 * a + 128]
        block = block + jnp.where(peer == 0, from_below, 0.0)
        block = block + jnp.where(peer == SKY_N - 1, from_above, 0.0)
        out_ref[:, a, :] = block
    out_ref[:, 3, :] = jnp.zeros((SKY_N, 128), F32) if second else index_ref[...]


def smooth_kernel(
    offsets_ref, chip_ref, core_ref, tm_ref, got_ref, knots_in_ref, wide_ref, one_ref, two_ref,
    three_ref, four_ref, *outs, last,
):
    knots_ref = outs[0]
    lane = iota((SKY_N, 128), 1)
    if last:
        sources_in_ref, step_ref, pick_ref, rims_ref = one_ref, two_ref, three_ref, four_ref
        pick = pick_ref[...]
        rims = [rims_ref[8 * i : 8 * i + 8, :] for i in range(4)]
    else:
        sides_ref, up_ref, down_ref = one_ref, two_ref, three_ref
        place, tm = chip_ref[0] * 2 + core_ref[0], tm_ref[0]
        below = jnp.where(tm > 0, up_ref[HEAD + 40 : HEAD + 44, :], 0.0)
        above = jnp.where(tm < TM_N - 1, down_ref[HEAD + 40 : HEAD + 44, :], 0.0)
        before = jnp.where(place == 0, below, sides_ref[0:4, :])
        after = jnp.where(place == SKY_N - 1, above, sides_ref[4:8, :])
        rims = rim_tiles(before, after)
        for i in range(4):
            outs[3][8 * i : 8 * i + 8, :] = rims[i]
        index = got_ref[:, 3, :]
        square = jnp.concatenate([index, index], 0).T
        block32 = (iota((32, 128), 0) + 1).astype(F32)
        pick = jnp.concatenate(
            [
                jnp.where(square[16 * (2 + c) : 16 * (2 + c) + 1, :] == block32, 1.0, 0.0)
                for c in range(4)
            ],
            0,
        ).astype(BF16)
        outs[2][...] = pick
    got = [got_ref[:, a, :] for a in range(3)]
    summed = split_dot(pick, jnp.concatenate(got, 1))
    row128 = iota((128, 128), 0)
    group128 = iota((128, 128), 1) >> 4
    keep = group128 == (row128 >> 5) + 2
    fold = fold_table()
    stack = []
    for a in range(3):
        one = jnp.where(keep, summed[:, 128 * a : 128 * a + 128], 0.0)
        stack.append(one[0:32] + one[32:64] + one[64:96] + one[96:128])
    high, low = halves(jnp.concatenate(stack, 0))
    spread = dot(jnp.concatenate([high, low], 1), jnp.concatenate([fold, fold], 0))
    in_row = (iota((8, 128), 1) >> 4) == iota((8, 128), 0)
    sub8, lane8 = iota((8, 128), 0), iota((8, 128), 1)
    grad = [jnp.zeros((8, 128), F32)] * 5
    for a in range(3):
        for r in range(5):
            if r < 4:
                piece = jnp.where(in_row, spread[32 * a + 8 * r : 32 * a + 8 * r + 8], 0.0)
            else:
                piece = jnp.where((lane < 32) | (lane >= 96), got[a], 0.0)
            grad[r] = jnp.where(sub8 == a, jnp.sum(piece, axis=0, keepdims=True), grad[r])
    bands, scale = [], None
    for i in range(4):
        tiles = [wide_ref[8 * i : 8 * i + 8, 128 * r : 128 * r + 128] for r in range(4)]
        if i < 3:
            bands.append([*tiles, rims[i]])
        else:
            scale = [*tiles, rims[i]]
    offsets = [offsets_ref[b] for b in range(3)]
    wraps = [(lane8 < offset, lane8 >= 128 - offset) for offset in offsets]
    delta = [g * f for g, f in zip(grad, scale, strict=True)]
    for _ in range(2):
        total = grad
        for b in range(3):
            low = [pltpu.roll(d, offsets[b], 1) for d in delta]
            high = [pltpu.roll(d, 128 - offsets[b], 1) for d in delta]
            first, final = wraps[b]
            total = [
                total[r]
                + bands[b][r]
                * (
                    jnp.where(first, low[(r + 4) % 5], low[r])
                    + jnp.where(final, high[(r + 1) % 5], high[r])
                )
                for r in range(5)
            ]
        delta = [t * f for t, f in zip(total, scale, strict=True)]
    for a in range(3):
        for r in range(4):
            tile = delta[r][a : a + 1]
            knots_ref[a, r : r + 1, :] = knots_in_ref[a, r : r + 1, :] + tile
    if last:
        outs[1][...] = sources_in_ref[...] + step_ref[...]
        return
    send_ref = outs[1]
    spreads = []
    for a in range(3):
        for r in range(4):
            tile = delta[r][a : a + 1]
            spreads.append(jnp.where(in_row, tile, 0.0))
    high, low = halves(jnp.concatenate(spreads, 0))
    blocks = dot(jnp.concatenate([high, low], 1), jnp.concatenate([fold, fold], 0))
    table = jnp.concatenate([blocks[32 * a : 32 * a + 32] for a in range(3)], 1)
    slots = [index[:, 16 * (2 + c) : 16 * (2 + c) + 1].astype(I32) - 1 for c in range(4)]
    slot = jnp.concatenate(slots, 0)
    by_block = jnp.where((iota((4 * SKY_N, 64), 1) & 31) == slot, 1.0, 0.0)
    found = split_dot(by_block, table)
    group = lane >> 4
    front = jnp.zeros((SKY_N, 128), F32)
    back = jnp.zeros((SKY_N, 128), F32)
    for c in range(4):
        rows = found[SKY_N * c : SKY_N * (c + 1)]
        part = [rows[:, 128 * a : 128 * a + 128] for a in range(3)]
        front = jnp.where(group == c, part[0], jnp.where(group == c + 4, part[1], front))
        back = jnp.where(group == c, part[2], back)
    send_ref[:, 0, :] = front
    send_ref[:, 1, :] = back


def run_kernel(body, scalars, outs, *args, scratch=(), flops=10_000_000, **static):
    specs = [
        pl.BlockSpec(memory_space=pltpu.SMEM if i < scalars else pltpu.VMEM)
        for i in range(len(args))
    ]
    shapes = [o if isinstance(o, jax.ShapeDtypeStruct) else jax.ShapeDtypeStruct(o, F32) for o in outs]

    def kernel(*refs):
        body(*refs, **static)

    return pl.pallas_call(
        kernel,
        out_shape=shapes,
        in_specs=specs,
        out_specs=[
            pl.BlockSpec(memory_space=pltpu.SMEM if s.dtype == I32 else pltpu.VMEM) for s in shapes
        ],
        scratch_shapes=[pltpu.VMEM(shape, F32) for shape in scratch],
        cost_estimate=pl.CostEstimate(flops=flops, bytes_accessed=2_000_000, transcendentals=0),
        compiler_params=pltpu.CompilerParams(vmem_limit_bytes=32 * 1024 * 1024),
    )(*args)


def half(*shape):
    return jax.ShapeDtypeStruct(shape, BF16)


def shifts(k):
    return [(i, (i + k) % TM_N) for i in range(TM_N)]


def per_device(
    observed,
    att_partials,
    src_partials,
    src_slot,
    knot_block,
    live_count,
    sources,
    inverses,
    attitude,
    band_coef,
    extra_diag,
    band_offsets,
):
    core = lax.axis_index("c").astype(I32).reshape(1)
    tm = lax.axis_index("tm").astype(I32).reshape(1)
    slot = src_slot.reshape(1, CROSS)
    kb = knot_block.reshape(1, CROSS)
    chip = lax.axis_index(("x", "z")).astype(I32).reshape(1)
    knots = attitude.reshape(3, 4, 128)
    bands = band_coef.reshape(3, 3, 4, 128)
    extra = extra_diag.reshape(3, 4, 128)

    dense = pl.pallas_call(
        payload_kernel,
        out_shape=jax.ShapeDtypeStruct((CHIPS, 4, 4, 128), F32),
        in_specs=[pl.BlockSpec(memory_space=pl.ANY)] * 3,
        out_specs=pl.BlockSpec(memory_space=pltpu.VMEM),
        scratch_shapes=[
            pltpu.VMEM((3, 4, 128), F32),
            pltpu.VMEM((3, 3, 4, 128), F32),
            pltpu.VMEM((3, 4, 128), F32),
            pltpu.SemaphoreType.DMA((3,)),
        ],
        compiler_params=pltpu.CompilerParams(vmem_limit_bytes=56 * 1024 * 1024),
    )(knots, bands, extra)
    near = lax.all_to_all(dense, ("x", "z"), 0, 0, tiled=True)
    (
        cols, places, by_source, base, by_lane, by_row, pack, index, peers, choose, up, down, wide,
        offsets,
    ) = run_kernel(
        prepare_kernel, 3,
        [
            (128, 128), half(128, 256), half(128, SRC_N), (CROSS, ROWS), half(384, 128),
            half(384, 128), half(SKY_N, 512), (SKY_N, 128), half(128, 128), (8, 128), (40, 128),
            (40, 128), (32, RUN), jax.ShapeDtypeStruct((3,), I32),
        ],
        live_count, core, band_offsets, observed, att_partials, src_partials, slot, kb, sources, bands, extra,
    )
    near, cols = lax.optimization_barrier((near, cols))
    far = lax.ppermute(near, "c", [(0, 1), (1, 0)])
    resid, plain, up, down, sides = run_kernel(
        first_kernel, 3,
        [(CROSS, ROWS), (HEAD, 128), (HEAD + 48, 128), (HEAD + 48, 128), (8, 128)],
        live_count, core, chip, near, far, att_partials, src_partials, cols, places, by_source,
        base, by_lane, choose, up, down,
    )
    across = lax.ppermute(plain, "tm", shifts(2))
    up = lax.ppermute(up, "tm", shifts(1))
    down = lax.ppermute(down, "tm", shifts(-1))
    back_shapes = [(SKY_N, 4, 128), (5, SRC_N)]
    outgoing, sources, resid = run_kernel(
        return_kernel, 2, [*back_shapes, (CROSS, ROWS)],
        live_count, tm, across, plain, up, down, up, down, inverses, sources, resid,
        att_partials, src_partials, cols, by_source, by_row, pack, index,
        scratch=[(HEAD, 128)], second=False,
    )
    got = lax.all_to_all(outgoing, SKY, 0, 0, tiled=True)
    knots, served, pick, rims = run_kernel(
        smooth_kernel, 4, [(3, 4, 128), (SKY_N, 2, 128), half(128, 128), (32, 128)],
        offsets, chip, core, tm, got, knots, wide, sides, up, down, choose, last=False,
    )
    arrived = lax.all_to_all(served, SKY, 0, 0, tiled=True)
    resid, mine = run_kernel(
        middle_kernel, 1, [(CROSS, ROWS), (HEAD + 8, 128)],
        live_count, arrived, resid, att_partials, src_partials, cols, peers, by_source, by_lane,
        choose,
    )
    across = lax.ppermute(mine, "tm", shifts(2))
    below = lax.ppermute(mine, "tm", shifts(1))
    above = lax.ppermute(mine, "tm", shifts(-1))
    outgoing, step = run_kernel(
        return_kernel, 2, back_shapes,
        live_count, tm, across, mine, below, above, up, down, inverses, sources, resid,
        att_partials, src_partials, cols, by_source, by_row, pack, index,
        scratch=[(HEAD, 128)], second=True,
    )
    got = lax.all_to_all(outgoing, SKY, 0, 0, tiled=True)
    knots, sources = run_kernel(
        smooth_kernel, 4, [(3, 4, 128), (5, SRC_N)],
        offsets, chip, core, tm, got, knots, wide, sources, step, pick, rims, last=True,
    )
    return (sources, knots.reshape(3, 1, RUN))


def solution(mesh):
    torus = Mesh(mesh.devices.reshape(4, 8, 2, mesh.shape["tm"]), SKY_TM)
    return jax.shard_map(
        per_device,
        mesh=torus,
        in_specs=(
            P(SKY_TM, None),
            P(None, SKY_TM, None),
            P(None, SKY_TM, None),
            P(SKY_TM),
            P(SKY_TM),
            P(SKY_TM),
            P(None, SKY),
            P(None, None, SKY),
            P(None, "tm", SKY),
            P(None, None, "tm", SKY),
            P(None, "tm", SKY),
            P(),
        ),
        out_specs=(P(None, SKY), P(None, "tm", SKY)),
        check_vma=False,
    )
```

```python
import jax
import jax.numpy as jnp
from jax import lax
from jax.experimental import pallas as pl
from jax.experimental.pallas import tpu as pltpu
from jax.sharding import Mesh
from jax.sharding import PartitionSpec as P

F32 = jnp.float32
BF16 = jnp.bfloat16
I32 = jnp.int32
ROWS = 128
KNOTS = 16
CROSS = 128
SKY_N = 64
CHIPS = 32
TM_N = 4
SRC_N = 1024
RUN = 512
HEAD = 40
SKY = ("x", "z", "c")
SKY_TM = ("x", "z", "c", "tm")


def iota(shape, dim):
    return lax.broadcasted_iota(I32, shape, dim)


def dot(a, b):
    return jnp.dot(a.astype(BF16), b.astype(BF16), preferred_element_type=F32)


def dot_nt(a, b):
    return lax.dot_general(
        a.astype(BF16), b.astype(BF16), (((1,), (1,)), ((), ())), preferred_element_type=F32
    )


def halves(x):
    high = x.astype(BF16)
    return high, (x - high.astype(F32)).astype(BF16)


def split_dot(twice, values):
    return dot(twice, jnp.concatenate(halves(values), 0))


def thirds(x):
    high = x.astype(BF16).astype(F32)
    rest = x - high
    middle = rest.astype(BF16).astype(F32)
    return high, middle, rest - middle


def b_spline(moment_row, knot):
    tau = 1.5 + (KNOTS - 3) * (moment_row.astype(F32) + 0.5) / ROWS
    dist = jnp.abs(tau - knot.astype(F32))
    inner = 2.0 / 3.0 - dist * dist + 0.5 * dist * dist * dist
    rest = 2.0 - dist
    outer = rest * rest * rest / 6.0
    return jnp.where(dist < 1.0, inner, jnp.where(dist < 2.0, outer, 0.0))


def spline_by_lane():
    return b_spline(iota((128, 128), 1), iota((128, 128), 0) & 15)


def spline_by_row():
    return b_spline(iota((128, 128), 0), iota((128, 128), 1) & 15)


def fold_table():
    return jnp.where((iota((128, 128), 0) & 15) == (iota((128, 128), 1) & 15), 1.0, 0.0)


def table_of(table):
    return table if isinstance(table, jax.Array) else table[...]


def attitude_term(att, masked, table_ref):
    count = masked[0].shape[0]
    high, low = halves(jnp.concatenate(masked, 0))
    spread = dot(jnp.concatenate([high, low, high], 1), table_of(table_ref))
    return sum(att[a].astype(F32) * spread[a * count : (a + 1) * count] for a in range(3))


def products_sum(products_ref, masked):
    lane = iota((128, 128), 1)
    square = jnp.zeros((128, 128), F32)
    for p in range(5):
        terms = [
            products_ref[128 * (3 * p + a) : 128 * (3 * p + a) + 128, :] * masked[a]
            for a in range(3)
        ]
        row = jnp.sum(terms[0] + terms[1] + terms[2], axis=1, keepdims=True)
        square = jnp.where(lane == p, row, square)
    return square


def send_normal(rhs, onehot, refs):
    rows = rhs.T[0:8]
    parts = dot(jnp.concatenate(thirds(rows), 0), onehot)
    normal = parts[0:8] + parts[8:16] + parts[16:24]
    for ref in refs:
        for j in range(8):
            ref[pl.ds(j, 5, stride=8), :] = normal[0:5, 128 * j : 128 * j + 128]


def gradients(att, resid, table_ref):
    high, low = halves(jnp.concatenate([att[a].astype(F32) * resid for a in range(3)], 0))
    return dot(jnp.concatenate([high, low, high], 1), table_of(table_ref))


def gather_source(values8, onehot):
    parts = dot_nt(onehot, jnp.concatenate(thirds(values8), 0))
    return [
        parts[:, p : p + 1] + parts[:, 8 + p : 9 + p] + parts[:, 16 + p : 17 + p] for p in range(5)
    ]


def padded_rows(x):
    return jnp.concatenate([x, jnp.zeros((8 - x.shape[0], x.shape[1]), F32)], 0)


def column(cols_ref, i):
    return cols_ref[:, i : i + 1].astype(I32)


def stacked_spline(table):
    high, low = halves(table)
    return jnp.concatenate([high, high, low], 0)


def prepare_kernel(
    live_ref, core_ref, offsets_in_ref, obs_ref, att_ref, src_ref, slot_ref, kb_ref, sources_ref,
    bands_ref, extra_ref, knots_in_ref,
    cols_ref, places_ref, by_source_ref, base_ref, by_lane_ref, by_row_ref, pack_ref, index_ref,
    peers_ref, choose_ref, up_ref, down_ref, wide_ref, ghost_ref, products_ref, normals_ref, rhs_ref,
    knots_ref, offsets_ref,
):
    live, core = live_ref[0], core_ref[0]
    knots_ref[...] = knots_in_ref[...]
    for b in range(3):
        offsets_ref[b] = offsets_in_ref[b]
    kb, slot = kb_ref[...], slot_ref[...]
    h, lb = kb >> 5, kb & 31
    sub, lane = iota((128, 128), 0), iota((128, 128), 1)
    square = jnp.zeros((128, 128), F32)
    for i, row in enumerate((h, lb, slot)):
        square = jnp.where(sub == i, row.astype(F32), square)
    turned = square.T
    hc, lbc, slotc = (turned[:, i : i + 1].astype(I32) for i in range(3))
    same = hc == h
    c = jnp.sum(jnp.where(same & (sub < lane), 1.0, 0.0), axis=0, keepdims=True).astype(I32)
    cc = jnp.sum(jnp.where(same & (lane < sub), 1.0, 0.0), axis=1, keepdims=True)
    cols_ref[...] = jnp.where(lane == 3, cc, turned)
    cc = cc.astype(I32)
    group = lane >> 4

    place = (lbc >> 3) * CHIPS + (hc >> 1) + jnp.where((hc & 1) == core, 0, 128)
    places = jnp.where(iota((128, 256), 1) == place, 1.0, 0.0)
    by_source = jnp.where(iota((128, SRC_N), 1) == slotc, 1.0, 0.0).astype(BF16)
    by_source_ref[...] = by_source
    values = gather_source(padded_rows(sources_ref[...]), by_source)
    src_term = jnp.zeros((CROSS, ROWS), F32)
    for p in range(5):
        src_term = src_term + src_ref[p].astype(F32) * values[p]
    used = jnp.where(iota((CROSS, 1), 0) < live, 1.0, 0.0)
    base = (obs_ref[...] - src_term) * used
    base_ref[...] = base
    by_row = stacked_spline(spline_by_row())
    rhs = jnp.zeros((128, 128), F32)
    normals = [jnp.zeros((128, 128), F32)] * 5
    for p in range(5):
        one = src_ref[p].astype(F32) * used
        rhs = jnp.where(lane == p, jnp.sum(one * base, axis=1, keepdims=True), rhs)
        products_ref[384 * p : 384 * p + 384, :] = gradients(att_ref, one, by_row)
        for q in range(p + 1):
            both = jnp.sum(one * src_ref[q].astype(F32), axis=1, keepdims=True)
            normals[q] = jnp.where(lane == p, both, normals[q])
            normals[p] = jnp.where(lane == q, both, normals[p])
    rhs_ref[...] = rhs
    for q in range(5):
        normals_ref[128 * q : 128 * q + 128, :] = normals[q]
    by_lane_ref[...] = stacked_spline(spline_by_lane())
    by_row_ref[...] = by_row

    peer = iota((SKY_N, 128), 0)
    to_row = jnp.where(lb <= 1, h - 1, jnp.where(lb >= 30, h + 1, jnp.full_like(h, -1)))
    own = jnp.where(peer == h, 1.0, 0.0)
    edge = jnp.where(peer == to_row, 1.0, 0.0)
    pack_ref[...] = jnp.concatenate([own, edge, own, edge], 1).astype(BF16)
    index_ref[...] = dot(own, jnp.where(group == cc + 2, (lbc + 1).astype(F32), 0.0))
    peers = jnp.where((iota((128, 128), 1) & 63) == hc, 1.0, 0.0)

    sub8 = iota((8, 128), 0)
    after = (h == SKY_N - 1) & (lb >= 30) & (sub8 < 4)
    before = (h == 0) & (lb <= 1) & (sub8 >= 4)
    chosen = (c == (sub8 & 3)) & (after | before) & (iota((8, 128), 1) < live)
    choose = jnp.where(chosen, 1.0, 0.0)
    choose_ref[...] = choose
    pieces = [att_ref[a] for a in range(3)] + [src_ref[p] for p in range(5)]
    pieces += [*halves(base), places.astype(BF16), peers.astype(BF16)]
    ghosts = dot(choose, jnp.concatenate(pieces, 1))
    items = [ghosts[:, 128 * i : 128 * i + 128] for i in range(8)]
    empty = jnp.zeros((8, 256), F32)
    places_ref[...] = jnp.concatenate([places, ghosts[:, 1280:1536], empty], 0).astype(BF16)
    peers_ref[...] = jnp.concatenate([peers, ghosts[:, 1536:1664], empty[:, 0:128]], 0).astype(BF16)
    ghost_slot = jnp.sum(choose * slot.astype(F32), axis=1, keepdims=True)
    ghost_block = jnp.sum(choose * lb.astype(F32), axis=1, keepdims=True)
    items.append(jnp.zeros((8, 128), F32))
    items.append(jnp.where(iota((8, 128), 1) < 64, ghost_slot, ghost_block))
    for a in range(3):
        ghost_ref[8 * a : 8 * a + 8, :] = items[a]
    ghost_ref[24:32, :] = ghosts[:, 1024:1152] + ghosts[:, 1152:1280]
    ghost_ref[32:40, :] = items[9]
    for q in range(5):
        even, odd = items[2 * q], items[2 * q + 1]
        up_ref[8 * q : 8 * q + 8, :] = jnp.concatenate([even[0:4], odd[0:4]], 0)
        down_ref[8 * q : 8 * q + 8, :] = jnp.concatenate([even[4:8], odd[4:8]], 0)

    bands = [axis_rows(bands_ref[b]) for b in range(3)]
    diag = axis_rows(extra_ref) + 2.0 * (bands[0] + bands[1] + bands[2])
    for b in range(3):
        wide_ref[8 * b : 8 * b + 8, :] = bands[b]
    wide_ref[24:32, :] = 1.0 / jnp.where(diag > 0.0, diag, 1.0)


def axis_rows(tiles):
    sub = iota((8, RUN), 0)
    out = jnp.zeros((8, RUN), F32)
    for a in range(3):
        out = jnp.where(sub == a, jnp.concatenate([tiles[a][r : r + 1] for r in range(4)], 1), out)
    return out


def payload_kernel(knots_hbm, bands_hbm, extra_hbm, out_ref, knots_ref, bands_ref, extra_ref, sems):
    copies = [
        pltpu.make_async_copy(source, target, sems.at[i])
        for i, (source, target) in enumerate(
            ((bands_hbm, bands_ref), (extra_hbm, extra_ref), (knots_hbm, knots_ref))
        )
    ]
    for copy in copies:
        copy.start()
    for copy in copies:
        copy.wait()
    lane = iota((1, 128), 1)

    def ends(tiles, width):
        low, high = tiles[0:1], tiles[3:4]
        return jnp.where(lane < width, low, jnp.where(lane >= 128 - width, high, 0.0))

    rows = []
    for a in range(3):
        bands = [bands_ref[b, a] for b in range(3)]
        diag = extra_ref[a] + 2.0 * (bands[0] + bands[1] + bands[2])
        row = ends(diag, 32) + pltpu.roll(ends(bands[0], 16), 48, 1)
        rows.append(row + pltpu.roll(ends(bands[1], 16), 80, 1))
    third = [ends(bands_ref[2, a], 16) for a in range(3)]
    rows.append(third[0] + pltpu.roll(third[1], 48, 1) + pltpu.roll(third[2], 80, 1))
    sub = iota((4, 128), 0)
    edge = jnp.zeros((4, 128), F32)
    for i, row in enumerate(rows):
        edge = jnp.where(sub == i, row, edge)
    for chip in range(CHIPS):
        out_ref[chip, 0:3] = knots_ref[...]
        out_ref[chip, 3] = edge


def rim_tiles(before, after):
    sub, lane = iota((8, 128), 0), iota((8, 128), 1)

    def tile(sources, width):
        out = jnp.zeros((8, 128), F32)
        for a, (row, turn) in enumerate(sources):
            both = [e[row : row + 1] for e in (after, before)]
            if turn:
                both = [pltpu.roll(e, 128 - turn, 1) for e in both]
            one = jnp.where(lane < width, both[0], jnp.where(lane >= 128 - width, both[1], 0.0))
            out = jnp.where(sub == a, one, out)
        return out

    bands = [
        tile([(a, 48) for a in range(3)], 16),
        tile([(a, 80) for a in range(3)], 16),
        tile([(3, 0), (3, 48), (3, 80)], 16),
    ]
    diag = tile([(a, 0) for a in range(3)], 32)
    return bands + [1.0 / jnp.where(diag > 0.0, diag, 1.0)]


def first_kernel(
    core_ref, chip_ref, near_ref, far_ref, cols_ref, places_ref, by_source_ref, by_lane_ref,
    up_in_ref, down_in_ref, ghost_ref, products_ref, rhs_in_ref,
    masked_ref, rhs_ref, plain_ref, up_ref, down_ref, sides_ref,
):
    tables = []
    for a in range(3):
        rows = [ref[:, a, r, :] for ref in (near_ref, far_ref) for r in range(4)]
        tables += halves(jnp.concatenate(rows, 0))
    found = dot(places_ref[...], jnp.concatenate(tables, 1))
    mine = (iota((128, 128), 1) >> 4) == (column(cols_ref, 1) & 7)
    facts = ghost_ref[32:40, :]
    ghost_mine = (iota((8, 128), 1) >> 4) == (facts[:, 64:65].astype(I32) & 7)
    masked, ghost_masked = [], []
    for a in range(3):
        whole = found[:, 256 * a : 256 * a + 128] + found[:, 256 * a + 128 : 256 * a + 256]
        masked.append(jnp.where(mine, whole[0:128], 0.0))
        ghost_masked.append(jnp.where(ghost_mine, whole[128:136], 0.0))
        masked_ref[128 * a : 128 * a + 128, :] = masked[a]
    rhs = rhs_in_ref[...] - products_sum(products_ref, masked)
    rhs_ref[...] = rhs
    send_normal(rhs, by_source_ref[...], (plain_ref, up_ref, down_ref))
    ghost_att = [ghost_ref[8 * a : 8 * a + 8, :] for a in range(3)]
    ghosts = ghost_ref[24:32, :] - attitude_term(ghost_att, ghost_masked, by_lane_ref)
    up_ref[HEAD : HEAD + 40, :] = up_in_ref[...]
    down_ref[HEAD : HEAD + 40, :] = down_in_ref[...]
    up_ref[HEAD + 32 : HEAD + 36, :] = ghosts[0:4]
    down_ref[HEAD + 32 : HEAD + 36, :] = ghosts[4:8]
    core, chip = core_ref[0], chip_ref[0]
    before = jnp.where(core == 0, jnp.maximum(chip - 1, 0), chip)
    after = jnp.where(core == 0, chip, jnp.minimum(chip + 1, CHIPS - 1))
    sides_ref[0:4, :] = far_ref[before, 3]
    sides_ref[4:8, :] = far_ref[after, 3]
    empty = jnp.zeros((4, 128), F32)
    final = jnp.where(core == 1, near_ref[CHIPS - 1, 3], far_ref[CHIPS - 1, 3])
    initial = jnp.where(core == 0, near_ref[0, 3], far_ref[0, 3])
    up_ref[HEAD + 40 : HEAD + 48, :] = jnp.concatenate([final, empty], 0)
    down_ref[HEAD + 40 : HEAD + 48, :] = jnp.concatenate([initial, empty], 0)


def beside_kernel(
    live_ref, masked_ref, resid_in_ref, att_ref, by_lane_ref, by_row_ref, grads_ref, *rest
):
    masked = [masked_ref[128 * a : 128 * a + 128, :] for a in range(3)]
    used = jnp.where(iota((CROSS, 1), 0) < live_ref[0], 1.0, 0.0)
    resid = resid_in_ref[...] - attitude_term(att_ref, masked, by_lane_ref) * used
    grads_ref[...] = gradients(att_ref, resid, by_row_ref)
    for ref in rest:
        ref[...] = resid


def middle_kernel(
    got_ref, resid_ref, rhs_in_ref, cols_ref, peers_ref, by_source_ref, by_lane_ref, choose_ref,
    ghost_ref, products_ref, masked_ref, send_ref,
):
    found = split_dot(peers_ref[...], jnp.concatenate([got_ref[:, 0, :], got_ref[:, 1, :]], 1))
    group = iota((136, 128), 1) >> 4
    cc = jnp.concatenate([column(cols_ref, 3), iota((8, 1), 0) & 3], 0)
    front, back = found[0:136, 0:128], found[0:136, 128:256]
    masked = [
        jnp.where(group == cc, front, 0.0),
        jnp.where(group == cc + 4, front, 0.0),
        jnp.where(group == cc, back, 0.0),
    ]
    for a in range(3):
        masked_ref[128 * a : 128 * a + 128, :] = masked[a][0:128]
    rhs = rhs_in_ref[...] - products_sum(products_ref, [m[0:128] for m in masked])
    send_normal(rhs, by_source_ref[...], (send_ref,))
    ghost_att = [ghost_ref[8 * a : 8 * a + 8, :] for a in range(3)]
    term = attitude_term(ghost_att, [m[128:136] for m in masked], by_lane_ref)
    ghosts = dot(choose_ref[...], jnp.concatenate(halves(resid_ref[...]), 1))
    send_ref[HEAD : HEAD + 8, :] = ghosts[:, 0:128] + ghosts[:, 128:256] - term


def return_kernel(
    live_ref, tm_ref, across_ref, own_ref, below_ref, above_ref, up_ref, down_ref, inverses_ref,
    sources_in_ref, grads_ref, products_ref, cols_ref, by_source_ref, by_row_ref, pack_ref,
    *rest, second,
):
    if second:
        out_ref, sources_ref = rest[:2]
    else:
        index_ref, resid_in_ref, src_ref, normals_ref, rhs_in_ref = rest[:5]
        out_ref, sources_ref, resid_ref, rhs_ref = rest[5:9]
    tm, total_ref = tm_ref[0], rest[-1]
    total_ref[...] = (
        own_ref[0:HEAD, :] + across_ref[0:HEAD, :] + below_ref[0:HEAD, :] + above_ref[0:HEAD, :]
    )
    normal = jnp.concatenate([total_ref[pl.ds(j, 5, stride=8), :] for j in range(8)], 1)
    sub8 = iota((8, SRC_N), 0)
    step = jnp.zeros((8, SRC_N), F32)
    for p in range(5):
        row = jnp.sum(inverses_ref[p] * normal, axis=0, keepdims=True)
        step = jnp.where(sub8 == p, row, step)
    sources_ref[...] = step[0:5] if second else sources_in_ref[...] + step[0:5]
    ghost8 = iota((8, 128), 0)
    there = jnp.where(ghost8 < 4, jnp.where(tm > 0, 1.0, 0.0), jnp.where(tm < TM_N - 1, 1.0, 0.0))

    def item(i):
        row = HEAD + 4 * i
        return jnp.concatenate([up_ref[row : row + 4, :], down_ref[row : row + 4, :]], 0)

    facts = item(9)
    ghost_slot = facts[:, 0:1].astype(I32)
    ghost_block = facts[:, 64:65].astype(I32)
    ghost_onehot = jnp.where(iota((8, SRC_N), 1) == ghost_slot, 1.0, 0.0)
    values = gather_source(step, by_source_ref[...])
    ghost_values = gather_source(step, ghost_onehot)
    ghost_change = jnp.zeros((8, ROWS), F32)
    for p in range(5):
        ghost_change = ghost_change + item(3 + p) * ghost_values[p]
    if second:
        ghost_resid = jnp.concatenate(
            [below_ref[HEAD : HEAD + 4, :], above_ref[HEAD + 4 : HEAD + 8, :]], 0
        )
    else:
        ghost_resid = item(8)
        used = jnp.where(iota((CROSS, 1), 0) < live_ref[0], 1.0, 0.0)
        change = jnp.zeros((CROSS, ROWS), F32)
        rhs = rhs_in_ref[...]
        for p in range(5):
            change = change + src_ref[p].astype(F32) * values[p]
            rhs = rhs - normals_ref[128 * p : 128 * p + 128, :] * values[p]
        resid_ref[...] = resid_in_ref[...] - used * change
        rhs_ref[...] = rhs
    ghost_resid = (ghost_resid - ghost_change) * there
    ghost_grads = gradients([item(a) for a in range(3)], ghost_resid, by_row_ref)
    parts = []
    for a in range(3):
        part = grads_ref[128 * a : 128 * a + 128, :]
        for p in range(5):
            low_row = 128 * (3 * p + a)
            part = part - products_ref[low_row : low_row + 128, :] * values[p]
        parts.append(part)
    lbc, cc = column(cols_ref, 1), column(cols_ref, 3)
    group = iota((128, 128), 1) >> 4
    edge_group = jnp.where(lbc <= 1, lbc, lbc - 24)
    own = group == cc + 2
    edge = group == edge_group
    high, low = halves(jnp.concatenate(parts, 1))
    own3, edge3 = jnp.concatenate([own] * 3, 1), jnp.concatenate([edge] * 3, 1)
    none = jnp.zeros_like(high)
    table = [jnp.where(mask, part, none) for part in (high, low) for mask in (own3, edge3)]
    packed = dot(pack_ref[...], jnp.concatenate(table, 0))
    peer = iota((SKY_N, 128), 0)
    ghost_group = iota((8, 128), 1) >> 4
    ghost_own = ghost_group == jnp.where(ghost8[:, 0:1] < 4, ghost_block - 24, ghost_block)
    for a in range(3):
        ghost = jnp.where(ghost_own, ghost_grads[8 * a : 8 * a + 8], 0.0)
        from_below = jnp.sum(jnp.where(ghost8 < 4, ghost, 0.0), axis=0, keepdims=True)
        from_above = jnp.sum(jnp.where(ghost8 >= 4, ghost, 0.0), axis=0, keepdims=True)
        block = packed[:, 128 * a : 128 * a + 128]
        block = block + jnp.where(peer == 0, from_below, 0.0)
        block = block + jnp.where(peer == SKY_N - 1, from_above, 0.0)
        out_ref[:, a, :] = block
    out_ref[:, 3, :] = jnp.zeros((SKY_N, 128), F32) if second else index_ref[...]


def smooth_kernel(
    offsets_ref, chip_ref, core_ref, tm_ref, got_ref, knots_in_ref, wide_ref, one_ref, two_ref,
    three_ref, four_ref, *outs, last,
):
    knots_ref = outs[0]
    lane = iota((SKY_N, 128), 1)
    if last:
        sources_in_ref, step_ref, pick_ref, rims_ref = one_ref, two_ref, three_ref, four_ref
        pick = pick_ref[...]
        rims = [rims_ref[8 * i : 8 * i + 8, :] for i in range(4)]
    else:
        sides_ref, up_ref, down_ref = one_ref, two_ref, three_ref
        place, tm = chip_ref[0] * 2 + core_ref[0], tm_ref[0]
        below = jnp.where(tm > 0, up_ref[HEAD + 40 : HEAD + 44, :], 0.0)
        above = jnp.where(tm < TM_N - 1, down_ref[HEAD + 40 : HEAD + 44, :], 0.0)
        before = jnp.where(place == 0, below, sides_ref[0:4, :])
        after = jnp.where(place == SKY_N - 1, above, sides_ref[4:8, :])
        rims = rim_tiles(before, after)
        for i in range(4):
            outs[3][8 * i : 8 * i + 8, :] = rims[i]
        index = got_ref[:, 3, :]
        square = jnp.concatenate([index, index], 0).T
        block32 = (iota((32, 128), 0) + 1).astype(F32)
        pick = jnp.concatenate(
            [
                jnp.where(square[16 * (2 + c) : 16 * (2 + c) + 1, :] == block32, 1.0, 0.0)
                for c in range(4)
            ],
            0,
        ).astype(BF16)
        outs[2][...] = pick
    got = [got_ref[:, a, :] for a in range(3)]
    summed = split_dot(pick, jnp.concatenate(got, 1))
    row128 = iota((128, 128), 0)
    group128 = iota((128, 128), 1) >> 4
    keep = group128 == (row128 >> 5) + 2
    fold = fold_table()
    stack = []
    for a in range(3):
        one = jnp.where(keep, summed[:, 128 * a : 128 * a + 128], 0.0)
        stack.append(one[0:32] + one[32:64] + one[64:96] + one[96:128])
    high, low = halves(jnp.concatenate(stack, 0))
    spread = dot(jnp.concatenate([high, low], 1), jnp.concatenate([fold, fold], 0))
    in_row = (iota((8, 128), 1) >> 4) == iota((8, 128), 0)
    sub8, lane8 = iota((8, 128), 0), iota((8, 128), 1)
    grad = [jnp.zeros((8, 128), F32)] * 5
    for a in range(3):
        for r in range(5):
            if r < 4:
                piece = jnp.where(in_row, spread[32 * a + 8 * r : 32 * a + 8 * r + 8], 0.0)
            else:
                piece = jnp.where((lane < 32) | (lane >= 96), got[a], 0.0)
            grad[r] = jnp.where(sub8 == a, jnp.sum(piece, axis=0, keepdims=True), grad[r])
    bands, scale = [], None
    for i in range(4):
        tiles = [wide_ref[8 * i : 8 * i + 8, 128 * r : 128 * r + 128] for r in range(4)]
        if i < 3:
            bands.append([*tiles, rims[i]])
        else:
            scale = [*tiles, rims[i]]
    offsets = [offsets_ref[b] for b in range(3)]
    wraps = [(lane8 < offset, lane8 >= 128 - offset) for offset in offsets]
    delta = [g * f for g, f in zip(grad, scale, strict=True)]
    for _ in range(2):
        total = grad
        for b in range(3):
            low = [pltpu.roll(d, offsets[b], 1) for d in delta]
            high = [pltpu.roll(d, 128 - offsets[b], 1) for d in delta]
            first, final = wraps[b]
            total = [
                total[r]
                + bands[b][r]
                * (
                    jnp.where(first, low[(r + 4) % 5], low[r])
                    + jnp.where(final, high[(r + 1) % 5], high[r])
                )
                for r in range(5)
            ]
        delta = [t * f for t, f in zip(total, scale, strict=True)]
    for a in range(3):
        for r in range(4):
            tile = delta[r][a : a + 1]
            knots_ref[a, r : r + 1, :] = knots_in_ref[a, r : r + 1, :] + tile
    if last:
        outs[1][...] = sources_in_ref[...] + step_ref[...]
        return
    send_ref = outs[1]
    spreads = []
    for a in range(3):
        for r in range(4):
            tile = delta[r][a : a + 1]
            spreads.append(jnp.where(in_row, tile, 0.0))
    high, low = halves(jnp.concatenate(spreads, 0))
    blocks = dot(jnp.concatenate([high, low], 1), jnp.concatenate([fold, fold], 0))
    table = jnp.concatenate([blocks[32 * a : 32 * a + 32] for a in range(3)], 1)
    slots = [index[:, 16 * (2 + c) : 16 * (2 + c) + 1].astype(I32) - 1 for c in range(4)]
    slot = jnp.concatenate(slots, 0)
    by_block = jnp.where((iota((4 * SKY_N, 64), 1) & 31) == slot, 1.0, 0.0)
    found = split_dot(by_block, table)
    group = lane >> 4
    front = jnp.zeros((SKY_N, 128), F32)
    back = jnp.zeros((SKY_N, 128), F32)
    for c in range(4):
        rows = found[SKY_N * c : SKY_N * (c + 1)]
        part = [rows[:, 128 * a : 128 * a + 128] for a in range(3)]
        front = jnp.where(group == c, part[0], jnp.where(group == c + 4, part[1], front))
        back = jnp.where(group == c, part[2], back)
    send_ref[:, 0, :] = front
    send_ref[:, 1, :] = back


def run_kernel(body, scalars, outs, *args, scratch=(), flops=10_000_000, **static):
    specs = [
        pl.BlockSpec(memory_space=pltpu.SMEM if i < scalars else pltpu.VMEM)
        for i in range(len(args))
    ]
    shapes = [o if isinstance(o, jax.ShapeDtypeStruct) else jax.ShapeDtypeStruct(o, F32) for o in outs]

    def kernel(*refs):
        body(*refs, **static)

    return pl.pallas_call(
        kernel,
        out_shape=shapes,
        in_specs=specs,
        out_specs=[
            pl.BlockSpec(memory_space=pltpu.SMEM if s.dtype == I32 else pltpu.VMEM) for s in shapes
        ],
        scratch_shapes=[pltpu.VMEM(shape, F32) for shape in scratch],
        cost_estimate=pl.CostEstimate(flops=flops, bytes_accessed=2_000_000, transcendentals=0),
        compiler_params=pltpu.CompilerParams(vmem_limit_bytes=32 * 1024 * 1024),
    )(*args)


def half(*shape):
    return jax.ShapeDtypeStruct(shape, BF16)


def shifts(k):
    return [(i, (i + k) % TM_N) for i in range(TM_N)]


def per_device(
    observed,
    att_partials,
    src_partials,
    src_slot,
    knot_block,
    live_count,
    sources,
    inverses,
    attitude,
    band_coef,
    extra_diag,
    band_offsets,
):
    core = lax.axis_index("c").astype(I32).reshape(1)
    tm = lax.axis_index("tm").astype(I32).reshape(1)
    slot = src_slot.reshape(1, CROSS)
    kb = knot_block.reshape(1, CROSS)
    chip = lax.axis_index(("x", "z")).astype(I32).reshape(1)
    knots = attitude.reshape(3, 4, 128)
    bands = band_coef.reshape(3, 3, 4, 128)
    extra = extra_diag.reshape(3, 4, 128)

    dense = pl.pallas_call(
        payload_kernel,
        out_shape=jax.ShapeDtypeStruct((CHIPS, 4, 4, 128), F32),
        in_specs=[pl.BlockSpec(memory_space=pl.ANY)] * 3,
        out_specs=pl.BlockSpec(memory_space=pltpu.VMEM),
        scratch_shapes=[
            pltpu.VMEM((3, 4, 128), F32),
            pltpu.VMEM((3, 3, 4, 128), F32),
            pltpu.VMEM((3, 4, 128), F32),
            pltpu.SemaphoreType.DMA((3,)),
        ],
        compiler_params=pltpu.CompilerParams(vmem_limit_bytes=56 * 1024 * 1024),
    )(knots, bands, extra)
    near = lax.all_to_all(dense, ("x", "z"), 0, 0, tiled=True)
    (
        cols, places, by_source, base, by_lane, by_row, pack, index, peers, choose, up, down, wide,
        ghost, products, normals, rhs, held, offsets,
    ) = run_kernel(
        prepare_kernel, 3,
        [
            (128, 128), half(144, 256), half(128, SRC_N), (CROSS, ROWS), half(384, 128),
            half(384, 128), half(SKY_N, 512), (SKY_N, 128), half(144, 128), (8, 128), (40, 128),
            (40, 128), (32, RUN), (40, 128), (1920, 128), (640, 128), (128, 128),
            (3, 4, 128), jax.ShapeDtypeStruct((3,), I32),
        ],
        live_count, core, band_offsets, observed, att_partials, src_partials, slot, kb, sources, bands, extra,
        knots,
    )
    near, cols = lax.optimization_barrier((near, cols))
    far = lax.ppermute(near, "c", [(0, 1), (1, 0)])
    masked, rhs, plain, up, down, sides = run_kernel(
        first_kernel, 2,
        [(384, 128), (128, 128), (HEAD, 128), (HEAD + 48, 128), (HEAD + 48, 128), (8, 128)],
        core, chip, near, far, cols, places, by_source, by_lane, up, down, ghost, products, rhs,
    )
    across = lax.ppermute(plain, "tm", shifts(2))
    up = lax.ppermute(up, "tm", shifts(1))
    down = lax.ppermute(down, "tm", shifts(-1))
    grads, resid = run_kernel(
        beside_kernel, 1, [(384, 128), (CROSS, ROWS)],
        live_count, masked, base, att_partials, by_lane, by_row,
    )
    outgoing, sources, resid, rhs = run_kernel(
        return_kernel, 2, [(SKY_N, 4, 128), (5, SRC_N), (CROSS, ROWS), (128, 128)],
        live_count, tm, across, plain, up, down, up, down, inverses, sources, grads, products,
        cols, by_source, by_row, pack, index, resid, src_partials, normals, rhs,
        scratch=[(HEAD, 128)], second=False,
    )
    got = lax.all_to_all(outgoing, SKY, 0, 0, tiled=True)
    knots, served, pick, rims = run_kernel(
        smooth_kernel, 4, [(3, 4, 128), (SKY_N, 2, 128), half(128, 128), (32, 128)],
        offsets, chip, core, tm, got, held, wide, sides, up, down, choose, last=False,
    )
    arrived = lax.all_to_all(served, SKY, 0, 0, tiled=True)
    masked, mine = run_kernel(
        middle_kernel, 0, [(384, 128), (HEAD + 8, 128)],
        arrived, resid, rhs, cols, peers, by_source, by_lane, choose, ghost, products,
    )
    across = lax.ppermute(mine, "tm", shifts(2))
    below = lax.ppermute(mine, "tm", shifts(1))
    above = lax.ppermute(mine, "tm", shifts(-1))
    (grads,) = run_kernel(
        beside_kernel, 1, [(384, 128)],
        live_count, masked, resid, att_partials, by_lane, by_row,
    )
    outgoing, step = run_kernel(
        return_kernel, 2, [(SKY_N, 4, 128), (5, SRC_N)],
        live_count, tm, across, mine, below, above, up, down, inverses, sources, grads, products,
        cols, by_source, by_row, pack, scratch=[(HEAD, 128)], second=True,
    )
    got = lax.all_to_all(outgoing, SKY, 0, 0, tiled=True)
    knots, sources = run_kernel(
        smooth_kernel, 4, [(3, 4, 128), (5, SRC_N)],
        offsets, chip, core, tm, got, knots, wide, sources, step, pick, rims, last=True,
    )
    return (sources, knots.reshape(3, 1, RUN))


def solution(mesh):
    torus = Mesh(mesh.devices.reshape(4, 8, 2, mesh.shape["tm"]), SKY_TM)
    return jax.shard_map(
        per_device,
        mesh=torus,
        in_specs=(
            P(SKY_TM, None),
            P(None, SKY_TM, None),
            P(None, SKY_TM, None),
            P(SKY_TM),
            P(SKY_TM),
            P(SKY_TM),
            P(None, SKY),
            P(None, None, SKY),
            P(None, "tm", SKY),
            P(None, None, "tm", SKY),
            P(None, "tm", SKY),
            P(),
        ),
        out_specs=(P(None, SKY), P(None, "tm", SKY)),
        check_vma=False,
    )
```

```python
import jax
import jax.numpy as jnp
from jax import lax
from jax.experimental import pallas as pl
from jax.experimental.pallas import tpu as pltpu
from jax.sharding import Mesh
from jax.sharding import PartitionSpec as P

F32 = jnp.float32
BF16 = jnp.bfloat16
I32 = jnp.int32
ROWS = 128
KNOTS = 16
CROSS = 128
SKY_N = 64
CHIPS = 32
TM_N = 4
SRC_N = 1024
RUN = 512
HEAD = 40
SKY = ("x", "z", "c")
SKY_TM = ("x", "z", "c", "tm")


def iota(shape, dim):
    return lax.broadcasted_iota(I32, shape, dim)


def dot(a, b):
    return jnp.dot(a.astype(BF16), b.astype(BF16), preferred_element_type=F32)


def dot_nt(a, b):
    return lax.dot_general(
        a.astype(BF16), b.astype(BF16), (((1,), (1,)), ((), ())), preferred_element_type=F32
    )


def halves(x):
    high = x.astype(BF16)
    return high, (x - high.astype(F32)).astype(BF16)


def split_dot(twice, values):
    return dot(twice, jnp.concatenate(halves(values), 0))


def thirds(x):
    high = x.astype(BF16).astype(F32)
    rest = x - high
    middle = rest.astype(BF16).astype(F32)
    return high, middle, rest - middle


def b_spline(moment_row, knot):
    tau = 1.5 + (KNOTS - 3) * (moment_row.astype(F32) + 0.5) / ROWS
    dist = jnp.abs(tau - knot.astype(F32))
    inner = 2.0 / 3.0 - dist * dist + 0.5 * dist * dist * dist
    rest = 2.0 - dist
    outer = rest * rest * rest / 6.0
    return jnp.where(dist < 1.0, inner, jnp.where(dist < 2.0, outer, 0.0))


def spline_by_lane():
    return b_spline(iota((128, 128), 1), iota((128, 128), 0) & 15)


def spline_by_row():
    return b_spline(iota((128, 128), 0), iota((128, 128), 1) & 15)


def fold_table():
    return jnp.where((iota((128, 128), 0) & 15) == (iota((128, 128), 1) & 15), 1.0, 0.0)


def table_of(table):
    return table if isinstance(table, jax.Array) else table[...]


def attitude_term(att, masked, table_ref):
    count = masked[0].shape[0]
    high, low = halves(jnp.concatenate(masked, 0))
    spread = dot(jnp.concatenate([high, low, high], 1), table_of(table_ref))
    return sum(att[a].astype(F32) * spread[a * count : (a + 1) * count] for a in range(3))


def products_sum(products_ref, masked):
    lane = iota((128, 128), 1)
    square = jnp.zeros((128, 128), F32)
    for p in range(5):
        terms = [
            products_ref[128 * (3 * p + a) : 128 * (3 * p + a) + 128, :] * masked[a]
            for a in range(3)
        ]
        row = jnp.sum(terms[0] + terms[1] + terms[2], axis=1, keepdims=True)
        square = jnp.where(lane == p, row, square)
    return square


def send_normal(rhs, onehot, refs):
    rows = rhs.T[0:8]
    parts = dot(jnp.concatenate(thirds(rows), 0), onehot)
    normal = parts[0:8] + parts[8:16] + parts[16:24]
    for ref in refs:
        for j in range(8):
            ref[pl.ds(j, 5, stride=8), :] = normal[0:5, 128 * j : 128 * j + 128]


def gradients(att, resid, table_ref):
    high, low = halves(jnp.concatenate([att[a].astype(F32) * resid for a in range(3)], 0))
    return dot(jnp.concatenate([high, low, high], 1), table_of(table_ref))


def gather_source(values8, onehot):
    parts = dot_nt(onehot, jnp.concatenate(thirds(values8), 0))
    return [
        parts[:, p : p + 1] + parts[:, 8 + p : 9 + p] + parts[:, 16 + p : 17 + p] for p in range(5)
    ]


def padded_rows(x):
    return jnp.concatenate([x, jnp.zeros((8 - x.shape[0], x.shape[1]), F32)], 0)


def column(cols_ref, i):
    return cols_ref[:, i : i + 1].astype(I32)


def stacked_spline(table):
    high, low = halves(table)
    return jnp.concatenate([high, high, low], 0)


def prepare_kernel(
    live_ref, core_ref, offsets_in_ref, obs_ref, att_ref, src_ref, slot_ref, kb_ref, sources_ref,
    bands_ref, extra_ref, knots_in_ref,
    cols_ref, places_ref, by_source_ref, base_ref, by_lane_ref, by_row_ref, pack_ref, index_ref,
    peers_ref, choose_ref, up_ref, down_ref, wide_ref, ghost_ref, products_ref, normals_ref, rhs_ref,
    knots_ref, offsets_ref,
):
    live, core = live_ref[0], core_ref[0]
    knots_ref[...] = knots_in_ref[...]
    for b in range(3):
        offsets_ref[b] = offsets_in_ref[b]
    kb, slot = kb_ref[...], slot_ref[...]
    h, lb = kb >> 5, kb & 31
    sub, lane = iota((128, 128), 0), iota((128, 128), 1)
    square = jnp.zeros((128, 128), F32)
    for i, row in enumerate((h, lb, slot)):
        square = jnp.where(sub == i, row.astype(F32), square)
    turned = square.T
    hc, lbc, slotc = (turned[:, i : i + 1].astype(I32) for i in range(3))
    same = hc == h
    c = jnp.sum(jnp.where(same & (sub < lane), 1.0, 0.0), axis=0, keepdims=True).astype(I32)
    cc = jnp.sum(jnp.where(same & (lane < sub), 1.0, 0.0), axis=1, keepdims=True)
    cols_ref[...] = jnp.where(lane == 3, cc, turned)
    cc = cc.astype(I32)
    group = lane >> 4

    place = (lbc >> 3) * CHIPS + (hc >> 1) + jnp.where((hc & 1) == core, 0, 128)
    places = jnp.where(iota((128, 256), 1) == place, 1.0, 0.0)
    by_source = jnp.where(iota((128, SRC_N), 1) == slotc, 1.0, 0.0).astype(BF16)
    by_source_ref[...] = by_source
    values = gather_source(padded_rows(sources_ref[...]), by_source)
    src_term = jnp.zeros((CROSS, ROWS), F32)
    for p in range(5):
        src_term = src_term + src_ref[p].astype(F32) * values[p]
    used = jnp.where(iota((CROSS, 1), 0) < live, 1.0, 0.0)
    base = (obs_ref[...] - src_term) * used
    base_ref[...] = base
    by_row = stacked_spline(spline_by_row())
    rhs = jnp.zeros((128, 128), F32)
    normals = [jnp.zeros((128, 128), F32)] * 5
    for p in range(5):
        one = src_ref[p].astype(F32) * used
        rhs = jnp.where(lane == p, jnp.sum(one * base, axis=1, keepdims=True), rhs)
        products_ref[384 * p : 384 * p + 384, :] = gradients(att_ref, one, by_row)
        for q in range(p + 1):
            both = jnp.sum(one * src_ref[q].astype(F32), axis=1, keepdims=True)
            normals[q] = jnp.where(lane == p, both, normals[q])
            normals[p] = jnp.where(lane == q, both, normals[p])
    rhs_ref[...] = rhs
    for q in range(5):
        normals_ref[128 * q : 128 * q + 128, :] = normals[q]
    by_lane_ref[...] = stacked_spline(spline_by_lane())
    by_row_ref[...] = by_row

    peer = iota((SKY_N, 128), 0)
    to_row = jnp.where(lb <= 1, h - 1, jnp.where(lb >= 30, h + 1, jnp.full_like(h, -1)))
    own = jnp.where(peer == h, 1.0, 0.0)
    edge = jnp.where(peer == to_row, 1.0, 0.0)
    pack_ref[...] = jnp.concatenate([own, edge, own, edge], 1).astype(BF16)
    index_ref[...] = dot(own, jnp.where(group == cc + 2, (lbc + 1).astype(F32), 0.0))
    peers = jnp.where((iota((128, 128), 1) & 63) == hc, 1.0, 0.0)

    sub8 = iota((8, 128), 0)
    after = (h == SKY_N - 1) & (lb >= 30) & (sub8 < 4)
    before = (h == 0) & (lb <= 1) & (sub8 >= 4)
    chosen = (c == (sub8 & 3)) & (after | before) & (iota((8, 128), 1) < live)
    choose = jnp.where(chosen, 1.0, 0.0)
    choose_ref[...] = choose
    pieces = [att_ref[a] for a in range(3)] + [src_ref[p] for p in range(5)]
    pieces += [*halves(base), places.astype(BF16), peers.astype(BF16)]
    ghosts = dot(choose, jnp.concatenate(pieces, 1))
    items = [ghosts[:, 128 * i : 128 * i + 128] for i in range(8)]
    empty = jnp.zeros((8, 256), F32)
    places_ref[...] = jnp.concatenate([places, ghosts[:, 1280:1536], empty], 0).astype(BF16)
    peers_ref[...] = jnp.concatenate([peers, ghosts[:, 1536:1664], empty[:, 0:128]], 0).astype(BF16)
    ghost_slot = jnp.sum(choose * slot.astype(F32), axis=1, keepdims=True)
    ghost_block = jnp.sum(choose * lb.astype(F32), axis=1, keepdims=True)
    items.append(jnp.zeros((8, 128), F32))
    items.append(jnp.where(iota((8, 128), 1) < 64, ghost_slot, ghost_block))
    for a in range(3):
        ghost_ref[8 * a : 8 * a + 8, :] = items[a]
    ghost_ref[24:32, :] = ghosts[:, 1024:1152] + ghosts[:, 1152:1280]
    ghost_ref[32:40, :] = items[9]
    for q in range(5):
        even, odd = items[2 * q], items[2 * q + 1]
        up_ref[8 * q : 8 * q + 8, :] = jnp.concatenate([even[0:4], odd[0:4]], 0)
        down_ref[8 * q : 8 * q + 8, :] = jnp.concatenate([even[4:8], odd[4:8]], 0)

    bands = [axis_rows(bands_ref[b]) for b in range(3)]
    diag = axis_rows(extra_ref) + 2.0 * (bands[0] + bands[1] + bands[2])
    for b in range(3):
        wide_ref[8 * b : 8 * b + 8, :] = bands[b]
    wide_ref[24:32, :] = 1.0 / jnp.where(diag > 0.0, diag, 1.0)


def axis_rows(tiles):
    sub = iota((8, RUN), 0)
    out = jnp.zeros((8, RUN), F32)
    for a in range(3):
        out = jnp.where(sub == a, jnp.concatenate([tiles[a][r : r + 1] for r in range(4)], 1), out)
    return out


def payload_kernel(knots_hbm, bands_hbm, extra_hbm, out_ref, knots_ref, bands_ref, extra_ref, sems):
    copies = [
        pltpu.make_async_copy(source, target, sems.at[i])
        for i, (source, target) in enumerate(
            ((bands_hbm, bands_ref), (extra_hbm, extra_ref), (knots_hbm, knots_ref))
        )
    ]
    for copy in copies:
        copy.start()
    for copy in copies:
        copy.wait()
    lane = iota((1, 128), 1)

    def ends(tiles, width):
        low, high = tiles[0:1], tiles[3:4]
        return jnp.where(lane < width, low, jnp.where(lane >= 128 - width, high, 0.0))

    rows = []
    for a in range(3):
        bands = [bands_ref[b, a] for b in range(3)]
        diag = extra_ref[a] + 2.0 * (bands[0] + bands[1] + bands[2])
        row = ends(diag, 32) + pltpu.roll(ends(bands[0], 16), 48, 1)
        rows.append(row + pltpu.roll(ends(bands[1], 16), 80, 1))
    third = [ends(bands_ref[2, a], 16) for a in range(3)]
    rows.append(third[0] + pltpu.roll(third[1], 48, 1) + pltpu.roll(third[2], 80, 1))
    sub = iota((4, 128), 0)
    edge = jnp.zeros((4, 128), F32)
    for i, row in enumerate(rows):
        edge = jnp.where(sub == i, row, edge)
    for chip in range(CHIPS):
        out_ref[chip, 0:3] = knots_ref[...]
        out_ref[chip, 3] = edge


def rim_tiles(before, after):
    sub, lane = iota((8, 128), 0), iota((8, 128), 1)

    def tile(sources, width):
        out = jnp.zeros((8, 128), F32)
        for a, (row, turn) in enumerate(sources):
            both = [e[row : row + 1] for e in (after, before)]
            if turn:
                both = [pltpu.roll(e, 128 - turn, 1) for e in both]
            one = jnp.where(lane < width, both[0], jnp.where(lane >= 128 - width, both[1], 0.0))
            out = jnp.where(sub == a, one, out)
        return out

    bands = [
        tile([(a, 48) for a in range(3)], 16),
        tile([(a, 80) for a in range(3)], 16),
        tile([(3, 0), (3, 48), (3, 80)], 16),
    ]
    diag = tile([(a, 0) for a in range(3)], 32)
    return bands + [1.0 / jnp.where(diag > 0.0, diag, 1.0)]


def first_kernel(
    core_ref, chip_ref, near_ref, far_ref, cols_ref, places_ref, by_source_ref, by_lane_ref,
    up_in_ref, down_in_ref, ghost_ref, products_ref, rhs_in_ref,
    masked_ref, rhs_ref, plain_ref, up_ref, down_ref, sides_ref,
):
    tables = []
    for a in range(3):
        rows = [ref[:, a, r, :] for ref in (near_ref, far_ref) for r in range(4)]
        tables += halves(jnp.concatenate(rows, 0))
    found = dot(places_ref[...], jnp.concatenate(tables, 1))
    mine = (iota((128, 128), 1) >> 4) == (column(cols_ref, 1) & 7)
    facts = ghost_ref[32:40, :]
    ghost_mine = (iota((8, 128), 1) >> 4) == (facts[:, 64:65].astype(I32) & 7)
    masked, ghost_masked = [], []
    for a in range(3):
        whole = found[:, 256 * a : 256 * a + 128] + found[:, 256 * a + 128 : 256 * a + 256]
        masked.append(jnp.where(mine, whole[0:128], 0.0))
        ghost_masked.append(jnp.where(ghost_mine, whole[128:136], 0.0))
        masked_ref[128 * a : 128 * a + 128, :] = masked[a]
    rhs = rhs_in_ref[...] - products_sum(products_ref, masked)
    rhs_ref[...] = rhs
    send_normal(rhs, by_source_ref[...], (plain_ref, up_ref, down_ref))
    ghost_att = [ghost_ref[8 * a : 8 * a + 8, :] for a in range(3)]
    ghosts = ghost_ref[24:32, :] - attitude_term(ghost_att, ghost_masked, by_lane_ref)
    up_ref[HEAD : HEAD + 40, :] = up_in_ref[...]
    down_ref[HEAD : HEAD + 40, :] = down_in_ref[...]
    up_ref[HEAD + 32 : HEAD + 36, :] = ghosts[0:4]
    down_ref[HEAD + 32 : HEAD + 36, :] = ghosts[4:8]
    core, chip = core_ref[0], chip_ref[0]
    before = jnp.where(core == 0, jnp.maximum(chip - 1, 0), chip)
    after = jnp.where(core == 0, chip, jnp.minimum(chip + 1, CHIPS - 1))
    sides_ref[0:4, :] = far_ref[before, 3]
    sides_ref[4:8, :] = far_ref[after, 3]
    empty = jnp.zeros((4, 128), F32)
    final = jnp.where(core == 1, near_ref[CHIPS - 1, 3], far_ref[CHIPS - 1, 3])
    initial = jnp.where(core == 0, near_ref[0, 3], far_ref[0, 3])
    up_ref[HEAD + 40 : HEAD + 48, :] = jnp.concatenate([final, empty], 0)
    down_ref[HEAD + 40 : HEAD + 48, :] = jnp.concatenate([initial, empty], 0)


def beside_kernel(
    live_ref, masked_ref, resid_in_ref, att_ref, by_lane_ref, by_row_ref, grads_ref, *rest
):
    masked = [masked_ref[128 * a : 128 * a + 128, :] for a in range(3)]
    used = jnp.where(iota((CROSS, 1), 0) < live_ref[0], 1.0, 0.0)
    resid = resid_in_ref[...] - attitude_term(att_ref, masked, by_lane_ref) * used
    grads_ref[...] = gradients(att_ref, resid, by_row_ref)
    for ref in rest:
        ref[...] = resid


def middle_kernel(
    got_ref, resid_ref, rhs_in_ref, cols_ref, peers_ref, by_source_ref, by_lane_ref, choose_ref,
    ghost_ref, products_ref, masked_ref, send_ref,
):
    found = split_dot(peers_ref[...], jnp.concatenate([got_ref[:, 0, :], got_ref[:, 1, :]], 1))
    group = iota((136, 128), 1) >> 4
    cc = jnp.concatenate([column(cols_ref, 3), iota((8, 1), 0) & 3], 0)
    front, back = found[0:136, 0:128], found[0:136, 128:256]
    masked = [
        jnp.where(group == cc, front, 0.0),
        jnp.where(group == cc + 4, front, 0.0),
        jnp.where(group == cc, back, 0.0),
    ]
    for a in range(3):
        masked_ref[128 * a : 128 * a + 128, :] = masked[a][0:128]
    rhs = rhs_in_ref[...] - products_sum(products_ref, [m[0:128] for m in masked])
    send_normal(rhs, by_source_ref[...], (send_ref,))
    ghost_att = [ghost_ref[8 * a : 8 * a + 8, :] for a in range(3)]
    term = attitude_term(ghost_att, [m[128:136] for m in masked], by_lane_ref)
    ghosts = dot(choose_ref[...], jnp.concatenate(halves(resid_ref[...]), 1))
    send_ref[HEAD : HEAD + 8, :] = ghosts[:, 0:128] + ghosts[:, 128:256] - term


def return_kernel(
    live_ref, tm_ref, across_ref, own_ref, below_ref, above_ref, up_ref, down_ref, inverses_ref,
    sources_in_ref, grads_ref, products_ref, cols_ref, by_source_ref, by_row_ref, pack_ref,
    *rest, second,
):
    if second:
        out_ref, sources_ref = rest[:2]
    else:
        index_ref, resid_in_ref, src_ref, normals_ref, rhs_in_ref = rest[:5]
        out_ref, sources_ref, resid_ref, rhs_ref = rest[5:9]
    tm, total_ref = tm_ref[0], rest[-1]
    total_ref[...] = (
        own_ref[0:HEAD, :] + across_ref[0:HEAD, :] + below_ref[0:HEAD, :] + above_ref[0:HEAD, :]
    )
    normal = jnp.concatenate([total_ref[pl.ds(j, 5, stride=8), :] for j in range(8)], 1)
    sub8 = iota((8, SRC_N), 0)
    step = jnp.zeros((8, SRC_N), F32)
    for p in range(5):
        row = jnp.sum(inverses_ref[p] * normal, axis=0, keepdims=True)
        step = jnp.where(sub8 == p, row, step)
    sources_ref[...] = step[0:5] if second else sources_in_ref[...] + step[0:5]
    ghost8 = iota((8, 128), 0)
    there = jnp.where(ghost8 < 4, jnp.where(tm > 0, 1.0, 0.0), jnp.where(tm < TM_N - 1, 1.0, 0.0))

    def item(i):
        row = HEAD + 4 * i
        return jnp.concatenate([up_ref[row : row + 4, :], down_ref[row : row + 4, :]], 0)

    facts = item(9)
    ghost_slot = facts[:, 0:1].astype(I32)
    ghost_block = facts[:, 64:65].astype(I32)
    ghost_onehot = jnp.where(iota((8, SRC_N), 1) == ghost_slot, 1.0, 0.0)
    values = gather_source(step, by_source_ref[...])
    ghost_values = gather_source(step, ghost_onehot)
    ghost_change = jnp.zeros((8, ROWS), F32)
    for p in range(5):
        ghost_change = ghost_change + item(3 + p) * ghost_values[p]
    if second:
        ghost_resid = jnp.concatenate(
            [below_ref[HEAD : HEAD + 4, :], above_ref[HEAD + 4 : HEAD + 8, :]], 0
        )
    else:
        ghost_resid = item(8)
        used = jnp.where(iota((CROSS, 1), 0) < live_ref[0], 1.0, 0.0)
        change = jnp.zeros((CROSS, ROWS), F32)
        rhs = rhs_in_ref[...]
        for p in range(5):
            change = change + src_ref[p].astype(F32) * values[p]
            rhs = rhs - normals_ref[128 * p : 128 * p + 128, :] * values[p]
        resid_ref[...] = resid_in_ref[...] - used * change
        rhs_ref[...] = rhs
    ghost_resid = (ghost_resid - ghost_change) * there
    ghost_grads = gradients([item(a) for a in range(3)], ghost_resid, by_row_ref)
    parts = []
    for a in range(3):
        part = grads_ref[128 * a : 128 * a + 128, :]
        for p in range(5):
            low_row = 128 * (3 * p + a)
            part = part - products_ref[low_row : low_row + 128, :] * values[p]
        parts.append(part)
    lbc, cc = column(cols_ref, 1), column(cols_ref, 3)
    group = iota((128, 128), 1) >> 4
    edge_group = jnp.where(lbc <= 1, lbc, lbc - 24)
    own = group == cc + 2
    edge = group == edge_group
    high, low = halves(jnp.concatenate(parts, 1))
    own3, edge3 = jnp.concatenate([own] * 3, 1), jnp.concatenate([edge] * 3, 1)
    none = jnp.zeros_like(high)
    table = [jnp.where(mask, part, none) for part in (high, low) for mask in (own3, edge3)]
    packed = dot(pack_ref[...], jnp.concatenate(table, 0))
    peer = iota((SKY_N, 128), 0)
    ghost_group = iota((8, 128), 1) >> 4
    ghost_own = ghost_group == jnp.where(ghost8[:, 0:1] < 4, ghost_block - 24, ghost_block)
    for a in range(3):
        ghost = jnp.where(ghost_own, ghost_grads[8 * a : 8 * a + 8], 0.0)
        from_below = jnp.sum(jnp.where(ghost8 < 4, ghost, 0.0), axis=0, keepdims=True)
        from_above = jnp.sum(jnp.where(ghost8 >= 4, ghost, 0.0), axis=0, keepdims=True)
        block = packed[:, 128 * a : 128 * a + 128]
        block = block + jnp.where(peer == 0, from_below, 0.0)
        block = block + jnp.where(peer == SKY_N - 1, from_above, 0.0)
        if second:
            out_ref[:, 0, 128 * a : 128 * a + 128] = block
        else:
            out_ref[:, a, :] = block
    if not second:
        out_ref[:, 3, :] = index_ref[...]


def smooth_kernel(
    offsets_ref, chip_ref, core_ref, tm_ref, got_ref, knots_in_ref, wide_ref, one_ref, two_ref,
    three_ref, four_ref, *outs, last,
):
    knots_ref = outs[0]
    lane = iota((SKY_N, 128), 1)
    if last:
        sources_in_ref, step_ref, pick_ref, rims_ref = one_ref, two_ref, three_ref, four_ref
        pick = pick_ref[...]
        rims = [rims_ref[8 * i : 8 * i + 8, :] for i in range(4)]
    else:
        sides_ref, up_ref, down_ref = one_ref, two_ref, three_ref
        place, tm = chip_ref[0] * 2 + core_ref[0], tm_ref[0]
        below = jnp.where(tm > 0, up_ref[HEAD + 40 : HEAD + 44, :], 0.0)
        above = jnp.where(tm < TM_N - 1, down_ref[HEAD + 40 : HEAD + 44, :], 0.0)
        before = jnp.where(place == 0, below, sides_ref[0:4, :])
        after = jnp.where(place == SKY_N - 1, above, sides_ref[4:8, :])
        rims = rim_tiles(before, after)
        for i in range(4):
            outs[3][8 * i : 8 * i + 8, :] = rims[i]
        index = got_ref[:, 3, :]
        square = jnp.concatenate([index, index], 0).T
        block32 = (iota((32, 128), 0) + 1).astype(F32)
        pick = jnp.concatenate(
            [
                jnp.where(square[16 * (2 + c) : 16 * (2 + c) + 1, :] == block32, 1.0, 0.0)
                for c in range(4)
            ],
            0,
        ).astype(BF16)
        outs[2][...] = pick
    got = [got_ref[:, 0, 128 * a : 128 * a + 128] if last else got_ref[:, a, :] for a in range(3)]
    summed = split_dot(pick, jnp.concatenate(got, 1))
    row128 = iota((128, 128), 0)
    group128 = iota((128, 128), 1) >> 4
    keep = group128 == (row128 >> 5) + 2
    fold = fold_table()
    stack = []
    for a in range(3):
        one = jnp.where(keep, summed[:, 128 * a : 128 * a + 128], 0.0)
        stack.append(one[0:32] + one[32:64] + one[64:96] + one[96:128])
    high, low = halves(jnp.concatenate(stack, 0))
    spread = dot(jnp.concatenate([high, low], 1), jnp.concatenate([fold, fold], 0))
    in_row = (iota((8, 128), 1) >> 4) == iota((8, 128), 0)
    sub8, lane8 = iota((8, 128), 0), iota((8, 128), 1)
    grad = [jnp.zeros((8, 128), F32)] * 5
    for a in range(3):
        for r in range(5):
            if r < 4:
                piece = jnp.where(in_row, spread[32 * a + 8 * r : 32 * a + 8 * r + 8], 0.0)
            else:
                piece = jnp.where((lane < 32) | (lane >= 96), got[a], 0.0)
            grad[r] = jnp.where(sub8 == a, jnp.sum(piece, axis=0, keepdims=True), grad[r])
    bands, scale = [], None
    for i in range(4):
        tiles = [wide_ref[8 * i : 8 * i + 8, 128 * r : 128 * r + 128] for r in range(4)]
        if i < 3:
            bands.append([*tiles, rims[i]])
        else:
            scale = [*tiles, rims[i]]
    offsets = [offsets_ref[b] for b in range(3)]
    wraps = [(lane8 < offset, lane8 >= 128 - offset) for offset in offsets]
    delta = [g * f for g, f in zip(grad, scale, strict=True)]
    for _ in range(2):
        total = grad
        for b in range(3):
            low = [pltpu.roll(d, offsets[b], 1) for d in delta]
            high = [pltpu.roll(d, 128 - offsets[b], 1) for d in delta]
            first, final = wraps[b]
            total = [
                total[r]
                + bands[b][r]
                * (
                    jnp.where(first, low[(r + 4) % 5], low[r])
                    + jnp.where(final, high[(r + 1) % 5], high[r])
                )
                for r in range(5)
            ]
        delta = [t * f for t, f in zip(total, scale, strict=True)]
    for a in range(3):
        for r in range(4):
            tile = delta[r][a : a + 1]
            knots_ref[a, r : r + 1, :] = knots_in_ref[a, r : r + 1, :] + tile
    if last:
        outs[1][...] = sources_in_ref[...] + step_ref[...]
        return
    send_ref = outs[1]
    spreads = []
    for a in range(3):
        for r in range(4):
            tile = delta[r][a : a + 1]
            spreads.append(jnp.where(in_row, tile, 0.0))
    high, low = halves(jnp.concatenate(spreads, 0))
    blocks = dot(jnp.concatenate([high, low], 1), jnp.concatenate([fold, fold], 0))
    table = jnp.concatenate([blocks[32 * a : 32 * a + 32] for a in range(3)], 1)
    slots = [index[:, 16 * (2 + c) : 16 * (2 + c) + 1].astype(I32) - 1 for c in range(4)]
    slot = jnp.concatenate(slots, 0)
    by_block = jnp.where((iota((4 * SKY_N, 64), 1) & 31) == slot, 1.0, 0.0)
    found = split_dot(by_block, table)
    group = lane >> 4
    front = jnp.zeros((SKY_N, 128), F32)
    back = jnp.zeros((SKY_N, 128), F32)
    for c in range(4):
        rows = found[SKY_N * c : SKY_N * (c + 1)]
        part = [rows[:, 128 * a : 128 * a + 128] for a in range(3)]
        front = jnp.where(group == c, part[0], jnp.where(group == c + 4, part[1], front))
        back = jnp.where(group == c, part[2], back)
    send_ref[:, 0, :] = front
    send_ref[:, 1, :] = back


def run_kernel(body, scalars, outs, *args, scratch=(), flops=10_000_000, **static):
    specs = [
        pl.BlockSpec(memory_space=pltpu.SMEM if i < scalars else pltpu.VMEM)
        for i in range(len(args))
    ]
    shapes = [o if isinstance(o, jax.ShapeDtypeStruct) else jax.ShapeDtypeStruct(o, F32) for o in outs]

    def kernel(*refs):
        body(*refs, **static)

    return pl.pallas_call(
        kernel,
        out_shape=shapes,
        in_specs=specs,
        out_specs=[
            pl.BlockSpec(memory_space=pltpu.SMEM if s.dtype == I32 else pltpu.VMEM) for s in shapes
        ],
        scratch_shapes=[pltpu.VMEM(shape, F32) for shape in scratch],
        cost_estimate=pl.CostEstimate(flops=flops, bytes_accessed=2_000_000, transcendentals=0),
        compiler_params=pltpu.CompilerParams(vmem_limit_bytes=32 * 1024 * 1024),
    )(*args)


def half(*shape):
    return jax.ShapeDtypeStruct(shape, BF16)


def shifts(k):
    return [(i, (i + k) % TM_N) for i in range(TM_N)]


def per_device(
    observed,
    att_partials,
    src_partials,
    src_slot,
    knot_block,
    live_count,
    sources,
    inverses,
    attitude,
    band_coef,
    extra_diag,
    band_offsets,
):
    core = lax.axis_index("c").astype(I32).reshape(1)
    tm = lax.axis_index("tm").astype(I32).reshape(1)
    slot = src_slot.reshape(1, CROSS)
    kb = knot_block.reshape(1, CROSS)
    chip = lax.axis_index(("x", "z")).astype(I32).reshape(1)
    knots = attitude.reshape(3, 4, 128)
    bands = band_coef.reshape(3, 3, 4, 128)
    extra = extra_diag.reshape(3, 4, 128)

    dense = pl.pallas_call(
        payload_kernel,
        out_shape=jax.ShapeDtypeStruct((CHIPS, 4, 4, 128), F32),
        in_specs=[pl.BlockSpec(memory_space=pl.ANY)] * 3,
        out_specs=pl.BlockSpec(memory_space=pltpu.VMEM),
        scratch_shapes=[
            pltpu.VMEM((3, 4, 128), F32),
            pltpu.VMEM((3, 3, 4, 128), F32),
            pltpu.VMEM((3, 4, 128), F32),
            pltpu.SemaphoreType.DMA((3,)),
        ],
        compiler_params=pltpu.CompilerParams(vmem_limit_bytes=56 * 1024 * 1024),
    )(knots, bands, extra)
    near = lax.all_to_all(dense, ("x", "z"), 0, 0, tiled=True)
    (
        cols, places, by_source, base, by_lane, by_row, pack, index, peers, choose, up, down, wide,
        ghost, products, normals, rhs, held, offsets,
    ) = run_kernel(
        prepare_kernel, 3,
        [
            (128, 128), half(144, 256), half(128, SRC_N), (CROSS, ROWS), half(384, 128),
            half(384, 128), half(SKY_N, 512), (SKY_N, 128), half(144, 128), (8, 128), (40, 128),
            (40, 128), (32, RUN), (40, 128), (1920, 128), (640, 128), (128, 128),
            (3, 4, 128), jax.ShapeDtypeStruct((3,), I32),
        ],
        live_count, core, band_offsets, observed, att_partials, src_partials, slot, kb, sources, bands, extra,
        knots,
    )
    near, cols = lax.optimization_barrier((near, cols))
    far = lax.ppermute(near, "c", [(0, 1), (1, 0)])
    masked, rhs, plain, up, down, sides = run_kernel(
        first_kernel, 2,
        [(384, 128), (128, 128), (HEAD, 128), (HEAD + 48, 128), (HEAD + 48, 128), (8, 128)],
        core, chip, near, far, cols, places, by_source, by_lane, up, down, ghost, products, rhs,
    )
    across = lax.ppermute(plain, "tm", shifts(2))
    up = lax.ppermute(up, "tm", shifts(1))
    down = lax.ppermute(down, "tm", shifts(-1))
    grads, resid = run_kernel(
        beside_kernel, 1, [(384, 128), (CROSS, ROWS)],
        live_count, masked, base, att_partials, by_lane, by_row,
    )
    outgoing, sources, resid, rhs = run_kernel(
        return_kernel, 2, [(SKY_N, 4, 128), (5, SRC_N), (CROSS, ROWS), (128, 128)],
        live_count, tm, across, plain, up, down, up, down, inverses, sources, grads, products,
        cols, by_source, by_row, pack, index, resid, src_partials, normals, rhs,
        scratch=[(HEAD, 128)], second=False,
    )
    got = lax.all_to_all(outgoing, SKY, 0, 0, tiled=True)
    knots, served, pick, rims = run_kernel(
        smooth_kernel, 4, [(3, 4, 128), (SKY_N, 2, 128), half(128, 128), (32, 128)],
        offsets, chip, core, tm, got, held, wide, sides, up, down, choose, last=False,
    )
    arrived = lax.all_to_all(served, SKY, 0, 0, tiled=True)
    masked, mine = run_kernel(
        middle_kernel, 0, [(384, 128), (HEAD + 8, 128)],
        arrived, resid, rhs, cols, peers, by_source, by_lane, choose, ghost, products,
    )
    across = lax.ppermute(mine, "tm", shifts(2))
    below = lax.ppermute(mine, "tm", shifts(1))
    above = lax.ppermute(mine, "tm", shifts(-1))
    (grads,) = run_kernel(
        beside_kernel, 1, [(384, 128)],
        live_count, masked, resid, att_partials, by_lane, by_row,
    )
    outgoing, step = run_kernel(
        return_kernel, 2, [(SKY_N, 1, 384), (5, SRC_N)],
        live_count, tm, across, mine, below, above, up, down, inverses, sources, grads, products,
        cols, by_source, by_row, pack, scratch=[(HEAD, 128)], second=True,
    )
    got = lax.all_to_all(outgoing, SKY, 0, 0, tiled=True)
    knots, sources = run_kernel(
        smooth_kernel, 4, [(3, 4, 128), (5, SRC_N)],
        offsets, chip, core, tm, got, knots, wide, sources, step, pick, rims, last=True,
    )
    return (sources, knots.reshape(3, 1, RUN))


def solution(mesh):
    torus = Mesh(mesh.devices.reshape(4, 8, 2, mesh.shape["tm"]), SKY_TM)
    return jax.shard_map(
        per_device,
        mesh=torus,
        in_specs=(
            P(SKY_TM, None),
            P(None, SKY_TM, None),
            P(None, SKY_TM, None),
            P(SKY_TM),
            P(SKY_TM),
            P(SKY_TM),
            P(None, SKY),
            P(None, None, SKY),
            P(None, "tm", SKY),
            P(None, None, "tm", SKY),
            P(None, "tm", SKY),
            P(),
        ),
        out_specs=(P(None, SKY), P(None, "tm", SKY)),
        check_vma=False,
    )
```

```python
import jax
import jax.numpy as jnp
from jax import lax
from jax.experimental import pallas as pl
from jax.experimental.pallas import tpu as pltpu
from jax.sharding import Mesh
from jax.sharding import PartitionSpec as P

F32 = jnp.float32
BF16 = jnp.bfloat16
I32 = jnp.int32
ROWS = 128
KNOTS = 16
CROSS = 128
SKY_N = 64
CHIPS = 32
TM_N = 4
SRC_N = 1024
RUN = 512
HEAD = 40
SKY = ("x", "z", "c")
SKY_TM = ("x", "z", "c", "tm")


def iota(shape, dim):
    return lax.broadcasted_iota(I32, shape, dim)


def dot(a, b):
    return jnp.dot(a.astype(BF16), b.astype(BF16), preferred_element_type=F32)


def dot_nt(a, b):
    return lax.dot_general(
        a.astype(BF16), b.astype(BF16), (((1,), (1,)), ((), ())), preferred_element_type=F32
    )


def halves(x):
    high = x.astype(BF16)
    return high, (x - high.astype(F32)).astype(BF16)


def split_dot(twice, values):
    return dot(twice, jnp.concatenate(halves(values), 0))


def thirds(x):
    high = x.astype(BF16).astype(F32)
    rest = x - high
    middle = rest.astype(BF16).astype(F32)
    return high, middle, rest - middle


def b_spline(moment_row, knot):
    tau = 1.5 + (KNOTS - 3) * (moment_row.astype(F32) + 0.5) / ROWS
    dist = jnp.abs(tau - knot.astype(F32))
    inner = 2.0 / 3.0 - dist * dist + 0.5 * dist * dist * dist
    rest = 2.0 - dist
    outer = rest * rest * rest / 6.0
    return jnp.where(dist < 1.0, inner, jnp.where(dist < 2.0, outer, 0.0))


def spline_by_lane():
    return b_spline(iota((128, 128), 1), iota((128, 128), 0) & 15)


def spline_by_row():
    return b_spline(iota((128, 128), 0), iota((128, 128), 1) & 15)


def fold_table():
    return jnp.where((iota((128, 128), 0) & 15) == (iota((128, 128), 1) & 15), 1.0, 0.0)


def table_of(table):
    return table if isinstance(table, jax.Array) else table[...]


def attitude_term(att, masked, table_ref):
    count = masked[0].shape[0]
    high, low = halves(jnp.concatenate(masked, 0))
    spread = dot(jnp.concatenate([high, low, high], 1), table_of(table_ref))
    return sum(att[a].astype(F32) * spread[a * count : (a + 1) * count] for a in range(3))


def products_sum(products_ref, masked):
    lane = iota((128, 128), 1)
    square = jnp.zeros((128, 128), F32)
    for p in range(5):
        terms = [
            products_ref[128 * (3 * p + a) : 128 * (3 * p + a) + 128, :] * masked[a]
            for a in range(3)
        ]
        row = jnp.sum(terms[0] + terms[1] + terms[2], axis=1, keepdims=True)
        square = jnp.where(lane == p, row, square)
    return square


def send_normal(rhs, onehot, refs):
    rows = rhs.T[0:8]
    parts = dot(jnp.concatenate(thirds(rows), 0), onehot)
    normal = parts[0:8] + parts[8:16] + parts[16:24]
    for ref in refs:
        for j in range(8):
            ref[pl.ds(j, 5, stride=8), :] = normal[0:5, 128 * j : 128 * j + 128]


def gradients(att, resid, table_ref):
    high, low = halves(jnp.concatenate([att[a].astype(F32) * resid for a in range(3)], 0))
    return dot(jnp.concatenate([high, low, high], 1), table_of(table_ref))


def gather_source(values8, onehot):
    parts = dot_nt(onehot, jnp.concatenate(thirds(values8), 0))
    return [
        parts[:, p : p + 1] + parts[:, 8 + p : 9 + p] + parts[:, 16 + p : 17 + p] for p in range(5)
    ]


def padded_rows(x):
    return jnp.concatenate([x, jnp.zeros((8 - x.shape[0], x.shape[1]), F32)], 0)


def column(cols_ref, i):
    return cols_ref[:, i : i + 1].astype(I32)


def stacked_spline(table):
    high, low = halves(table)
    return jnp.concatenate([high, high, low], 0)


def prepare_kernel(
    live_ref, core_ref, offsets_in_ref, obs_ref, att_ref, src_ref, slot_ref, kb_ref, sources_ref,
    bands_ref, extra_ref, knots_in_ref,
    cols_ref, places_ref, by_source_ref, base_ref, by_lane_ref, by_row_ref, pack_ref, index_ref,
    peers_ref, choose_ref, up_ref, down_ref, wide_ref, ghost_ref, products_ref, normals_ref, rhs_ref,
    knots_ref, offsets_ref,
):
    live, core = live_ref[0], core_ref[0]
    knots_ref[...] = knots_in_ref[...]
    for b in range(3):
        offsets_ref[b] = offsets_in_ref[b]
    kb, slot = kb_ref[...], slot_ref[...]
    h, lb = kb >> 5, kb & 31
    sub, lane = iota((128, 128), 0), iota((128, 128), 1)
    square = jnp.zeros((128, 128), F32)
    for i, row in enumerate((h, lb, slot)):
        square = jnp.where(sub == i, row.astype(F32), square)
    turned = square.T
    hc, lbc, slotc = (turned[:, i : i + 1].astype(I32) for i in range(3))
    same = hc == h
    c = jnp.sum(jnp.where(same & (sub < lane), 1.0, 0.0), axis=0, keepdims=True).astype(I32)
    cc = jnp.sum(jnp.where(same & (lane < sub), 1.0, 0.0), axis=1, keepdims=True)
    cols_ref[...] = jnp.where(lane == 3, cc, turned)
    cc = cc.astype(I32)
    group = lane >> 4

    place = (lbc >> 3) * CHIPS + (hc >> 1) + jnp.where((hc & 1) == core, 0, 128)
    places = jnp.where(iota((128, 256), 1) == place, 1.0, 0.0)
    by_source = jnp.where(iota((128, SRC_N), 1) == slotc, 1.0, 0.0).astype(BF16)
    by_source_ref[...] = by_source
    values = gather_source(padded_rows(sources_ref[...]), by_source)
    src_term = jnp.zeros((CROSS, ROWS), F32)
    for p in range(5):
        src_term = src_term + src_ref[p].astype(F32) * values[p]
    used = jnp.where(iota((CROSS, 1), 0) < live, 1.0, 0.0)
    base = (obs_ref[...] - src_term) * used
    base_ref[...] = base
    by_row = stacked_spline(spline_by_row())
    rhs = jnp.zeros((128, 128), F32)
    normals = [jnp.zeros((128, 128), F32)] * 5
    for p in range(5):
        one = src_ref[p].astype(F32) * used
        rhs = jnp.where(lane == p, jnp.sum(one * base, axis=1, keepdims=True), rhs)
        products_ref[384 * p : 384 * p + 384, :] = gradients(att_ref, one, by_row)
        for q in range(p + 1):
            both = jnp.sum(one * src_ref[q].astype(F32), axis=1, keepdims=True)
            normals[q] = jnp.where(lane == p, both, normals[q])
            normals[p] = jnp.where(lane == q, both, normals[p])
    rhs_ref[...] = rhs
    for q in range(5):
        normals_ref[128 * q : 128 * q + 128, :] = normals[q]
    by_lane_ref[...] = stacked_spline(spline_by_lane())
    by_row_ref[...] = by_row

    peer = iota((SKY_N, 128), 0)
    to_row = jnp.where(lb <= 1, h - 1, jnp.where(lb >= 30, h + 1, jnp.full_like(h, -1)))
    own = jnp.where(peer == h, 1.0, 0.0)
    edge = jnp.where(peer == to_row, 1.0, 0.0)
    pack_ref[...] = jnp.concatenate([own, edge, own, edge], 1).astype(BF16)
    index_ref[...] = dot(own, jnp.where(group == cc + 2, (lbc + 1).astype(F32), 0.0))
    peers = jnp.where((iota((128, 128), 1) & 63) == hc, 1.0, 0.0)

    sub8 = iota((8, 128), 0)
    after = (h == SKY_N - 1) & (lb >= 30) & (sub8 < 4)
    before = (h == 0) & (lb <= 1) & (sub8 >= 4)
    chosen = (c == (sub8 & 3)) & (after | before) & (iota((8, 128), 1) < live)
    choose = jnp.where(chosen, 1.0, 0.0)
    choose_ref[...] = choose
    pieces = [att_ref[a] for a in range(3)] + [src_ref[p] for p in range(5)]
    pieces += [*halves(base), places.astype(BF16), peers.astype(BF16)]
    ghosts = dot(choose, jnp.concatenate(pieces, 1))
    items = [ghosts[:, 128 * i : 128 * i + 128] for i in range(8)]
    empty = jnp.zeros((8, 256), F32)
    places_ref[...] = jnp.concatenate([places, ghosts[:, 1280:1536], empty], 0).astype(BF16)
    peers_ref[...] = jnp.concatenate([peers, ghosts[:, 1536:1664], empty[:, 0:128]], 0).astype(BF16)
    ghost_slot = jnp.sum(choose * slot.astype(F32), axis=1, keepdims=True)
    ghost_block = jnp.sum(choose * lb.astype(F32), axis=1, keepdims=True)
    items.append(jnp.zeros((8, 128), F32))
    items.append(jnp.where(iota((8, 128), 1) < 64, ghost_slot, ghost_block))
    for a in range(3):
        ghost_ref[8 * a : 8 * a + 8, :] = items[a]
    ghost_ref[24:32, :] = ghosts[:, 1024:1152] + ghosts[:, 1152:1280]
    ghost_ref[32:40, :] = items[9]
    for q in range(5):
        even, odd = items[2 * q], items[2 * q + 1]
        up_ref[8 * q : 8 * q + 8, :] = jnp.concatenate([even[0:4], odd[0:4]], 0)
        down_ref[8 * q : 8 * q + 8, :] = jnp.concatenate([even[4:8], odd[4:8]], 0)

    bands = [axis_rows(bands_ref[b]) for b in range(3)]
    diag = axis_rows(extra_ref) + 2.0 * (bands[0] + bands[1] + bands[2])
    for b in range(3):
        wide_ref[8 * b : 8 * b + 8, :] = bands[b]
    wide_ref[24:32, :] = 1.0 / jnp.where(diag > 0.0, diag, 1.0)


def axis_rows(tiles):
    sub = iota((8, RUN), 0)
    out = jnp.zeros((8, RUN), F32)
    for a in range(3):
        out = jnp.where(sub == a, jnp.concatenate([tiles[a][r : r + 1] for r in range(4)], 1), out)
    return out


def payload_kernel(knots_hbm, bands_hbm, extra_hbm, out_ref, knots_ref, bands_ref, extra_ref, sems):
    copies = [
        pltpu.make_async_copy(source, target, sems.at[i])
        for i, (source, target) in enumerate(
            ((bands_hbm, bands_ref), (extra_hbm, extra_ref), (knots_hbm, knots_ref))
        )
    ]
    for copy in copies:
        copy.start()
    for copy in copies:
        copy.wait()
    lane = iota((1, 128), 1)

    def ends(tiles, width):
        low, high = tiles[0:1], tiles[3:4]
        return jnp.where(lane < width, low, jnp.where(lane >= 128 - width, high, 0.0))

    rows = []
    for a in range(3):
        bands = [bands_ref[b, a] for b in range(3)]
        diag = extra_ref[a] + 2.0 * (bands[0] + bands[1] + bands[2])
        row = ends(diag, 32) + pltpu.roll(ends(bands[0], 16), 48, 1)
        rows.append(row + pltpu.roll(ends(bands[1], 16), 80, 1))
    third = [ends(bands_ref[2, a], 16) for a in range(3)]
    rows.append(third[0] + pltpu.roll(third[1], 48, 1) + pltpu.roll(third[2], 80, 1))
    sub = iota((4, 128), 0)
    edge = jnp.zeros((4, 128), F32)
    for i, row in enumerate(rows):
        edge = jnp.where(sub == i, row, edge)
    for chip in range(CHIPS):
        out_ref[chip, 0:3] = knots_ref[...]
        out_ref[chip, 3] = edge


def rim_tiles(before, after):
    sub, lane = iota((8, 128), 0), iota((8, 128), 1)

    def tile(sources, width):
        out = jnp.zeros((8, 128), F32)
        for a, (row, turn) in enumerate(sources):
            both = [e[row : row + 1] for e in (after, before)]
            if turn:
                both = [pltpu.roll(e, 128 - turn, 1) for e in both]
            one = jnp.where(lane < width, both[0], jnp.where(lane >= 128 - width, both[1], 0.0))
            out = jnp.where(sub == a, one, out)
        return out

    bands = [
        tile([(a, 48) for a in range(3)], 16),
        tile([(a, 80) for a in range(3)], 16),
        tile([(3, 0), (3, 48), (3, 80)], 16),
    ]
    diag = tile([(a, 0) for a in range(3)], 32)
    return bands + [1.0 / jnp.where(diag > 0.0, diag, 1.0)]


def first_kernel(
    core_ref, chip_ref, near_ref, far_ref, cols_ref, places_ref, by_source_ref, by_lane_ref,
    ghost_ref, products_ref, rhs_in_ref,
    masked_ref, rhs_ref, plain_ref, up_ref, down_ref, sides_ref,
):
    tables = []
    for a in range(3):
        rows = [ref[:, a, r, :] for ref in (near_ref, far_ref) for r in range(4)]
        tables += halves(jnp.concatenate(rows, 0))
    found = dot(places_ref[...], jnp.concatenate(tables, 1))
    mine = (iota((128, 128), 1) >> 4) == (column(cols_ref, 1) & 7)
    facts = ghost_ref[32:40, :]
    ghost_mine = (iota((8, 128), 1) >> 4) == (facts[:, 64:65].astype(I32) & 7)
    masked, ghost_masked = [], []
    for a in range(3):
        whole = found[:, 256 * a : 256 * a + 128] + found[:, 256 * a + 128 : 256 * a + 256]
        masked.append(jnp.where(mine, whole[0:128], 0.0))
        ghost_masked.append(jnp.where(ghost_mine, whole[128:136], 0.0))
        masked_ref[128 * a : 128 * a + 128, :] = masked[a]
    rhs = rhs_in_ref[...] - products_sum(products_ref, masked)
    rhs_ref[...] = rhs
    send_normal(rhs, by_source_ref[...], (plain_ref, up_ref, down_ref))
    ghost_att = [ghost_ref[8 * a : 8 * a + 8, :] for a in range(3)]
    ghosts = ghost_ref[24:32, :] - attitude_term(ghost_att, ghost_masked, by_lane_ref)
    up_ref[HEAD : HEAD + 8, :] = ghosts
    down_ref[HEAD : HEAD + 8, :] = ghosts
    core, chip = core_ref[0], chip_ref[0]
    before = jnp.where(core == 0, jnp.maximum(chip - 1, 0), chip)
    after = jnp.where(core == 0, chip, jnp.minimum(chip + 1, CHIPS - 1))
    sides_ref[0:4, :] = far_ref[before, 3]
    sides_ref[4:8, :] = far_ref[after, 3]
    empty = jnp.zeros((4, 128), F32)
    final = jnp.where(core == 1, near_ref[CHIPS - 1, 3], far_ref[CHIPS - 1, 3])
    initial = jnp.where(core == 0, near_ref[0, 3], far_ref[0, 3])
    up_ref[HEAD + 8 : HEAD + 16, :] = jnp.concatenate([final, empty], 0)
    down_ref[HEAD + 8 : HEAD + 16, :] = jnp.concatenate([initial, empty], 0)


def beside_kernel(
    live_ref, masked_ref, resid_in_ref, att_ref, by_lane_ref, by_row_ref, grads_ref, *rest
):
    masked = [masked_ref[128 * a : 128 * a + 128, :] for a in range(3)]
    used = jnp.where(iota((CROSS, 1), 0) < live_ref[0], 1.0, 0.0)
    resid = resid_in_ref[...] - attitude_term(att_ref, masked, by_lane_ref) * used
    grads_ref[...] = gradients(att_ref, resid, by_row_ref)
    for ref in rest:
        ref[...] = resid


def middle_kernel(
    got_ref, resid_ref, rhs_in_ref, cols_ref, peers_ref, by_source_ref, by_lane_ref, choose_ref,
    ghost_ref, products_ref, masked_ref, send_ref,
):
    found = split_dot(peers_ref[...], jnp.concatenate([got_ref[:, 0, :], got_ref[:, 1, :]], 1))
    group = iota((136, 128), 1) >> 4
    cc = jnp.concatenate([column(cols_ref, 3), iota((8, 1), 0) & 3], 0)
    front, back = found[0:136, 0:128], found[0:136, 128:256]
    masked = [
        jnp.where(group == cc, front, 0.0),
        jnp.where(group == cc + 4, front, 0.0),
        jnp.where(group == cc, back, 0.0),
    ]
    for a in range(3):
        masked_ref[128 * a : 128 * a + 128, :] = masked[a][0:128]
    rhs = rhs_in_ref[...] - products_sum(products_ref, [m[0:128] for m in masked])
    send_normal(rhs, by_source_ref[...], (send_ref,))
    ghost_att = [ghost_ref[8 * a : 8 * a + 8, :] for a in range(3)]
    term = attitude_term(ghost_att, [m[128:136] for m in masked], by_lane_ref)
    ghosts = dot(choose_ref[...], jnp.concatenate(halves(resid_ref[...]), 1))
    send_ref[HEAD : HEAD + 8, :] = ghosts[:, 0:128] + ghosts[:, 128:256] - term


def return_kernel(
    live_ref, tm_ref, across_ref, own_ref, below_ref, above_ref, up_ref, down_ref, inverses_ref,
    sources_in_ref, grads_ref, products_ref, cols_ref, by_source_ref, by_row_ref, pack_ref,
    *rest, second,
):
    if second:
        out_ref, sources_ref = rest[:2]
    else:
        index_ref, resid_in_ref, src_ref, normals_ref, rhs_in_ref = rest[:5]
        out_ref, sources_ref, resid_ref, rhs_ref = rest[5:9]
    tm, total_ref = tm_ref[0], rest[-1]
    total_ref[...] = (
        own_ref[0:HEAD, :] + across_ref[0:HEAD, :] + below_ref[0:HEAD, :] + above_ref[0:HEAD, :]
    )
    normal = jnp.concatenate([total_ref[pl.ds(j, 5, stride=8), :] for j in range(8)], 1)
    sub8 = iota((8, SRC_N), 0)
    step = jnp.zeros((8, SRC_N), F32)
    for p in range(5):
        row = jnp.sum(inverses_ref[p] * normal, axis=0, keepdims=True)
        step = jnp.where(sub8 == p, row, step)
    sources_ref[...] = step[0:5] if second else sources_in_ref[...] + step[0:5]
    ghost8 = iota((8, 128), 0)
    there = jnp.where(ghost8 < 4, jnp.where(tm > 0, 1.0, 0.0), jnp.where(tm < TM_N - 1, 1.0, 0.0))

    def item(i):
        row = 4 * i
        return jnp.concatenate([up_ref[row : row + 4, :], down_ref[row : row + 4, :]], 0)

    facts = item(9)
    ghost_slot = facts[:, 0:1].astype(I32)
    ghost_block = facts[:, 64:65].astype(I32)
    ghost_onehot = jnp.where(iota((8, SRC_N), 1) == ghost_slot, 1.0, 0.0)
    values = gather_source(step, by_source_ref[...])
    ghost_values = gather_source(step, ghost_onehot)
    ghost_change = jnp.zeros((8, ROWS), F32)
    for p in range(5):
        ghost_change = ghost_change + item(3 + p) * ghost_values[p]
    ghost_resid = jnp.concatenate(
        [below_ref[HEAD : HEAD + 4, :], above_ref[HEAD + 4 : HEAD + 8, :]], 0
    )
    if not second:
        used = jnp.where(iota((CROSS, 1), 0) < live_ref[0], 1.0, 0.0)
        change = jnp.zeros((CROSS, ROWS), F32)
        rhs = rhs_in_ref[...]
        for p in range(5):
            change = change + src_ref[p].astype(F32) * values[p]
            rhs = rhs - normals_ref[128 * p : 128 * p + 128, :] * values[p]
        resid_ref[...] = resid_in_ref[...] - used * change
        rhs_ref[...] = rhs
    ghost_resid = (ghost_resid - ghost_change) * there
    ghost_grads = gradients([item(a) for a in range(3)], ghost_resid, by_row_ref)
    parts = []
    for a in range(3):
        part = grads_ref[128 * a : 128 * a + 128, :]
        for p in range(5):
            low_row = 128 * (3 * p + a)
            part = part - products_ref[low_row : low_row + 128, :] * values[p]
        parts.append(part)
    lbc, cc = column(cols_ref, 1), column(cols_ref, 3)
    group = iota((128, 128), 1) >> 4
    edge_group = jnp.where(lbc <= 1, lbc, lbc - 24)
    own = group == cc + 2
    edge = group == edge_group
    high, low = halves(jnp.concatenate(parts, 1))
    own3, edge3 = jnp.concatenate([own] * 3, 1), jnp.concatenate([edge] * 3, 1)
    none = jnp.zeros_like(high)
    table = [jnp.where(mask, part, none) for part in (high, low) for mask in (own3, edge3)]
    packed = dot(pack_ref[...], jnp.concatenate(table, 0))
    peer = iota((SKY_N, 128), 0)
    ghost_group = iota((8, 128), 1) >> 4
    ghost_own = ghost_group == jnp.where(ghost8[:, 0:1] < 4, ghost_block - 24, ghost_block)
    for a in range(3):
        ghost = jnp.where(ghost_own, ghost_grads[8 * a : 8 * a + 8], 0.0)
        from_below = jnp.sum(jnp.where(ghost8 < 4, ghost, 0.0), axis=0, keepdims=True)
        from_above = jnp.sum(jnp.where(ghost8 >= 4, ghost, 0.0), axis=0, keepdims=True)
        block = packed[:, 128 * a : 128 * a + 128]
        block = block + jnp.where(peer == 0, from_below, 0.0)
        block = block + jnp.where(peer == SKY_N - 1, from_above, 0.0)
        if second:
            out_ref[:, 0, 128 * a : 128 * a + 128] = block
        else:
            out_ref[:, a, :] = block
    if not second:
        out_ref[:, 3, :] = index_ref[...]


def smooth_kernel(
    offsets_ref, chip_ref, core_ref, tm_ref, got_ref, knots_in_ref, wide_ref, one_ref, two_ref,
    three_ref, four_ref, *outs, last,
):
    knots_ref = outs[0]
    lane = iota((SKY_N, 128), 1)
    if last:
        sources_in_ref, step_ref, pick_ref, rims_ref = one_ref, two_ref, three_ref, four_ref
        pick = pick_ref[...]
        rims = [rims_ref[8 * i : 8 * i + 8, :] for i in range(4)]
    else:
        sides_ref, up_ref, down_ref = one_ref, two_ref, three_ref
        place, tm = chip_ref[0] * 2 + core_ref[0], tm_ref[0]
        below = jnp.where(tm > 0, up_ref[HEAD + 8 : HEAD + 12, :], 0.0)
        above = jnp.where(tm < TM_N - 1, down_ref[HEAD + 8 : HEAD + 12, :], 0.0)
        before = jnp.where(place == 0, below, sides_ref[0:4, :])
        after = jnp.where(place == SKY_N - 1, above, sides_ref[4:8, :])
        rims = rim_tiles(before, after)
        for i in range(4):
            outs[3][8 * i : 8 * i + 8, :] = rims[i]
        index = got_ref[:, 3, :]
        square = jnp.concatenate([index, index], 0).T
        block32 = (iota((32, 128), 0) + 1).astype(F32)
        pick = jnp.concatenate(
            [
                jnp.where(square[16 * (2 + c) : 16 * (2 + c) + 1, :] == block32, 1.0, 0.0)
                for c in range(4)
            ],
            0,
        ).astype(BF16)
        outs[2][...] = pick
    got = [got_ref[:, 0, 128 * a : 128 * a + 128] if last else got_ref[:, a, :] for a in range(3)]
    summed = split_dot(pick, jnp.concatenate(got, 1))
    row128 = iota((128, 128), 0)
    group128 = iota((128, 128), 1) >> 4
    keep = group128 == (row128 >> 5) + 2
    fold = fold_table()
    stack = []
    for a in range(3):
        one = jnp.where(keep, summed[:, 128 * a : 128 * a + 128], 0.0)
        stack.append(one[0:32] + one[32:64] + one[64:96] + one[96:128])
    high, low = halves(jnp.concatenate(stack, 0))
    spread = dot(jnp.concatenate([high, low], 1), jnp.concatenate([fold, fold], 0))
    in_row = (iota((8, 128), 1) >> 4) == iota((8, 128), 0)
    sub8, lane8 = iota((8, 128), 0), iota((8, 128), 1)
    grad = [jnp.zeros((8, 128), F32)] * 5
    for a in range(3):
        for r in range(5):
            if r < 4:
                piece = jnp.where(in_row, spread[32 * a + 8 * r : 32 * a + 8 * r + 8], 0.0)
            else:
                piece = jnp.where((lane < 32) | (lane >= 96), got[a], 0.0)
            grad[r] = jnp.where(sub8 == a, jnp.sum(piece, axis=0, keepdims=True), grad[r])
    bands, scale = [], None
    for i in range(4):
        tiles = [wide_ref[8 * i : 8 * i + 8, 128 * r : 128 * r + 128] for r in range(4)]
        if i < 3:
            bands.append([*tiles, rims[i]])
        else:
            scale = [*tiles, rims[i]]
    offsets = [offsets_ref[b] for b in range(3)]
    wraps = [(lane8 < offset, lane8 >= 128 - offset) for offset in offsets]
    delta = [g * f for g, f in zip(grad, scale, strict=True)]
    for _ in range(2):
        total = grad
        for b in range(3):
            low = [pltpu.roll(d, offsets[b], 1) for d in delta]
            high = [pltpu.roll(d, 128 - offsets[b], 1) for d in delta]
            first, final = wraps[b]
            total = [
                total[r]
                + bands[b][r]
                * (
                    jnp.where(first, low[(r + 4) % 5], low[r])
                    + jnp.where(final, high[(r + 1) % 5], high[r])
                )
                for r in range(5)
            ]
        delta = [t * f for t, f in zip(total, scale, strict=True)]
    for a in range(3):
        for r in range(4):
            tile = delta[r][a : a + 1]
            knots_ref[a, r : r + 1, :] = knots_in_ref[a, r : r + 1, :] + tile
    if last:
        outs[1][...] = sources_in_ref[...] + step_ref[...]
        return
    send_ref = outs[1]
    spreads = []
    for a in range(3):
        for r in range(4):
            tile = delta[r][a : a + 1]
            spreads.append(jnp.where(in_row, tile, 0.0))
    high, low = halves(jnp.concatenate(spreads, 0))
    blocks = dot(jnp.concatenate([high, low], 1), jnp.concatenate([fold, fold], 0))
    table = jnp.concatenate([blocks[32 * a : 32 * a + 32] for a in range(3)], 1)
    slots = [index[:, 16 * (2 + c) : 16 * (2 + c) + 1].astype(I32) - 1 for c in range(4)]
    slot = jnp.concatenate(slots, 0)
    by_block = jnp.where((iota((4 * SKY_N, 64), 1) & 31) == slot, 1.0, 0.0)
    found = split_dot(by_block, table)
    group = lane >> 4
    front = jnp.zeros((SKY_N, 128), F32)
    back = jnp.zeros((SKY_N, 128), F32)
    for c in range(4):
        rows = found[SKY_N * c : SKY_N * (c + 1)]
        part = [rows[:, 128 * a : 128 * a + 128] for a in range(3)]
        front = jnp.where(group == c, part[0], jnp.where(group == c + 4, part[1], front))
        back = jnp.where(group == c, part[2], back)
    send_ref[:, 0, :] = front
    send_ref[:, 1, :] = back


def run_kernel(body, scalars, outs, *args, scratch=(), flops=10_000_000, **static):
    specs = [
        pl.BlockSpec(memory_space=pltpu.SMEM if i < scalars else pltpu.VMEM)
        for i in range(len(args))
    ]
    shapes = [o if isinstance(o, jax.ShapeDtypeStruct) else jax.ShapeDtypeStruct(o, F32) for o in outs]

    def kernel(*refs):
        body(*refs, **static)

    return pl.pallas_call(
        kernel,
        out_shape=shapes,
        in_specs=specs,
        out_specs=[
            pl.BlockSpec(memory_space=pltpu.SMEM if s.dtype == I32 else pltpu.VMEM) for s in shapes
        ],
        scratch_shapes=[pltpu.VMEM(shape, F32) for shape in scratch],
        cost_estimate=pl.CostEstimate(flops=flops, bytes_accessed=2_000_000, transcendentals=0),
        compiler_params=pltpu.CompilerParams(vmem_limit_bytes=32 * 1024 * 1024),
    )(*args)


def half(*shape):
    return jax.ShapeDtypeStruct(shape, BF16)


def shifts(k):
    return [(i, (i + k) % TM_N) for i in range(TM_N)]


def per_device(
    observed,
    att_partials,
    src_partials,
    src_slot,
    knot_block,
    live_count,
    sources,
    inverses,
    attitude,
    band_coef,
    extra_diag,
    band_offsets,
):
    core = lax.axis_index("c").astype(I32).reshape(1)
    tm = lax.axis_index("tm").astype(I32).reshape(1)
    slot = src_slot.reshape(1, CROSS)
    kb = knot_block.reshape(1, CROSS)
    chip = lax.axis_index(("x", "z")).astype(I32).reshape(1)
    knots = attitude.reshape(3, 4, 128)
    bands = band_coef.reshape(3, 3, 4, 128)
    extra = extra_diag.reshape(3, 4, 128)

    dense = pl.pallas_call(
        payload_kernel,
        out_shape=jax.ShapeDtypeStruct((CHIPS, 4, 4, 128), F32),
        in_specs=[pl.BlockSpec(memory_space=pl.ANY)] * 3,
        out_specs=pl.BlockSpec(memory_space=pltpu.VMEM),
        scratch_shapes=[
            pltpu.VMEM((3, 4, 128), F32),
            pltpu.VMEM((3, 3, 4, 128), F32),
            pltpu.VMEM((3, 4, 128), F32),
            pltpu.SemaphoreType.DMA((3,)),
        ],
        compiler_params=pltpu.CompilerParams(vmem_limit_bytes=56 * 1024 * 1024),
    )(knots, bands, extra)
    near = lax.all_to_all(dense, ("x", "z"), 0, 0, tiled=True)
    (
        cols, places, by_source, base, by_lane, by_row, pack, index, peers, choose, up, down, wide,
        ghost, products, normals, rhs, held, offsets,
    ) = run_kernel(
        prepare_kernel, 3,
        [
            (128, 128), half(144, 256), half(128, SRC_N), (CROSS, ROWS), half(384, 128),
            half(384, 128), half(SKY_N, 512), (SKY_N, 128), half(144, 128), (8, 128), (40, 128),
            (40, 128), (32, RUN), (40, 128), (1920, 128), (640, 128), (128, 128),
            (3, 4, 128), jax.ShapeDtypeStruct((3,), I32),
        ],
        live_count, core, band_offsets, observed, att_partials, src_partials, slot, kb, sources, bands, extra,
        knots,
    )
    ghosts_below = lax.ppermute(up, "tm", shifts(1))
    ghosts_above = lax.ppermute(down, "tm", shifts(-1))
    near, cols, ghosts_below, ghosts_above = lax.optimization_barrier(
        (near, cols, ghosts_below, ghosts_above)
    )
    far = lax.ppermute(near, "c", [(0, 1), (1, 0)])
    masked, rhs, plain, up, down, sides = run_kernel(
        first_kernel, 2,
        [(384, 128), (128, 128), (HEAD, 128), (HEAD + 16, 128), (HEAD + 16, 128), (8, 128)],
        core, chip, near, far, cols, places, by_source, by_lane, ghost, products, rhs,
    )
    across = lax.ppermute(plain, "tm", shifts(2))
    up = lax.ppermute(up, "tm", shifts(1))
    down = lax.ppermute(down, "tm", shifts(-1))
    grads, resid = run_kernel(
        beside_kernel, 1, [(384, 128), (CROSS, ROWS)],
        live_count, masked, base, att_partials, by_lane, by_row,
    )
    outgoing, sources, resid, rhs = run_kernel(
        return_kernel, 2, [(SKY_N, 4, 128), (5, SRC_N), (CROSS, ROWS), (128, 128)],
        live_count, tm, across, plain, up, down, ghosts_below, ghosts_above, inverses, sources, grads, products,
        cols, by_source, by_row, pack, index, resid, src_partials, normals, rhs,
        scratch=[(HEAD, 128)], second=False,
    )
    got = lax.all_to_all(outgoing, SKY, 0, 0, tiled=True)
    knots, served, pick, rims = run_kernel(
        smooth_kernel, 4, [(3, 4, 128), (SKY_N, 2, 128), half(128, 128), (32, 128)],
        offsets, chip, core, tm, got, held, wide, sides, up, down, choose, last=False,
    )
    arrived = lax.all_to_all(served, SKY, 0, 0, tiled=True)
    masked, mine = run_kernel(
        middle_kernel, 0, [(384, 128), (HEAD + 8, 128)],
        arrived, resid, rhs, cols, peers, by_source, by_lane, choose, ghost, products,
    )
    across = lax.ppermute(mine, "tm", shifts(2))
    below = lax.ppermute(mine, "tm", shifts(1))
    above = lax.ppermute(mine, "tm", shifts(-1))
    (grads,) = run_kernel(
        beside_kernel, 1, [(384, 128)],
        live_count, masked, resid, att_partials, by_lane, by_row,
    )
    outgoing, step = run_kernel(
        return_kernel, 2, [(SKY_N, 1, 384), (5, SRC_N)],
        live_count, tm, across, mine, below, above, ghosts_below, ghosts_above, inverses, sources, grads, products,
        cols, by_source, by_row, pack, scratch=[(HEAD, 128)], second=True,
    )
    got = lax.all_to_all(outgoing, SKY, 0, 0, tiled=True)
    knots, sources = run_kernel(
        smooth_kernel, 4, [(3, 4, 128), (5, SRC_N)],
        offsets, chip, core, tm, got, knots, wide, sources, step, pick, rims, last=True,
    )
    return (sources, knots.reshape(3, 1, RUN))


def solution(mesh):
    torus = Mesh(mesh.devices.reshape(4, 8, 2, mesh.shape["tm"]), SKY_TM)
    return jax.shard_map(
        per_device,
        mesh=torus,
        in_specs=(
            P(SKY_TM, None),
            P(None, SKY_TM, None),
            P(None, SKY_TM, None),
            P(SKY_TM),
            P(SKY_TM),
            P(SKY_TM),
            P(None, SKY),
            P(None, None, SKY),
            P(None, "tm", SKY),
            P(None, None, "tm", SKY),
            P(None, "tm", SKY),
            P(),
        ),
        out_specs=(P(None, SKY), P(None, "tm", SKY)),
        check_vma=False,
    )
```

```python
import jax
import jax.numpy as jnp
from jax import lax
from jax.experimental import pallas as pl
from jax.experimental.pallas import tpu as pltpu
from jax.sharding import Mesh
from jax.sharding import PartitionSpec as P

F32 = jnp.float32
BF16 = jnp.bfloat16
I32 = jnp.int32
ROWS = 128
KNOTS = 16
CROSS = 128
SKY_N = 64
CHIPS = 32
TM_N = 4
SRC_N = 1024
RUN = 512
HEAD = 40
SKY = ("x", "z", "c")
SKY_TM = ("x", "z", "c", "tm")


def iota(shape, dim):
    return lax.broadcasted_iota(I32, shape, dim)


def dot(a, b):
    return jnp.dot(a.astype(BF16), b.astype(BF16), preferred_element_type=F32)


def dot_nt(a, b):
    return lax.dot_general(
        a.astype(BF16), b.astype(BF16), (((1,), (1,)), ((), ())), preferred_element_type=F32
    )


def halves(x):
    high = x.astype(BF16)
    return high, (x - high.astype(F32)).astype(BF16)


def split_dot(twice, values):
    return dot(twice, jnp.concatenate(halves(values), 0))


def thirds(x):
    high = x.astype(BF16).astype(F32)
    rest = x - high
    middle = rest.astype(BF16).astype(F32)
    return high, middle, rest - middle


def b_spline(moment_row, knot):
    tau = 1.5 + (KNOTS - 3) * (moment_row.astype(F32) + 0.5) / ROWS
    dist = jnp.abs(tau - knot.astype(F32))
    inner = 2.0 / 3.0 - dist * dist + 0.5 * dist * dist * dist
    rest = 2.0 - dist
    outer = rest * rest * rest / 6.0
    return jnp.where(dist < 1.0, inner, jnp.where(dist < 2.0, outer, 0.0))


def spline_by_lane():
    return b_spline(iota((128, 128), 1), iota((128, 128), 0) & 15)


def spline_by_row():
    return b_spline(iota((128, 128), 0), iota((128, 128), 1) & 15)


def fold_table():
    return jnp.where((iota((128, 128), 0) & 15) == (iota((128, 128), 1) & 15), 1.0, 0.0)


def table_of(table):
    return table if isinstance(table, jax.Array) else table[...]


def attitude_term(att, masked, table_ref):
    count = masked[0].shape[0]
    high, low = halves(jnp.concatenate(masked, 0))
    spread = dot(jnp.concatenate([high, low, high], 1), table_of(table_ref))
    return sum(att[a].astype(F32) * spread[a * count : (a + 1) * count] for a in range(3))


def products_sum(products_ref, masked):
    lane = iota((128, 128), 1)
    square = jnp.zeros((128, 128), F32)
    for p in range(5):
        terms = [
            products_ref[128 * (3 * p + a) : 128 * (3 * p + a) + 128, :] * masked[a]
            for a in range(3)
        ]
        row = jnp.sum(terms[0] + terms[1] + terms[2], axis=1, keepdims=True)
        square = jnp.where(lane == p, row, square)
    return square


def send_normal(rhs, onehot, refs):
    rows = rhs.T[0:8]
    parts = dot(jnp.concatenate(thirds(rows), 0), onehot)
    normal = parts[0:8] + parts[8:16] + parts[16:24]
    for ref in refs:
        for j in range(8):
            ref[pl.ds(j, 5, stride=8), :] = normal[0:5, 128 * j : 128 * j + 128]


def gradients(att, resid, table_ref):
    high, low = halves(jnp.concatenate([att[a].astype(F32) * resid for a in range(3)], 0))
    return dot(jnp.concatenate([high, low, high], 1), table_of(table_ref))


def gather_source(values8, onehot):
    parts = dot_nt(onehot, jnp.concatenate(thirds(values8), 0))
    return [
        parts[:, p : p + 1] + parts[:, 8 + p : 9 + p] + parts[:, 16 + p : 17 + p] for p in range(5)
    ]


def padded_rows(x):
    return jnp.concatenate([x, jnp.zeros((8 - x.shape[0], x.shape[1]), F32)], 0)


def column(cols_ref, i):
    return cols_ref[:, i : i + 1].astype(I32)


def stacked_spline(table):
    high, low = halves(table)
    return jnp.concatenate([high, high, low], 0)


def prepare_kernel(
    live_ref, core_ref, offsets_in_ref, obs_ref, att_ref, src_ref, slot_ref, kb_ref, sources_ref,
    bands_ref, extra_ref, knots_in_ref,
    cols_ref, places_ref, by_source_ref, base_ref, by_lane_ref, by_row_ref, pack_ref, index_ref,
    peers_ref, choose_ref, up_ref, down_ref, wide_ref, ghost_ref, products_ref, normals_ref, rhs_ref,
    knots_ref, offsets_ref,
):
    live, core = live_ref[0], core_ref[0]
    knots_ref[...] = knots_in_ref[...]
    for b in range(3):
        offsets_ref[b] = offsets_in_ref[b]
    kb, slot = kb_ref[...], slot_ref[...]
    h, lb = kb >> 5, kb & 31
    sub, lane = iota((128, 128), 0), iota((128, 128), 1)
    square = jnp.zeros((128, 128), F32)
    for i, row in enumerate((h, lb, slot)):
        square = jnp.where(sub == i, row.astype(F32), square)
    turned = square.T
    hc, lbc, slotc = (turned[:, i : i + 1].astype(I32) for i in range(3))
    same = hc == h
    c = jnp.sum(jnp.where(same & (sub < lane), 1.0, 0.0), axis=0, keepdims=True).astype(I32)
    cc = jnp.sum(jnp.where(same & (lane < sub), 1.0, 0.0), axis=1, keepdims=True)
    cols_ref[...] = jnp.where(lane == 3, cc, turned)
    cc = cc.astype(I32)
    group = lane >> 4

    place = (lbc >> 3) * CHIPS + (hc >> 1) + jnp.where((hc & 1) == core, 0, 128)
    places = jnp.where(iota((128, 256), 1) == place, 1.0, 0.0)
    by_source = jnp.where(iota((128, SRC_N), 1) == slotc, 1.0, 0.0).astype(BF16)
    by_source_ref[...] = by_source
    values = gather_source(padded_rows(sources_ref[...]), by_source)
    src_term = jnp.zeros((CROSS, ROWS), F32)
    for p in range(5):
        src_term = src_term + src_ref[p].astype(F32) * values[p]
    used = jnp.where(iota((CROSS, 1), 0) < live, 1.0, 0.0)
    base = (obs_ref[...] - src_term) * used
    base_ref[...] = base
    by_row = stacked_spline(spline_by_row())
    rhs = jnp.zeros((128, 128), F32)
    normals = [jnp.zeros((128, 128), F32)] * 5
    for p in range(5):
        one = src_ref[p].astype(F32) * used
        rhs = jnp.where(lane == p, jnp.sum(one * base, axis=1, keepdims=True), rhs)
        products_ref[384 * p : 384 * p + 384, :] = gradients(att_ref, one, by_row)
        for q in range(p + 1):
            both = jnp.sum(one * src_ref[q].astype(F32), axis=1, keepdims=True)
            normals[q] = jnp.where(lane == p, both, normals[q])
            normals[p] = jnp.where(lane == q, both, normals[p])
    rhs_ref[...] = rhs
    for q in range(5):
        normals_ref[128 * q : 128 * q + 128, :] = normals[q]
    by_lane_ref[...] = stacked_spline(spline_by_lane())
    by_row_ref[...] = by_row

    peer = iota((SKY_N, 128), 0)
    to_row = jnp.where(lb <= 1, h - 1, jnp.where(lb >= 30, h + 1, jnp.full_like(h, -1)))
    own = jnp.where(peer == h, 1.0, 0.0)
    edge = jnp.where(peer == to_row, 1.0, 0.0)
    pack_ref[...] = jnp.concatenate([own, edge, own, edge], 1).astype(BF16)
    index_ref[...] = dot(own, jnp.where(group == cc + 2, (lbc + 1).astype(F32), 0.0))
    peers = jnp.where((iota((128, 128), 1) & 63) == hc, 1.0, 0.0)

    sub8 = iota((8, 128), 0)
    after = (h == SKY_N - 1) & (lb >= 30) & (sub8 < 4)
    before = (h == 0) & (lb <= 1) & (sub8 >= 4)
    chosen = (c == (sub8 & 3)) & (after | before) & (iota((8, 128), 1) < live)
    choose = jnp.where(chosen, 1.0, 0.0)
    choose_ref[...] = choose
    pieces = [att_ref[a] for a in range(3)] + [src_ref[p] for p in range(5)]
    pieces += [*halves(base), places.astype(BF16), peers.astype(BF16)]
    ghosts = dot(choose, jnp.concatenate(pieces, 1))
    items = [ghosts[:, 128 * i : 128 * i + 128] for i in range(8)]
    empty = jnp.zeros((8, 256), F32)
    places_ref[...] = jnp.concatenate([places, ghosts[:, 1280:1536], empty], 0).astype(BF16)
    peers_ref[...] = jnp.concatenate([peers, ghosts[:, 1536:1664], empty[:, 0:128]], 0).astype(BF16)
    ghost_slot = jnp.sum(choose * slot.astype(F32), axis=1, keepdims=True)
    ghost_block = jnp.sum(choose * lb.astype(F32), axis=1, keepdims=True)
    items.append(jnp.zeros((8, 128), F32))
    items.append(jnp.where(iota((8, 128), 1) < 64, ghost_slot, ghost_block))
    for a in range(3):
        ghost_ref[8 * a : 8 * a + 8, :] = items[a]
    ghost_ref[24:32, :] = ghosts[:, 1024:1152] + ghosts[:, 1152:1280]
    ghost_ref[32:40, :] = items[9]
    for q in range(5):
        even, odd = items[2 * q], items[2 * q + 1]
        up_ref[8 * q : 8 * q + 8, :] = jnp.concatenate([even[0:4], odd[0:4]], 0)
        down_ref[8 * q : 8 * q + 8, :] = jnp.concatenate([even[4:8], odd[4:8]], 0)

    bands = [axis_rows(bands_ref[b]) for b in range(3)]
    diag = axis_rows(extra_ref) + 2.0 * (bands[0] + bands[1] + bands[2])
    for b in range(3):
        wide_ref[8 * b : 8 * b + 8, :] = bands[b]
    wide_ref[24:32, :] = 1.0 / jnp.where(diag > 0.0, diag, 1.0)


def axis_rows(tiles):
    sub = iota((8, RUN), 0)
    out = jnp.zeros((8, RUN), F32)
    for a in range(3):
        out = jnp.where(sub == a, jnp.concatenate([tiles[a][r : r + 1] for r in range(4)], 1), out)
    return out


def payload_kernel(knots_hbm, bands_hbm, extra_hbm, out_ref, knots_ref, bands_ref, extra_ref, sems):
    copies = [
        pltpu.make_async_copy(source, target, sems.at[i])
        for i, (source, target) in enumerate(
            ((knots_hbm, knots_ref), (bands_hbm, bands_ref), (extra_hbm, extra_ref))
        )
    ]
    for copy in copies:
        copy.start()
    copies[0].wait()
    for chip in range(CHIPS):
        out_ref[chip, 0:3] = knots_ref[...]
    for copy in copies[1:]:
        copy.wait()
    lane = iota((1, 128), 1)

    def ends(tiles, width):
        low, high = tiles[0:1], tiles[3:4]
        return jnp.where(lane < width, low, jnp.where(lane >= 128 - width, high, 0.0))

    rows = []
    for a in range(3):
        bands = [bands_ref[b, a] for b in range(3)]
        diag = extra_ref[a] + 2.0 * (bands[0] + bands[1] + bands[2])
        row = ends(diag, 32) + pltpu.roll(ends(bands[0], 16), 48, 1)
        rows.append(row + pltpu.roll(ends(bands[1], 16), 80, 1))
    third = [ends(bands_ref[2, a], 16) for a in range(3)]
    rows.append(third[0] + pltpu.roll(third[1], 48, 1) + pltpu.roll(third[2], 80, 1))
    sub = iota((4, 128), 0)
    edge = jnp.zeros((4, 128), F32)
    for i, row in enumerate(rows):
        edge = jnp.where(sub == i, row, edge)
    for chip in range(CHIPS):
        out_ref[chip, 3] = edge


def rim_tiles(before, after):
    sub, lane = iota((8, 128), 0), iota((8, 128), 1)

    def tile(sources, width):
        out = jnp.zeros((8, 128), F32)
        for a, (row, turn) in enumerate(sources):
            both = [e[row : row + 1] for e in (after, before)]
            if turn:
                both = [pltpu.roll(e, 128 - turn, 1) for e in both]
            one = jnp.where(lane < width, both[0], jnp.where(lane >= 128 - width, both[1], 0.0))
            out = jnp.where(sub == a, one, out)
        return out

    bands = [
        tile([(a, 48) for a in range(3)], 16),
        tile([(a, 80) for a in range(3)], 16),
        tile([(3, 0), (3, 48), (3, 80)], 16),
    ]
    diag = tile([(a, 0) for a in range(3)], 32)
    return bands + [1.0 / jnp.where(diag > 0.0, diag, 1.0)]


def first_kernel(
    core_ref, chip_ref, near_ref, far_ref, cols_ref, places_ref, by_source_ref, by_lane_ref,
    up_in_ref, down_in_ref, ghost_ref, products_ref, rhs_in_ref,
    masked_ref, rhs_ref, plain_ref, up_ref, down_ref, sides_ref,
):
    tables = []
    for a in range(3):
        rows = [ref[:, a, r, :] for ref in (near_ref, far_ref) for r in range(4)]
        tables += halves(jnp.concatenate(rows, 0))
    found = dot(places_ref[...], jnp.concatenate(tables, 1))
    mine = (iota((128, 128), 1) >> 4) == (column(cols_ref, 1) & 7)
    facts = ghost_ref[32:40, :]
    ghost_mine = (iota((8, 128), 1) >> 4) == (facts[:, 64:65].astype(I32) & 7)
    masked, ghost_masked = [], []
    for a in range(3):
        whole = found[:, 256 * a : 256 * a + 128] + found[:, 256 * a + 128 : 256 * a + 256]
        masked.append(jnp.where(mine, whole[0:128], 0.0))
        ghost_masked.append(jnp.where(ghost_mine, whole[128:136], 0.0))
        masked_ref[128 * a : 128 * a + 128, :] = masked[a]
    rhs = rhs_in_ref[...] - products_sum(products_ref, masked)
    rhs_ref[...] = rhs
    send_normal(rhs, by_source_ref[...], (plain_ref, up_ref, down_ref))
    ghost_att = [ghost_ref[8 * a : 8 * a + 8, :] for a in range(3)]
    ghosts = ghost_ref[24:32, :] - attitude_term(ghost_att, ghost_masked, by_lane_ref)
    up_ref[HEAD : HEAD + 40, :] = up_in_ref[...]
    down_ref[HEAD : HEAD + 40, :] = down_in_ref[...]
    up_ref[HEAD + 32 : HEAD + 36, :] = ghosts[0:4]
    down_ref[HEAD + 32 : HEAD + 36, :] = ghosts[4:8]
    core, chip = core_ref[0], chip_ref[0]
    before = jnp.where(core == 0, jnp.maximum(chip - 1, 0), chip)
    after = jnp.where(core == 0, chip, jnp.minimum(chip + 1, CHIPS - 1))
    sides_ref[0:4, :] = far_ref[before, 3]
    sides_ref[4:8, :] = far_ref[after, 3]
    empty = jnp.zeros((4, 128), F32)
    final = jnp.where(core == 1, near_ref[CHIPS - 1, 3], far_ref[CHIPS - 1, 3])
    initial = jnp.where(core == 0, near_ref[0, 3], far_ref[0, 3])
    up_ref[HEAD + 40 : HEAD + 48, :] = jnp.concatenate([final, empty], 0)
    down_ref[HEAD + 40 : HEAD + 48, :] = jnp.concatenate([initial, empty], 0)


def beside_kernel(
    live_ref, masked_ref, resid_in_ref, att_ref, by_lane_ref, by_row_ref, grads_ref, *rest
):
    masked = [masked_ref[128 * a : 128 * a + 128, :] for a in range(3)]
    used = jnp.where(iota((CROSS, 1), 0) < live_ref[0], 1.0, 0.0)
    resid = resid_in_ref[...] - attitude_term(att_ref, masked, by_lane_ref) * used
    grads_ref[...] = gradients(att_ref, resid, by_row_ref)
    for ref in rest:
        ref[...] = resid


def middle_kernel(
    got_ref, resid_ref, rhs_in_ref, cols_ref, peers_ref, by_source_ref, by_lane_ref, choose_ref,
    ghost_ref, products_ref, masked_ref, send_ref,
):
    found = split_dot(peers_ref[...], jnp.concatenate([got_ref[:, 0, :], got_ref[:, 1, :]], 1))
    group = iota((136, 128), 1) >> 4
    cc = jnp.concatenate([column(cols_ref, 3), iota((8, 1), 0) & 3], 0)
    front, back = found[0:136, 0:128], found[0:136, 128:256]
    masked = [
        jnp.where(group == cc, front, 0.0),
        jnp.where(group == cc + 4, front, 0.0),
        jnp.where(group == cc, back, 0.0),
    ]
    for a in range(3):
        masked_ref[128 * a : 128 * a + 128, :] = masked[a][0:128]
    rhs = rhs_in_ref[...] - products_sum(products_ref, [m[0:128] for m in masked])
    send_normal(rhs, by_source_ref[...], (send_ref,))
    ghost_att = [ghost_ref[8 * a : 8 * a + 8, :] for a in range(3)]
    term = attitude_term(ghost_att, [m[128:136] for m in masked], by_lane_ref)
    ghosts = dot(choose_ref[...], jnp.concatenate(halves(resid_ref[...]), 1))
    send_ref[HEAD : HEAD + 8, :] = ghosts[:, 0:128] + ghosts[:, 128:256] - term


def return_kernel(
    live_ref, tm_ref, across_ref, own_ref, below_ref, above_ref, up_ref, down_ref, inverses_ref,
    sources_in_ref, grads_ref, products_ref, cols_ref, by_source_ref, by_row_ref, pack_ref,
    *rest, second,
):
    if second:
        out_ref, sources_ref = rest[:2]
    else:
        index_ref, resid_in_ref, src_ref, normals_ref, rhs_in_ref = rest[:5]
        out_ref, sources_ref, resid_ref, rhs_ref = rest[5:9]
    tm, total_ref = tm_ref[0], rest[-1]
    total_ref[...] = (
        own_ref[0:HEAD, :] + across_ref[0:HEAD, :] + below_ref[0:HEAD, :] + above_ref[0:HEAD, :]
    )
    normal = jnp.concatenate([total_ref[pl.ds(j, 5, stride=8), :] for j in range(8)], 1)
    sub8 = iota((8, SRC_N), 0)
    step = jnp.zeros((8, SRC_N), F32)
    for p in range(5):
        row = jnp.sum(inverses_ref[p] * normal, axis=0, keepdims=True)
        step = jnp.where(sub8 == p, row, step)
    sources_ref[...] = step[0:5] if second else sources_in_ref[...] + step[0:5]
    ghost8 = iota((8, 128), 0)
    there = jnp.where(ghost8 < 4, jnp.where(tm > 0, 1.0, 0.0), jnp.where(tm < TM_N - 1, 1.0, 0.0))

    def item(i):
        row = HEAD + 4 * i
        return jnp.concatenate([up_ref[row : row + 4, :], down_ref[row : row + 4, :]], 0)

    facts = item(9)
    ghost_slot = facts[:, 0:1].astype(I32)
    ghost_block = facts[:, 64:65].astype(I32)
    ghost_onehot = jnp.where(iota((8, SRC_N), 1) == ghost_slot, 1.0, 0.0)
    values = gather_source(step, by_source_ref[...])
    ghost_values = gather_source(step, ghost_onehot)
    ghost_change = jnp.zeros((8, ROWS), F32)
    for p in range(5):
        ghost_change = ghost_change + item(3 + p) * ghost_values[p]
    if second:
        ghost_resid = jnp.concatenate(
            [below_ref[HEAD : HEAD + 4, :], above_ref[HEAD + 4 : HEAD + 8, :]], 0
        )
    else:
        ghost_resid = item(8)
        used = jnp.where(iota((CROSS, 1), 0) < live_ref[0], 1.0, 0.0)
        change = jnp.zeros((CROSS, ROWS), F32)
        rhs = rhs_in_ref[...]
        for p in range(5):
            change = change + src_ref[p].astype(F32) * values[p]
            rhs = rhs - normals_ref[128 * p : 128 * p + 128, :] * values[p]
        resid_ref[...] = resid_in_ref[...] - used * change
        rhs_ref[...] = rhs
    ghost_resid = (ghost_resid - ghost_change) * there
    ghost_grads = gradients([item(a) for a in range(3)], ghost_resid, by_row_ref)
    parts = []
    for a in range(3):
        part = grads_ref[128 * a : 128 * a + 128, :]
        for p in range(5):
            low_row = 128 * (3 * p + a)
            part = part - products_ref[low_row : low_row + 128, :] * values[p]
        parts.append(part)
    lbc, cc = column(cols_ref, 1), column(cols_ref, 3)
    group = iota((128, 128), 1) >> 4
    edge_group = jnp.where(lbc <= 1, lbc, lbc - 24)
    own = group == cc + 2
    edge = group == edge_group
    high, low = halves(jnp.concatenate(parts, 1))
    own3, edge3 = jnp.concatenate([own] * 3, 1), jnp.concatenate([edge] * 3, 1)
    none = jnp.zeros_like(high)
    table = [jnp.where(mask, part, none) for part in (high, low) for mask in (own3, edge3)]
    packed = dot(pack_ref[...], jnp.concatenate(table, 0))
    peer = iota((SKY_N, 128), 0)
    ghost_group = iota((8, 128), 1) >> 4
    ghost_own = ghost_group == jnp.where(ghost8[:, 0:1] < 4, ghost_block - 24, ghost_block)
    for a in range(3):
        ghost = jnp.where(ghost_own, ghost_grads[8 * a : 8 * a + 8], 0.0)
        from_below = jnp.sum(jnp.where(ghost8 < 4, ghost, 0.0), axis=0, keepdims=True)
        from_above = jnp.sum(jnp.where(ghost8 >= 4, ghost, 0.0), axis=0, keepdims=True)
        block = packed[:, 128 * a : 128 * a + 128]
        block = block + jnp.where(peer == 0, from_below, 0.0)
        block = block + jnp.where(peer == SKY_N - 1, from_above, 0.0)
        if second:
            out_ref[:, 0, 128 * a : 128 * a + 128] = block
        else:
            out_ref[:, a, :] = block
    if not second:
        out_ref[:, 3, :] = index_ref[...]


def smooth_kernel(
    offsets_ref, chip_ref, core_ref, tm_ref, got_ref, knots_in_ref, wide_ref, one_ref, two_ref,
    three_ref, four_ref, *outs, last,
):
    knots_ref = outs[0]
    lane = iota((SKY_N, 128), 1)
    if last:
        sources_in_ref, step_ref, pick_ref, rims_ref = one_ref, two_ref, three_ref, four_ref
        pick = pick_ref[...]
        rims = [rims_ref[8 * i : 8 * i + 8, :] for i in range(4)]
    else:
        sides_ref, up_ref, down_ref = one_ref, two_ref, three_ref
        place, tm = chip_ref[0] * 2 + core_ref[0], tm_ref[0]
        below = jnp.where(tm > 0, up_ref[HEAD + 40 : HEAD + 44, :], 0.0)
        above = jnp.where(tm < TM_N - 1, down_ref[HEAD + 40 : HEAD + 44, :], 0.0)
        before = jnp.where(place == 0, below, sides_ref[0:4, :])
        after = jnp.where(place == SKY_N - 1, above, sides_ref[4:8, :])
        rims = rim_tiles(before, after)
        for i in range(4):
            outs[3][8 * i : 8 * i + 8, :] = rims[i]
        index = got_ref[:, 3, :]
        square = jnp.concatenate([index, index], 0).T
        block32 = (iota((32, 128), 0) + 1).astype(F32)
        pick = jnp.concatenate(
            [
                jnp.where(square[16 * (2 + c) : 16 * (2 + c) + 1, :] == block32, 1.0, 0.0)
                for c in range(4)
            ],
            0,
        ).astype(BF16)
        outs[2][...] = pick
    got = [got_ref[:, 0, 128 * a : 128 * a + 128] if last else got_ref[:, a, :] for a in range(3)]
    summed = split_dot(pick, jnp.concatenate(got, 1))
    row128 = iota((128, 128), 0)
    group128 = iota((128, 128), 1) >> 4
    keep = group128 == (row128 >> 5) + 2
    fold = fold_table()
    stack = []
    for a in range(3):
        one = jnp.where(keep, summed[:, 128 * a : 128 * a + 128], 0.0)
        stack.append(one[0:32] + one[32:64] + one[64:96] + one[96:128])
    high, low = halves(jnp.concatenate(stack, 0))
    spread = dot(jnp.concatenate([high, low], 1), jnp.concatenate([fold, fold], 0))
    in_row = (iota((8, 128), 1) >> 4) == iota((8, 128), 0)
    sub8, lane8 = iota((8, 128), 0), iota((8, 128), 1)
    grad = [jnp.zeros((8, 128), F32)] * 5
    for a in range(3):
        for r in range(5):
            if r < 4:
                piece = jnp.where(in_row, spread[32 * a + 8 * r : 32 * a + 8 * r + 8], 0.0)
                here = sub8 == a
            else:
                piece = got[a]
                here = (sub8 == a) & ((lane8 < 32) | (lane8 >= 96))
            grad[r] = jnp.where(here, jnp.sum(piece, axis=0, keepdims=True), grad[r])
    bands, scale = [], None
    for i in range(4):
        tiles = [wide_ref[8 * i : 8 * i + 8, 128 * r : 128 * r + 128] for r in range(4)]
        if i < 3:
            bands.append([*tiles, rims[i]])
        else:
            scale = [*tiles, rims[i]]
    offsets = [offsets_ref[b] for b in range(3)]
    wraps = [(lane8 < offset, lane8 >= 128 - offset) for offset in offsets]
    delta = [g * f for g, f in zip(grad, scale, strict=True)]
    for _ in range(2):
        total = grad
        for b in range(3):
            low = [pltpu.roll(d, offsets[b], 1) for d in delta]
            high = [pltpu.roll(d, 128 - offsets[b], 1) for d in delta]
            first, final = wraps[b]
            total = [
                total[r]
                + bands[b][r]
                * (
                    jnp.where(first, low[(r + 4) % 5], low[r])
                    + jnp.where(final, high[(r + 1) % 5], high[r])
                )
                for r in range(5)
            ]
        delta = [t * f for t, f in zip(total, scale, strict=True)]
    for a in range(3):
        for r in range(4):
            tile = delta[r][a : a + 1]
            knots_ref[a, r : r + 1, :] = knots_in_ref[a, r : r + 1, :] + tile
    if last:
        outs[1][...] = sources_in_ref[...] + step_ref[...]
        return
    send_ref = outs[1]
    spreads = []
    for a in range(3):
        for r in range(4):
            tile = delta[r][a : a + 1]
            spreads.append(jnp.where(in_row, tile, 0.0))
    high, low = halves(jnp.concatenate(spreads, 0))
    blocks = dot(jnp.concatenate([high, low], 1), jnp.concatenate([fold, fold], 0))
    table = jnp.concatenate([blocks[32 * a : 32 * a + 32] for a in range(3)], 1)
    slots = [index[:, 16 * (2 + c) : 16 * (2 + c) + 1].astype(I32) - 1 for c in range(4)]
    slot = jnp.concatenate(slots, 0)
    by_block = jnp.where((iota((4 * SKY_N, 64), 1) & 31) == slot, 1.0, 0.0)
    found = split_dot(by_block, table)
    group = lane >> 4
    front = jnp.zeros((SKY_N, 128), F32)
    back = jnp.zeros((SKY_N, 128), F32)
    for c in range(4):
        rows = found[SKY_N * c : SKY_N * (c + 1)]
        part = [rows[:, 128 * a : 128 * a + 128] for a in range(3)]
        front = jnp.where(group == c, part[0], jnp.where(group == c + 4, part[1], front))
        back = jnp.where(group == c, part[2], back)
    send_ref[:, 0, :] = front
    send_ref[:, 1, :] = back


def run_kernel(body, scalars, outs, *args, scratch=(), flops=10_000_000, **static):
    specs = [
        pl.BlockSpec(memory_space=pltpu.SMEM if i < scalars else pltpu.VMEM)
        for i in range(len(args))
    ]
    shapes = [o if isinstance(o, jax.ShapeDtypeStruct) else jax.ShapeDtypeStruct(o, F32) for o in outs]

    def kernel(*refs):
        body(*refs, **static)

    return pl.pallas_call(
        kernel,
        out_shape=shapes,
        in_specs=specs,
        out_specs=[
            pl.BlockSpec(memory_space=pltpu.SMEM if s.dtype == I32 else pltpu.VMEM) for s in shapes
        ],
        scratch_shapes=[pltpu.VMEM(shape, F32) for shape in scratch],
        cost_estimate=pl.CostEstimate(flops=flops, bytes_accessed=2_000_000, transcendentals=0),
        compiler_params=pltpu.CompilerParams(vmem_limit_bytes=32 * 1024 * 1024),
    )(*args)


def half(*shape):
    return jax.ShapeDtypeStruct(shape, BF16)


def shifts(k):
    return [(i, (i + k) % TM_N) for i in range(TM_N)]


def per_device(
    observed,
    att_partials,
    src_partials,
    src_slot,
    knot_block,
    live_count,
    sources,
    inverses,
    attitude,
    band_coef,
    extra_diag,
    band_offsets,
):
    core = lax.axis_index("c").astype(I32).reshape(1)
    tm = lax.axis_index("tm").astype(I32).reshape(1)
    slot = src_slot.reshape(1, CROSS)
    kb = knot_block.reshape(1, CROSS)
    chip = lax.axis_index(("x", "z")).astype(I32).reshape(1)
    knots = attitude.reshape(3, 4, 128)
    bands = band_coef.reshape(3, 3, 4, 128)
    extra = extra_diag.reshape(3, 4, 128)

    dense = pl.pallas_call(
        payload_kernel,
        out_shape=jax.ShapeDtypeStruct((CHIPS, 4, 4, 128), F32),
        in_specs=[pl.BlockSpec(memory_space=pl.ANY)] * 3,
        out_specs=pl.BlockSpec(memory_space=pltpu.VMEM),
        scratch_shapes=[
            pltpu.VMEM((3, 4, 128), F32),
            pltpu.VMEM((3, 3, 4, 128), F32),
            pltpu.VMEM((3, 4, 128), F32),
            pltpu.SemaphoreType.DMA((3,)),
        ],
        compiler_params=pltpu.CompilerParams(vmem_limit_bytes=56 * 1024 * 1024),
    )(knots, bands, extra)
    near = lax.all_to_all(dense, ("x", "z"), 0, 0, tiled=True)
    (
        cols, places, by_source, base, by_lane, by_row, pack, index, peers, choose, up, down, wide,
        ghost, products, normals, rhs, held, offsets,
    ) = run_kernel(
        prepare_kernel, 3,
        [
            (128, 128), half(144, 256), half(128, SRC_N), (CROSS, ROWS), half(384, 128),
            half(384, 128), half(SKY_N, 512), (SKY_N, 128), half(144, 128), (8, 128), (40, 128),
            (40, 128), (32, RUN), (40, 128), (1920, 128), (640, 128), (128, 128),
            (3, 4, 128), jax.ShapeDtypeStruct((3,), I32),
        ],
        live_count, core, band_offsets, observed, att_partials, src_partials, slot, kb, sources, bands, extra,
        knots,
    )
    near, cols = lax.optimization_barrier((near, cols))
    far = lax.ppermute(near, "c", [(0, 1), (1, 0)])
    masked, rhs, plain, up, down, sides = run_kernel(
        first_kernel, 2,
        [(384, 128), (128, 128), (HEAD, 128), (HEAD + 48, 128), (HEAD + 48, 128), (8, 128)],
        core, chip, near, far, cols, places, by_source, by_lane, up, down, ghost, products, rhs,
    )
    across = lax.ppermute(plain, "tm", shifts(2))
    up = lax.ppermute(up, "tm", shifts(1))
    down = lax.ppermute(down, "tm", shifts(-1))
    grads, resid = run_kernel(
        beside_kernel, 1, [(384, 128), (CROSS, ROWS)],
        live_count, masked, base, att_partials, by_lane, by_row,
    )
    outgoing, sources, resid, rhs = run_kernel(
        return_kernel, 2, [(SKY_N, 4, 128), (5, SRC_N), (CROSS, ROWS), (128, 128)],
        live_count, tm, across, plain, up, down, up, down, inverses, sources, grads, products,
        cols, by_source, by_row, pack, index, resid, src_partials, normals, rhs,
        scratch=[(HEAD, 128)], second=False,
    )
    got = lax.all_to_all(outgoing, SKY, 0, 0, tiled=True)
    knots, served, pick, rims = run_kernel(
        smooth_kernel, 4, [(3, 4, 128), (SKY_N, 2, 128), half(128, 128), (32, 128)],
        offsets, chip, core, tm, got, held, wide, sides, up, down, choose, last=False,
    )
    arrived = lax.all_to_all(served, SKY, 0, 0, tiled=True)
    masked, mine = run_kernel(
        middle_kernel, 0, [(384, 128), (HEAD + 8, 128)],
        arrived, resid, rhs, cols, peers, by_source, by_lane, choose, ghost, products,
    )
    across = lax.ppermute(mine, "tm", shifts(2))
    below = lax.ppermute(mine, "tm", shifts(1))
    above = lax.ppermute(mine, "tm", shifts(-1))
    (grads,) = run_kernel(
        beside_kernel, 1, [(384, 128)],
        live_count, masked, resid, att_partials, by_lane, by_row,
    )
    outgoing, step = run_kernel(
        return_kernel, 2, [(SKY_N, 1, 384), (5, SRC_N)],
        live_count, tm, across, mine, below, above, up, down, inverses, sources, grads, products,
        cols, by_source, by_row, pack, scratch=[(HEAD, 128)], second=True,
    )
    got = lax.all_to_all(outgoing, SKY, 0, 0, tiled=True)
    knots, sources = run_kernel(
        smooth_kernel, 4, [(3, 4, 128), (5, SRC_N)],
        offsets, chip, core, tm, got, knots, wide, sources, step, pick, rims, last=True,
    )
    return (sources, knots.reshape(3, 1, RUN))


def solution(mesh):
    torus = Mesh(mesh.devices.reshape(4, 8, 2, mesh.shape["tm"]), SKY_TM)
    return jax.shard_map(
        per_device,
        mesh=torus,
        in_specs=(
            P(SKY_TM, None),
            P(None, SKY_TM, None),
            P(None, SKY_TM, None),
            P(SKY_TM),
            P(SKY_TM),
            P(SKY_TM),
            P(None, SKY),
            P(None, None, SKY),
            P(None, "tm", SKY),
            P(None, None, "tm", SKY),
            P(None, "tm", SKY),
            P(),
        ),
        out_specs=(P(None, SKY), P(None, "tm", SKY)),
        check_vma=False,
    )
```
